32 devices in a mesh: seq: 16 (over z, y, x), dp: 2 (over core).
Axes of the slice: x: 2, y: 2, z: 4, core: 2. Of those that a mesh axis runs over, the one named last changes fastest.
Arguments:
- tokens: bfloat16 [2, 12288, 768], P('dp', 'seq'), may hold values from -6 to 6
- lengths: int32 [2, 3], P('dp'), may hold values from 2049 to 4096, as said below
- cotangent: bfloat16 [2, 12288, 768], P('dp', 'seq'), may hold values from -6 to 6
- norm1_gain: float32 [768], replicated, may hold values from 0.25 to 1.75
- norm1_shift: float32 [768], replicated, may hold values from -3 to 3
- query_weight: bfloat16 [768, 768], replicated, may hold values from -0.21875 to 0.21875
- query_bias: float32 [768], replicated, may hold values from -3 to 3
- keyval_weight: bfloat16 [768, 128], replicated, may hold values from -0.21875 to 0.21875
- value_bias: float32 [64], replicated, may hold values from -3 to 3
- out_weight: bfloat16 [768, 768], replicated, may hold values from -6 to 6
- out_bias: float32 [768], replicated, may hold values from -3 to 3
- norm2_gain: float32 [768], replicated, may hold values from 0.25 to 1.75
- norm2_shift: float32 [768], replicated, may hold values from -3 to 3
- up_weight: bfloat16 [768, 3072], replicated, may hold values from -0.21875 to 0.21875
- up_bias: float32 [3072], replicated, may hold values from -3 to 3
- down_weight: bfloat16 [3072, 768], replicated, may hold values from -0.109375 to 0.109375
- down_bias: float32 [768], replicated, may hold values from -3 to 3
Outputs:
- out_tokens: bfloat16 [2, 12288, 768], P('dp', 'seq')
- grad_tokens: float32 [2, 12288, 768], P('dp', 'seq')
- grad_norm1_gain: float32 [768], replicated
- grad_norm1_shift: float32 [768], replicated
- grad_query_weight: float32 [768, 768], replicated
- grad_query_bias: float32 [768], replicated
- grad_keyval_weight: float32 [768, 128], replicated
- grad_value_bias: float32 [64], replicated
- grad_out_weight: float32 [768, 768], replicated
- grad_out_bias: float32 [768], replicated
- grad_norm2_gain: float32 [768], replicated
- grad_norm2_shift: float32 [768], replicated
- grad_up_weight: float32 [768, 3072], replicated
- grad_up_bias: float32 [3072], replicated
- grad_down_weight: float32 [3072, 768], replicated
- grad_down_bias: float32 [768], replicated
The draws below stay inside these ranges and needn't reach their ends.
Inputs may be any that keep to these rules, and one draw needn't show every extreme that they name: `lengths`: valid tokens of each 4096-slot row, the valid ones first; every group has at least one row with all 4096 slots valid.
All inputs are finite; a program needn't handle non-finite values.
Results may differ from the reference program's by a relative error of at most 0.011.
Values may be sent and summed in bfloat16 or wider, within the bound.
A program may use at most 320 MiB of HBM per device.

```python
import jax
import jax.numpy as jnp
from jax import lax

D = 768
HEADS = 12
HEAD = 64
FF = 3072
ROW = 4096
GROUP_TOK = 12288
ROWS_G = 3
N_DP = 2


def draw_lengths(key, part):
    key = jax.random.fold_in(key, 7)
    first_key, second_key = jax.random.split(key)
    padding = jax.random.randint(first_key, (N_DP, ROWS_G), 0, ROW // 2)
    full_row = jax.random.randint(second_key, (N_DP, 1), 0, ROWS_G)
    places = jnp.arange(ROWS_G, dtype=jnp.int32)[None, :]
    padding = jnp.where(places == full_row, 0, padding)
    return (ROW - padding).astype(jnp.int32)


def steps_of(stream_key, dims, cuts, least, top_value):
    factor_of = 1.0
    for dim, blocks in cuts:
        heights = jax.random.uniform(jax.random.fold_in(jax.random.fold_in(stream_key, 6), dim), (blocks,), jnp.float32, least / len(cuts), top_value / len(cuts))
        factor_of = factor_of * jnp.repeat(jnp.exp(heights), dims[dim] // blocks).reshape((-1,) + (1,) * (len(dims) - 1 - dim))
    return factor_of


def normal_values(key, dims, scale, limit, cuts=(), kind=jnp.bfloat16):
    drawn = scale * jax.random.normal(key, dims, jnp.float32)
    if cuts:
        drawn = drawn * steps_of(key, dims, cuts, -0.22, 0.18)
    return jnp.clip(drawn, -limit, limit).astype(kind)


def setup_inputs(seed: int = 0) -> dict:
    keys = jax.random.split(jax.random.key(seed), 18)
    tokens = normal_values(keys[0], (N_DP, GROUP_TOK, D), 1.0, 6.0, ((0, 2), (1, 16)))
    lengths = draw_lengths(jax.random.fold_in(keys[17], 71), 0)
    cotangent = normal_values(keys[2], (N_DP, GROUP_TOK, D), 1.0, 6.0, ((0, 2), (1, 16)))
    norm1_gain = jnp.clip(1.0 + 0.15 * jax.random.normal(keys[3], (D,), jnp.float32), 0.25, 1.75)
    norm1_shift = normal_values(keys[4], (D,), 0.5, 3.0, (), jnp.float32)
    query_weight = normal_values(keys[5], (D, D), D ** -0.5, 0.21875)
    query_bias = normal_values(keys[6], (D,), 0.5, 3.0, (), jnp.float32)
    keyval_weight = normal_values(keys[7], (D, 2 * HEAD), D ** -0.5, 0.21875)
    value_bias = normal_values(keys[8], (HEAD,), 0.5, 3.0, (), jnp.float32)
    out_weight = normal_values(keys[9], (D, D), (max(1, 4 * D // ROW)) ** -0.5, 6.0)
    out_bias = normal_values(keys[10], (D,), 0.5, 3.0, (), jnp.float32)
    norm2_gain = jnp.clip(1.0 + 0.15 * jax.random.normal(keys[11], (D,), jnp.float32), 0.25, 1.75)
    norm2_shift = normal_values(keys[12], (D,), 0.5, 3.0, (), jnp.float32)
    up_weight = normal_values(keys[13], (D, FF), D ** -0.5, 0.21875)
    up_bias = normal_values(keys[14], (FF,), 0.5, 3.0, (), jnp.float32)
    down_weight = normal_values(keys[15], (FF, D), FF ** -0.5, 0.109375)
    down_bias = normal_values(keys[16], (D,), 0.5, 3.0, (), jnp.float32)
    return {"tokens": tokens, "lengths": lengths, "cotangent": cotangent, "norm1_gain": norm1_gain, "norm1_shift": norm1_shift, "query_weight": query_weight, "query_bias": query_bias, "keyval_weight": keyval_weight, "value_bias": value_bias, "out_weight": out_weight, "out_bias": out_bias, "norm2_gain": norm2_gain, "norm2_shift": norm2_shift, "up_weight": up_weight, "up_bias": up_bias, "down_weight": down_weight, "down_bias": down_bias}


epsilon = 1e-05
masked_score = -1e+30

@jax.custom_vjp
def low(v):
    return lax.optimization_barrier(v.astype(jnp.bfloat16)).astype(jnp.float32)

@jax.custom_vjp
def low_back(v):
    return v

def low_keep(v):
    return (low(v), None)

def low_pass(kept, grad):
    return (grad,)

def back_keep(v):
    return (v, None)

def back_low(kept, grad):
    return (low(grad),)
low.defvjp(low_keep, low_pass)
low_back.defvjp(back_keep, back_low)

def normed(values, gains, shifts):
    center = values - lax.optimization_barrier(jnp.mean(values, axis=-1, keepdims=True))
    spread = lax.optimization_barrier(jnp.mean(center * center, axis=-1, keepdims=True))
    return center * lax.rsqrt(spread + epsilon) * gains + shifts

def product(left_op, right_op):
    return jnp.dot(left_op, right_op, precision=lax.Precision.HIGHEST)

def row_layer(weights, row_tokens, row_length):
    gain_one, shift_one, query_weight, query_bias, keyval_weight, value_bias, out_weight, out_bias, gain_two, shift_two, up_weight, up_bias, down_weight, down_bias = weights
    normal_one = low(normed(row_tokens, gain_one, shift_one))
    queries = low_back(low(product(normal_one, query_weight) + query_bias))
    kv_bias = jnp.concatenate([jnp.zeros((HEAD,), jnp.float32), value_bias])
    keyvals = low_back(low(product(normal_one, keyval_weight) + kv_bias))
    query_heads = queries.reshape(ROW, HEADS, HEAD)
    raw_scores = jnp.einsum('qhd,kd->hqk', query_heads, keyvals[:, :HEAD], precision=lax.Precision.HIGHEST)
    raw_scores = low_back(raw_scores * HEAD ** (-0.5))
    places = jnp.arange(ROW, dtype=jnp.int32)
    allowed = (places[None, :] <= places[:, None]) & (places[None, :] < row_length)
    scores = jnp.where(allowed[None], raw_scores, masked_score)
    row_max = lax.optimization_barrier(jnp.max(scores, axis=-1, keepdims=True))
    exponent = jnp.exp(scores - row_max)
    probability = exponent / lax.optimization_barrier(jnp.sum(exponent, axis=-1, keepdims=True))
    mixture = jnp.einsum('hqk,kd->qhd', low(probability), keyvals[:, HEAD:], precision=lax.Precision.HIGHEST)
    attended = low_back(low(mixture.reshape(ROW, D)))
    projected = low_back(product(attended, out_weight) + out_bias)
    residual = row_tokens + projected
    normal_two = low(normed(residual, gain_two, shift_two))
    hidden_pre = low_back(product(normal_two, up_weight) + up_bias)
    activated = low(jax.nn.gelu(hidden_pre, approximate=True))
    return residual + product(activated, down_weight) + down_bias

def reference(tokens, lengths, cotangent, norm1_gain, norm1_shift, query_weight, query_bias, keyval_weight, value_bias, out_weight, out_bias, norm2_gain, norm2_shift, up_weight, up_bias, down_weight, down_bias):
    row_total = N_DP * ROWS_G
    inputs = tokens.astype(jnp.float32).reshape(row_total, ROW, D)
    weights = tuple((weight_arg.astype(jnp.float32) for weight_arg in (norm1_gain, norm1_shift, query_weight, query_bias, keyval_weight, value_bias, out_weight, out_bias, norm2_gain, norm2_shift, up_weight, up_bias, down_weight, down_bias)))
    flat_lengths = lengths.reshape(row_total).astype(jnp.int32)

    def forward(layer_inputs, layer_weights):
        layer_fn = jax.checkpoint(row_layer)

        def scan_step(running, pieces):
            return (running, layer_fn(layer_weights, pieces[0], pieces[1]))
        _, outputs = lax.scan(scan_step, jnp.float32(0.0), (layer_inputs, flat_lengths))
        return outputs
    outputs, pullback = jax.vjp(forward, inputs, weights)
    grad_inputs, grads_w = pullback(cotangent.astype(jnp.float32).reshape(row_total, ROW, D))
    out_shape = (N_DP, GROUP_TOK, D)
    return (outputs.reshape(out_shape).astype(jnp.bfloat16), grad_inputs.reshape(out_shape), grads_w[0], grads_w[1], grads_w[2], grads_w[3], grads_w[4], grads_w[5], grads_w[6], grads_w[7], grads_w[8], grads_w[9], grads_w[10], grads_w[11], grads_w[12], grads_w[13])
```

```python
from functools import partial

import jax
import jax.numpy as jnp
import numpy as np
from jax import lax
from jax.experimental import pallas as pl
from jax.experimental.pallas import tpu as pltpu
from jax.sharding import PartitionSpec as P

ROW = 4096
CHUNK = 128
BLOCK = 512
PAD = BLOCK - CHUNK
LOG2E = 1.4426950408889634
BIG = -1e30
SAFE = 60.0
epsilon = 1e-05
bf16 = jnp.bfloat16
f32 = jnp.float32

TRIPLES = (0, 2, 4, 3, 1, 5, 6, 8, 9, 7, 10, 12, 14, 15, 13, 11)


class Plan:
    def __init__(self, devices, shard_len):
        self.devices = devices
        self.per_dev = shard_len // CHUNK
        per_row = ROW // CHUNK
        half = per_row // 2
        pairs = self.per_dev // 2
        unit = len(TRIPLES)
        assert devices % unit == 0 and shard_len * unit % ROW == 0
        self.work = np.zeros((devices, self.per_dev), np.int32)
        for dev in range(devices):
            triple = dev // unit * unit + TRIPLES[dev % unit]
            for i in range(pairs):
                row, c = divmod(triple * pairs + i, half)
                self.work[dev, i] = row * per_row + c
                self.work[dev, pairs + i] = row * per_row + per_row - 1 - c
        self.row = self.work // per_row
        self.slot = self.work % per_row
        self.first_row = self.row.min(axis=1)
        self.last_row = self.row.max(axis=1)
        self.row_sel = self.row - self.first_row[:, None]
        moves = []
        self.pick = np.zeros((devices, self.per_dev), np.int32)
        for dev in range(devices):
            for slot in range(self.per_dev):
                src, chunk = divmod(int(self.work[dev, slot]), self.per_dev)
                if src == dev:
                    self.pick[dev, slot] = chunk
                else:
                    moves.append((src, chunk, dev, slot))
        degree = max(
            max(sum(m[0] == d for m in moves), sum(m[2] == d for m in moves)) for d in range(devices)
        )
        self.colors = [[] for _ in range(degree)]
        out_used = [dict() for _ in range(devices)]
        in_used = [dict() for _ in range(devices)]
        for move in moves:
            s, t = move[0], move[2]
            a = next(k for k in range(degree) if k not in out_used[s])
            b = next(k for k in range(degree) if k not in in_used[t])
            if a != b and a in in_used[t]:
                node, side, path = t, "in", []
                want = a
                while True:
                    used = in_used[node] if side == "in" else out_used[node]
                    if want not in used:
                        break
                    edge = used[want]
                    path.append((edge, want))
                    node = edge[0] if side == "in" else edge[2]
                    side = "out" if side == "in" else "in"
                    want = b if want == a else a
                for edge, k in path:
                    del out_used[edge[0]][k]
                    del in_used[edge[2]][k]
                for edge, k in path:
                    other = b if k == a else a
                    out_used[edge[0]][other] = edge
                    in_used[edge[2]][other] = edge
            out_used[s][a] = move
            in_used[t][a] = move
        self.send_chunk = np.zeros((degree, devices), np.int32)
        self.send_slot = np.zeros((degree, devices), np.int32)
        self.back = np.zeros((devices, self.per_dev), np.int32)
        for dev in range(devices):
            for k, m in in_used[dev].items():
                self.pick[dev, m[3]] = self.per_dev + k
                self.send_slot[k, dev] = m[3]
            for k, m in out_used[dev].items():
                self.colors[k].append((m[0], m[2]))
                self.send_chunk[k, dev] = m[1]
                self.back[dev, m[1]] = self.per_dev + k
            for slot in range(self.per_dev):
                src, chunk = divmod(int(self.work[dev, slot]), self.per_dev)
                if src == dev:
                    self.back[dev, chunk] = slot
        self.degree = degree
        rows_of = [
            set(range(d * shard_len // ROW, ((d + 1) * shard_len - 1) // ROW + 1))
            for d in range(devices)
        ]
        self.reach = 0
        for d in range(devices):
            for e in range(devices):
                if rows_of[d] & rows_of[e]:
                    self.reach = max(self.reach, abs(d - e))
        self.share = {
            off: [
                (d, d + off)
                for d in range(devices)
                if 0 <= d + off < devices and rows_of[d] & rows_of[d + off]
            ]
            for off in range(-self.reach, self.reach + 1)
        }


def take_chunks(options, index):
    count = index.shape[0]
    return jnp.concatenate(
        [lax.dynamic_slice_in_dim(options, index[i] * CHUNK, CHUNK, 0) for i in range(count)], axis=0
    )


def to_work(plan, device, value):
    received = [
        lax.ppermute(
            lax.dynamic_slice_in_dim(
                value, jnp.asarray(plan.send_chunk[k])[device] * CHUNK, CHUNK, 0
            ),
            "seq",
            plan.colors[k],
        )
        for k in range(plan.degree)
    ]
    return take_chunks(jnp.concatenate([value] + received, axis=0), jnp.asarray(plan.pick)[device])


def to_home(plan, device, value):
    received = [
        lax.ppermute(
            lax.dynamic_slice_in_dim(
                value, jnp.asarray(plan.send_slot[k])[device] * CHUNK, CHUNK, 0
            ),
            "seq",
            [(b, a) for a, b in plan.colors[k]],
        )
        for k in range(plan.degree)
    ]
    return take_chunks(jnp.concatenate([value] + received, axis=0), jnp.asarray(plan.back)[device])


def normed(values, gains, shifts):
    center = values - jnp.mean(values, axis=-1, keepdims=True)
    spread = jnp.mean(center * center, axis=-1, keepdims=True)
    return center * lax.rsqrt(spread + epsilon) * gains + shifts


def contract(left_op, right_op, left_dim, right_dim):
    return lax.dot_general(
        left_op, right_op, (((left_dim,), (right_dim,)), ((), ())), preferred_element_type=f32
    )


def wide(block, heads, head_dim):
    return jnp.concatenate([block[h * head_dim : (h + 1) * head_dim] for h in range(heads)], axis=1)


def tall(block, heads):
    return jnp.concatenate([block[:, h * CHUNK : (h + 1) * CHUNK] for h in range(heads)], axis=0)


def hi_lo(value, count):
    parts = []
    for _ in range(count):
        part = value.astype(bf16)
        parts.append(part)
        value = value - part.astype(f32)
    return parts


def scaled_queries(q_block, heads, head_dim, extra):
    q = wide(q_block, heads, head_dim)
    hi, lo = hi_lo(q.astype(f32) * (LOG2E * head_dim ** (-0.5)), 2)
    width = q.shape[1]
    ones = jnp.ones((1, width), f32)
    rows = jnp.concatenate(
        extra + [ones, jnp.zeros((2 * head_dim - 1 - len(extra), width), f32)], axis=0
    ).astype(bf16)
    return q, jnp.concatenate([hi, lo, rows], axis=0)


def triangle(heads):
    key = lax.broadcasted_iota(jnp.int32, (CHUNK, heads * CHUNK), 0)
    query = lax.broadcasted_iota(jnp.int32, (CHUNK, heads * CHUNK), 1) % CHUNK
    return key <= query


def first_scores(k_block, q_aug, heads):
    s = contract(k_block, q_aug, 1, 0)
    return jnp.concatenate([s[:PAD], jnp.where(triangle(heads), s[PAD:], BIG)], axis=0)


def attend_kernel(heads, head_dim, meta, q_ref, k_ref, vt_ref, o_ref, lse_ref, acc, top):
    i = pl.program_id(0)
    n = pl.num_programs(0)
    row = meta[i]
    end = (meta[n + i] + 1) * CHUNK + PAD
    blocks = meta[n + i] // (BLOCK // CHUNK) + 1
    zero = jnp.zeros((1, heads * CHUNK), f32)
    _, q_aug = scaled_queries(q_ref[...], heads, head_dim, [zero, zero, zero])

    def scores(j):
        off = pl.multiple_of(end - (j + 1) * BLOCK, CHUNK)
        return contract(k_ref[row, pl.ds(off, BLOCK), :], q_aug, 1, 0)

    def values(j):
        off = pl.multiple_of(end - (j + 1) * BLOCK, CHUNK)
        return vt_ref[row, :, pl.ds(off, BLOCK)]

    def masked(s):
        return jnp.concatenate([s[:PAD], jnp.where(triangle(heads), s[PAD:], BIG)], axis=0)

    @pl.when(meta[2 * n] > 0)
    def _():
        p = jnp.exp2(masked(scores(0))).astype(bf16)
        acc[...] = contract(values(0), p, 1, 0)

        def step(j, _):
            p = jnp.exp2(scores(j)).astype(bf16)
            acc[...] += contract(values(j), p, 1, 0)
            return 0

        lax.fori_loop(1, blocks, step, 0)
        top[...] = jnp.zeros_like(top)

    @pl.when(meta[2 * n] == 0)
    def _():
        s = masked(scores(0))
        m = jnp.max(s, axis=0, keepdims=True)
        top[...] = m
        acc[...] = contract(values(0), jnp.exp2(s - m).astype(bf16), 1, 0)

        def step(j, _):
            s = scores(j)
            old = top[...]
            m = jnp.maximum(old, jnp.max(s, axis=0, keepdims=True))
            top[...] = m
            p = jnp.exp2(s - m).astype(bf16)
            acc[...] = acc[...] * jnp.exp2(old - m) + contract(values(j), p, 1, 0)
            return 0

        lax.fori_loop(1, blocks, step, 0)

    total = acc[head_dim : head_dim + 1, :]
    o_ref[...] = tall(acc[:head_dim, :] / total, heads).astype(bf16)
    lse_ref[0] = top[...] + jnp.log2(total)


def back_kernel(
    heads, head_dim, meta, q_ref, g_ref, o_ref, lse_ref, k_ref, v_ref, kt_ref, dq_ref, dkv_ref, acc
):
    i = pl.program_id(0)
    n = pl.num_programs(0)
    row = meta[i]
    end = (meta[n + i] + 1) * CHUNK + PAD
    blocks = meta[n + i] // (BLOCK // CHUNK) + 1

    @pl.when(i == 0)
    def _():
        dkv_ref[...] = jnp.zeros_like(dkv_ref)

    lse_parts = [part.astype(f32) for part in hi_lo(-lse_ref[0], 3)]
    q, q_aug = scaled_queries(q_ref[...], heads, head_dim, lse_parts)
    g = wide(g_ref[...], heads, head_dim)
    o = wide(o_ref[...], heads, head_dim)
    delta = jnp.sum(g.astype(f32) * o.astype(f32), axis=0, keepdims=True)
    delta_parts = [part.astype(f32) for part in hi_lo(-delta, 3)]
    fill = jnp.zeros((head_dim - 3, heads * CHUNK), f32)
    g_aug = jnp.concatenate([g, jnp.concatenate(delta_parts + [fill], axis=0).astype(bf16)], axis=0)

    def block(j, first):
        off = pl.multiple_of(end - (j + 1) * BLOCK, CHUNK)
        at = pl.ds(off, BLOCK)
        s = contract(k_ref[row, at, :], q_aug, 1, 0)
        if first:
            s = jnp.concatenate([s[:PAD], jnp.where(triangle(heads), s[PAD:], BIG)], axis=0)
        dp = contract(v_ref[row, at, :], g_aug, 1, 0)
        p = jnp.exp2(s)
        ds = (p * dp).astype(bf16)
        p = p.astype(bf16)
        dq = contract(kt_ref[row, :, at], ds, 1, 0)
        if first:
            acc[...] = dq
        else:
            acc[...] += dq
        dkv_ref[row, :head_dim, at] += contract(q, ds, 1, 1)
        dkv_ref[row, head_dim:, at] += contract(g, p, 1, 1)

    block(0, True)

    def step(j, _):
        block(j, False)
        return 0

    lax.fori_loop(1, blocks, step, 0)
    dq_ref[...] = tall(acc[...] * head_dim ** (-0.5), heads).astype(bf16)

    @pl.when(i == n - 1)
    def _():
        dkv_ref[:, :head_dim] = dkv_ref[:, :head_dim] * head_dim ** (-0.5)


def whole(shape):
    return pl.BlockSpec(shape, lambda i, meta: (0,) * len(shape))


def column(rows):
    return pl.BlockSpec((rows, CHUNK), lambda i, meta: (0, i))


def lead(shape):
    return pl.BlockSpec((1,) + shape, lambda i, meta: (i,) + (0,) * len(shape))


def per_device(
    plan,
    tokens,
    lengths,
    cotangent,
    norm1_gain,
    norm1_shift,
    query_weight,
    query_bias,
    keyval_weight,
    value_bias,
    out_weight,
    out_bias,
    norm2_gain,
    norm2_shift,
    up_weight,
    up_bias,
    down_weight,
    down_bias,
):
    device = lax.axis_index("seq")
    shard_len, width = tokens.shape[1:]
    head_dim = keyval_weight.shape[1] // 2
    heads = width // head_dim
    columns = heads * CHUNK
    chunks = plan.per_dev
    limit = dict(vmem_limit_bytes=56 * 2**20)

    home_tokens = tokens[0]
    home_inputs = home_tokens.astype(f32)
    normal_home = normed(home_inputs, norm1_gain, norm1_shift).astype(bf16)
    kv_bias = jnp.concatenate([jnp.zeros((head_dim,), f32), value_bias])
    keyvals = (contract(normal_home, keyval_weight, 1, 0) + kv_bias).astype(bf16)

    reach = plan.reach
    window = jnp.concatenate(
        [
            keyvals if off == 0 else lax.ppermute(keyvals, "seq", plan.share[-off])
            for off in range(-reach, reach + 1)
        ],
        axis=0,
    )
    origin = (device - reach) * shard_len
    row_ids = jnp.stack([jnp.asarray(plan.first_row)[device], jnp.asarray(plan.last_row)[device]])
    starts = row_ids * ROW - origin
    key_slot = jnp.arange(ROW + PAD, dtype=jnp.int32) - PAD
    k_aug, v_aug, vt_aug, kt_all = [], [], [], []
    for r in range(2):
        rows = lax.dynamic_slice_in_dim(window, starts[r], ROW, 0)
        rows = jnp.concatenate([jnp.zeros((PAD, 2 * head_dim), bf16), rows], axis=0)
        keys, vals = rows[:, :head_dim], rows[:, head_dim:]
        live = (key_slot >= 0) & (key_slot < lengths[0][row_ids[r]])
        bias = jnp.where(live, 0.0, BIG).astype(bf16)[:, None]
        ones = jnp.ones((ROW + PAD, 3), bf16)
        k_aug.append(
            jnp.concatenate(
                [keys, keys, ones, bias, jnp.zeros((ROW + PAD, 2 * head_dim - 4), bf16)], axis=1
            )
        )
        v_aug.append(
            jnp.concatenate([vals, ones, jnp.zeros((ROW + PAD, head_dim - 3), bf16)], axis=1)
        )
        vt_aug.append(
            jnp.concatenate(
                [vals.T, jnp.ones((1, ROW + PAD), bf16), jnp.zeros((15, ROW + PAD), bf16)], axis=0
            )
        )
        kt_all.append(keys.T)
    k_aug, v_aug, vt_aug, kt_all = map(jnp.stack, (k_aug, v_aug, vt_aug, kt_all))

    work_tokens = to_work(plan, device, home_tokens)
    upstream = to_work(plan, device, cotangent[0])
    inputs = work_tokens.astype(f32)
    normal_one = normed(inputs, norm1_gain, norm1_shift).astype(bf16)
    queries = (contract(query_weight, normal_one, 0, 1) + query_bias[:, None]).astype(bf16)

    q_norm = jnp.max(jnp.sum(jnp.square(queries.astype(f32).reshape(heads, head_dim, -1)), axis=1))
    k_norm = jnp.max(jnp.sum(jnp.square(window[:, :head_dim].astype(f32)), axis=1))
    bound = jnp.sqrt(q_norm * k_norm) * (LOG2E * head_dim ** (-0.5))
    meta = jnp.concatenate(
        [
            jnp.asarray(plan.row_sel)[device],
            jnp.asarray(plan.slot)[device],
            (bound < SAFE).astype(jnp.int32)[None],
        ]
    )

    key_rows = ROW + PAD
    attended, lse = pl.pallas_call(
        partial(attend_kernel, heads, head_dim),
        grid_spec=pltpu.PrefetchScalarGridSpec(
            num_scalar_prefetch=1,
            grid=(chunks,),
            in_specs=[
                column(width),
                whole((2, key_rows, 4 * head_dim)),
                whole((2, head_dim + 16, key_rows)),
            ],
            out_specs=[column(width), lead((1, columns))],
            scratch_shapes=[pltpu.VMEM((head_dim + 16, columns), f32), pltpu.VMEM((1, columns), f32)],
        ),
        out_shape=[
            jax.ShapeDtypeStruct((width, shard_len), bf16),
            jax.ShapeDtypeStruct((chunks, 1, columns), f32),
        ],
        compiler_params=pltpu.CompilerParams(**limit),
        name="attend",
    )(meta, queries, k_aug, vt_aug)

    residual = inputs + contract(attended, out_weight, 0, 0) + out_bias
    normal_two = normed(residual, norm2_gain, norm2_shift).astype(bf16)
    hidden_pre = contract(normal_two, up_weight, 1, 0) + up_bias
    activated = jax.nn.gelu(hidden_pre, approximate=True).astype(bf16)
    outputs = (residual + contract(activated, down_weight, 1, 0) + down_bias).astype(bf16)
    outputs = to_home(plan, device, outputs)
    upstream_wide = upstream.astype(f32)
    grad_down = contract(activated, upstream, 0, 0)
    grad_down_bias = jnp.sum(upstream_wide, axis=0)
    grad_act = contract(upstream, down_weight, 1, 1)
    _, gelu_back = jax.vjp(partial(jax.nn.gelu, approximate=True), hidden_pre)
    grad_hidden = gelu_back(grad_act)[0].astype(bf16)
    grad_up = contract(normal_two, grad_hidden, 0, 0)
    grad_up_bias = jnp.sum(grad_hidden.astype(f32), axis=0)
    grad_normal_two = contract(grad_hidden, up_weight, 1, 1)
    _, norm_two_back = jax.vjp(normed, residual, norm2_gain, norm2_shift)
    grad_res_part, grad_gain_two, grad_shift_two = norm_two_back(grad_normal_two)
    grad_residual = upstream_wide + grad_res_part
    grad_proj = grad_residual.astype(bf16)
    grad_out_w = contract(attended, grad_proj, 1, 0)
    grad_out_b = jnp.sum(grad_proj.astype(f32), axis=0)
    grad_att = contract(out_weight, grad_proj, 1, 1).astype(bf16)
    home_residual = to_home(plan, device, grad_proj).astype(f32)

    grad_queries, grad_rows = pl.pallas_call(
        partial(back_kernel, heads, head_dim),
        grid_spec=pltpu.PrefetchScalarGridSpec(
            num_scalar_prefetch=1,
            grid=(chunks,),
            in_specs=[
                column(width),
                column(width),
                column(width),
                lead((1, columns)),
                whole((2, key_rows, 4 * head_dim)),
                whole((2, key_rows, 2 * head_dim)),
                whole((2, head_dim, key_rows)),
            ],
            out_specs=[column(width), whole((2, 2 * head_dim, key_rows))],
            scratch_shapes=[pltpu.VMEM((head_dim, columns), f32)],
        ),
        out_shape=[
            jax.ShapeDtypeStruct((width, shard_len), bf16),
            jax.ShapeDtypeStruct((2, 2 * head_dim, key_rows), f32),
        ],
        compiler_params=pltpu.CompilerParams(**limit),
        name="attend_back",
    )(meta, queries, grad_att, attended, lse, k_aug, v_aug, kt_all)

    grad_window = jnp.zeros(((2 * reach + 1) * shard_len, 2 * head_dim), f32)
    same = row_ids[0] == row_ids[1]
    for r in range(2):
        part = grad_rows[r][:, PAD:].T
        if r == 1:
            part = jnp.where(same, 0.0, part)
        old = lax.dynamic_slice_in_dim(grad_window, starts[r], ROW, 0)
        grad_window = lax.dynamic_update_slice_in_dim(grad_window, old + part, starts[r], 0)
    grad_window = grad_window.astype(bf16)
    returned = jnp.zeros((shard_len, 2 * head_dim), f32)
    for off in range(-reach, reach + 1):
        piece = grad_window[(off + reach) * shard_len : (off + reach + 1) * shard_len]
        if off != 0:
            piece = lax.ppermute(piece, "seq", plan.share[off])
        returned = returned + piece.astype(f32)
    grad_kv = returned.astype(bf16)

    grad_queries_home = to_home(plan, device, grad_queries.T)
    grad_qw = contract(normal_one, grad_queries, 0, 1)
    grad_qb = jnp.sum(grad_queries.astype(f32), axis=1)
    grad_kvw = contract(normal_home, grad_kv, 0, 0)
    grad_vb = jnp.sum(grad_kv[:, head_dim:].astype(f32), axis=0)
    grad_normal_one = contract(grad_queries_home, query_weight, 1, 1) + contract(
        grad_kv, keyval_weight, 1, 1
    )
    _, norm_one_back = jax.vjp(normed, home_inputs, norm1_gain, norm1_shift)
    grad_in_part, grad_gain_one, grad_shift_one = norm_one_back(grad_normal_one)
    grad_inputs = home_residual + grad_in_part
    big = (grad_qw, grad_kvw, grad_out_w, grad_up, grad_down)
    small = (
        grad_gain_one,
        grad_shift_one,
        grad_qb,
        grad_vb,
        grad_out_b,
        grad_gain_two,
        grad_shift_two,
        grad_up_bias,
        grad_down_bias,
    )
    sizes = np.cumsum([v.shape[0] for v in small])[:-1]
    small = jnp.split(lax.psum(jnp.concatenate(small), ("seq", "dp")), sizes)
    big = [
        v.astype(f32) for v in lax.psum(tuple(v.astype(bf16) for v in big), ("seq", "dp"))
    ]
    gain_one, shift_one, qb, vb, out_b, gain_two, shift_two, up_b, down_b = small
    qw, kvw, out_w, up_w, down_w = big
    return (
        outputs[None],
        grad_inputs[None],
        gain_one,
        shift_one,
        qw,
        qb,
        kvw,
        vb,
        out_w,
        out_b,
        gain_two,
        shift_two,
        up_w,
        up_b,
        down_w,
        down_b,
    )


def solution(mesh):
    split = P("dp", "seq", None)
    devices = mesh.shape["seq"]

    def run(*arrays):
        plan = Plan(devices, arrays[0].shape[1] // devices)
        return jax.shard_map(
            partial(per_device, plan),
            mesh=mesh,
            in_specs=(split, P("dp", None), split) + (P(),) * 14,
            out_specs=(split, split) + (P(),) * 14,
            check_vma=False,
        )(*arrays)

    return run
```

```python
from functools import partial

import jax
import jax.numpy as jnp
import numpy as np
from jax import lax
from jax.experimental import pallas as pl
from jax.experimental.pallas import tpu as pltpu
from jax.sharding import PartitionSpec as P

ROW = 4096
CHUNK = 128
BLOCK = 512
PAD = BLOCK - CHUNK
LOG2E = 1.4426950408889634
BIG = -1e30
MARGIN = BLOCK
PIECE = 1024
DELAYS = (2, 8, 4, 3, 3, 2, 3, 5, 8, 3)
SAFE = 60.0
epsilon = 1e-05
GELU = 0.7978845608028654
bf16 = jnp.bfloat16
f32 = jnp.float32


class Plan:
    def __init__(self, devices, shard_len):
        self.devices = devices
        self.shard_len = shard_len
        self.per_dev = shard_len // CHUNK
        self.per_row = ROW // CHUNK
        assert shard_len % CHUNK == 0 and shard_len <= ROW
        ends = [(d + 1) * shard_len - self.first_row(d) * ROW for d in range(devices)]
        self.span = -(-max(ends) // BLOCK) * BLOCK
        self.window = MARGIN + self.span
        self.reach = max(
            d - e for d in range(devices) for e in range(d + 1) if self.first_row(d) <= self.last_row(e)
        )

    def first_row(self, device):
        return device * self.shard_len // ROW

    def last_row(self, device):
        return ((device + 1) * self.shard_len - 1) // ROW

    def feeds(self, source, holder):
        return (
            (source >= 0) & (holder < self.devices) & (self.first_row(holder) <= self.last_row(source))
        )

    def place(self, source, holder):
        return MARGIN + source * self.shard_len - self.first_row(holder) * ROW

    def chunk(self, device, i):
        return device * self.per_dev + i - self.first_row(device) * self.per_row


class Summing:
    def __init__(self, plan, pieces, height, mat, inbox, extra, sems):
        self.pieces, self.height = pieces, height
        self.mat, self.inbox, self.extra = mat, inbox, extra
        self.out_send, self.out_recv, self.back_send, self.back_recv, self.free = sems
        self.bits = plan.devices.bit_length() - 1
        self.halvings = 1 + min(self.bits, 4)
        self.swaps = self.bits + 1 - self.halvings
        self.stages = 2 * self.halvings + self.swaps
        self.seq, self.dp = lax.axis_index("seq"), lax.axis_index("dp")

    @staticmethod
    def scratch(plan, pieces, height, width):
        bits = plan.devices.bit_length() - 1
        halvings = 1 + min(bits, 4)
        swaps = bits + 1 - halvings
        last = height >> halvings
        dma = pltpu.SemaphoreType.DMA
        return [
            pltpu.VMEM((pieces, height - last, width), bf16),
            pltpu.VMEM((max(swaps, 1), pieces, last, width), bf16),
            dma((halvings + swaps, pieces)),
            dma((halvings + swaps, pieces)),
            dma((halvings, pieces)),
            dma((halvings, pieces)),
            pltpu.SemaphoreType.REGULAR((halvings, pieces)),
        ]

    def partners(self):
        bits = [(self.seq >> b) & 1 for b in range(self.bits)]
        return [(self.seq, 1 - self.dp)] + [
            (self.seq + (1 - 2 * bit) * (1 << b), self.dp) for b, bit in enumerate(bits)
        ]

    def turn(self, t, p):
        if t == 0:
            return self.dp, {"seq": self.seq, "dp": 1 - self.dp}
        if t < 4:
            b = (p + (t - 1)) % 3
            step = jnp.where(b == 0, 1, jnp.where(b == 1, 2, 4))
        else:
            step = 1 << (t - 1)
        bit = (self.seq // step) % 2
        return bit, {"seq": self.seq + (1 - 2 * bit) * step, "dp": self.dp}

    def base(self, t, p):
        at = 0
        for u in range(t):
            bit, _ = self.turn(u, p)
            at = at + bit * (self.height >> (u + 1))
        return at

    def rows(self, start, size):
        return pl.ds(pl.multiple_of(start, size), size)

    def copy(self, stage, p):
        h, w = self.halvings, self.swaps
        if stage < h:
            t, size = stage, self.height >> (stage + 1)
            bit, device = self.turn(t, p)
            src = self.mat.at[p, self.rows(self.base(t, p) + (1 - bit) * size, size)]
            dst = self.inbox.at[p, pl.ds(self.height - 2 * size, size)]
            sems = self.out_send.at[t, p], self.out_recv.at[t, p]
        elif stage < h + w:
            t, size = stage, self.height >> h
            _, device = self.turn(t, p)
            src = self.mat.at[p, self.rows(self.base(h, p), size)]
            dst = self.extra.at[t - h, p]
            sems = self.out_send.at[t, p], self.out_recv.at[t, p]
        else:
            t = self.stages - 1 - stage
            size = self.height >> (t + 1)
            _, device = self.turn(t, p)
            src = self.mat.at[p, self.rows(self.base(t + 1, p), size)]
            dst = src
            sems = self.back_send.at[t, p], self.back_recv.at[t, p]
        return pltpu.make_async_remote_copy(
            src_ref=src,
            dst_ref=dst,
            send_sem=sems[0],
            recv_sem=sems[1],
            device_id=device,
            device_id_type=pl.DeviceIdType.MESH,
        )

    def event(self, stage, p):
        if stage > 0:
            before = stage - 1
            self.copy(before, p).wait()
            h = self.halvings
            if before < h:
                size = self.height >> (before + 1)
                at = self.rows(self.base(before + 1, p), size)
                self.mat[p, at, :] = self.mat[p, at, :] + self.inbox[p, pl.ds(self.height - 2 * size, size), :]
                _, device = self.turn(before, p)
                pl.semaphore_signal(
                    self.free.at[before, p], inc=1, device_id=device, device_id_type=pl.DeviceIdType.MESH
                )
            elif before < h + self.swaps:
                at = self.rows(self.base(h, p), self.height >> h)
                self.mat[p, at, :] = self.mat[p, at, :] + self.extra[before - h, p]
        if stage >= self.halvings + self.swaps and stage < self.stages:
            pl.semaphore_wait(self.free.at[self.stages - 1 - stage, p], 1)
        if stage < self.stages:
            self.copy(stage, p).start()

    def step(self, n, starts, first=None, last=None):
        for stage in range(self.stages, -1, -1):
            p = n - starts[stage]

            @pl.when((p >= 0) & (p < self.pieces))
            def _():
                if stage == 0 and first is not None:
                    first(p)
                self.event(stage, p)
                if stage == self.stages and last is not None:
                    last(p)

    def starts(self, delays):
        h = self.halvings
        full = [delays[s] for s in range(h)] + [delays[h - 1]] * self.swaps + list(delays[5 : 5 + h])
        at = [0]
        for d in full:
            at.append(at[-1] + d)
        return at


def line(ref):
    return ref[...].reshape(1, ref.shape[0])


def remote(src, dst, send, recv, device):
    return pltpu.make_async_remote_copy(
        src_ref=src,
        dst_ref=dst,
        send_sem=send,
        recv_sem=recv,
        device_id={"seq": device},
        device_id_type=pl.DeviceIdType.MESH,
    )


def greet(plan, me, others=()):
    barrier = pltpu.get_barrier_semaphore()
    count = len(others)
    for seq, dp in others:
        pl.semaphore_signal(
            barrier, inc=1, device_id={"seq": seq, "dp": dp}, device_id_type=pl.DeviceIdType.MESH
        )
    for off in range(1, plan.reach + 1):
        for there, device in ((plan.feeds(me, me + off), me + off), (plan.feeds(me - off, me), me - off)):
            count = count + jnp.where(there, 1, 0)

            @pl.when(there)
            def _():
                pl.semaphore_signal(
                    barrier, inc=1, device_id={"seq": device}, device_id_type=pl.DeviceIdType.MESH
                )

    pl.semaphore_wait(barrier, count)


def gather_kernel(
    plan,
    tok_ref, gain_ref, shift_ref, wkv_ref, kvb_ref, wq_ref, qb_ref,
    normal_ref, q_ref, win_ref,
    kv_ref, kv_send, kv_recv,
):
    me = lax.axis_index("seq")
    greet(plan, me)

    def copy(off, source, holder):
        at = pl.multiple_of(plan.place(source, holder), CHUNK)
        return remote(
            kv_ref, win_ref.at[pl.ds(at, plan.shard_len)], kv_send.at[off - 1], kv_recv.at[off - 1], holder
        )

    normal = normed(tok_ref[...].astype(f32), line(gain_ref), line(shift_ref)).astype(bf16)
    normal_ref[...] = normal
    bias = line(kvb_ref)
    bias = jnp.concatenate([jnp.zeros_like(bias), bias], axis=1)
    kv_ref[...] = (contract(normal, wkv_ref[...], 1, 0) + bias).astype(bf16)
    for off in range(1, plan.reach + 1):

        @pl.when(plan.feeds(me, me + off))
        def _():
            copy(off, me, me + off).start()

    own = pl.multiple_of(plan.place(me, me), CHUNK)
    win_ref[pl.ds(own, plan.shard_len), :] = kv_ref[...]
    q_ref[...] = (contract(normal, wq_ref[...], 1, 0) + line(qb_ref)).T.astype(bf16)
    for off in range(1, plan.reach + 1):

        @pl.when(plan.feeds(me, me + off))
        def _():
            copy(off, me, me + off).wait_send()

        @pl.when(plan.feeds(me - off, me))
        def _():
            at = pl.multiple_of(plan.place(me - off, me), CHUNK)
            remote(
                kv_ref, win_ref.at[pl.ds(at, plan.shard_len)], kv_send.at[off - 1], kv_recv.at[off - 1], me - off
            ).wait_recv()


def normed(values, gains, shifts):
    center = values - jnp.mean(values, axis=-1, keepdims=True)
    spread = jnp.mean(center * center, axis=-1, keepdims=True)
    return center * lax.rsqrt(spread + epsilon) * gains + shifts


def contract(left_op, right_op, left_dim, right_dim):
    return lax.dot_general(
        left_op, right_op, (((left_dim,), (right_dim,)), ((), ())), preferred_element_type=f32
    )


def wide(block, heads, head_dim):
    return jnp.concatenate([block[h * head_dim : (h + 1) * head_dim] for h in range(heads)], axis=1)


def tall(block, heads):
    return jnp.concatenate([block[:, h * CHUNK : (h + 1) * CHUNK] for h in range(heads)], axis=0)


def hi_lo(value, count):
    parts = []
    for _ in range(count):
        part = value.astype(bf16)
        parts.append(part.astype(f32))
        value = value - parts[-1]
    return parts


def scaled_queries(q, head_dim, lse_parts, row):
    width = q.shape[1]
    hi, lo = hi_lo(q.astype(f32) * (LOG2E * head_dim ** (-0.5)), 2)
    first = jnp.broadcast_to(jnp.where(row == 0, 1.0, 0.0), (1, width))
    fill = jnp.zeros((2 * head_dim - 5, width), f32)
    return jnp.concatenate([hi, lo] + lse_parts + [first, 1.0 - first, fill], axis=0).astype(bf16)


def triangle(heads):
    key = lax.broadcasted_iota(jnp.int32, (CHUNK, heads * CHUNK), 0)
    query = lax.broadcasted_iota(jnp.int32, (CHUNK, heads * CHUNK), 1) % CHUNK
    return key <= query


def causal(s, heads):
    return jnp.concatenate([s[:PAD], jnp.where(triangle(heads), s[PAD:], BIG)], axis=0)


def attend_kernel(
    plan, heads, head_dim, len_ref, q_ref, win_ref, o_ref, rest_ref, lse_ref, k_ref, v_ref, kt_ref, vt_ref, acc, top, norm
):
    i = pl.program_id(0)
    me = lax.axis_index("seq")
    place = plan.chunk(me, i)
    row = place // (ROW // CHUNK)
    end = MARGIN + (place + 1) * CHUNK
    blocks = place % (ROW // CHUNK) // (BLOCK // CHUNK) + 1

    @pl.when(i == 0)
    def _():
        first, second = len_ref[0, plan.first_row(me)], len_ref[0, plan.last_row(me)]
        filled = plan.place(me, me) + plan.shard_len - MARGIN
        lane = lax.broadcasted_iota(jnp.int32, (BLOCK, 2 * head_dim), 1)
        vt_ref[head_dim:, :] = jnp.where(
            lax.broadcasted_iota(jnp.int32, (16, vt_ref.shape[1]), 0) == 0, 1.0, 0.0
        ).astype(bf16)
        norm[...] = jnp.zeros_like(norm)

        def fill(b, _):
            at = pl.ds(pl.multiple_of(b * BLOCK, BLOCK), BLOCK)
            pos = b * BLOCK - MARGIN + lax.broadcasted_iota(jnp.int32, (BLOCK, 2 * head_dim), 0)
            inside = (pos >= 0) & (pos < filled)
            both = jnp.where(inside, win_ref[at, :].astype(f32), 0.0)
            swapped = pltpu.roll(both, head_dim, 1)
            k_ref[at, : 2 * head_dim] = jnp.where(lane < head_dim, both, swapped).astype(bf16)
            one = (pos >= 0) & (pos < first)
            two = (pos >= ROW) & (pos < ROW + second)
            bias = jnp.where(lane == 3, jnp.where(one, 0.0, BIG), jnp.where(two, 0.0, BIG))
            marks = jnp.where(lane < 3, 1.0, jnp.where(lane < 5, bias, 0.0))
            k_ref[at, 2 * head_dim :] = marks.astype(bf16)
            v_ref[at, :] = jnp.where(
                lane >= head_dim, both, jnp.where(lane < 3, 1.0, 0.0)
            ).astype(bf16)
            turned = both.T
            kt_ref[:, at] = turned[:head_dim].astype(bf16)
            vt_ref[:head_dim, at] = turned[head_dim:].astype(bf16)
            norm[...] = jnp.maximum(
                norm[...],
                jnp.max(jnp.sum(jnp.square(turned[:head_dim]), axis=0, keepdims=True), axis=1, keepdims=True),
            )
            return 0

        lax.fori_loop(0, k_ref.shape[0] // BLOCK, fill, 0)

    zero = jnp.zeros((1, heads * CHUNK), f32)
    q = wide(q_ref[...], heads, head_dim)
    q_aug = scaled_queries(q, head_dim, [zero, zero, zero], row)
    q_norm = jnp.max(jnp.sum(jnp.square(q.astype(f32)), axis=0, keepdims=True), axis=1, keepdims=True)
    limit = (SAFE / LOG2E) ** 2 * head_dim
    safe = jnp.max(jnp.where(q_norm * norm[...] < limit, 1, 0)) > 0

    def scores(j):
        off = pl.multiple_of(end - (j + 1) * BLOCK, CHUNK)
        return contract(k_ref[pl.ds(off, BLOCK), :], q_aug, 1, 0)

    def values(j):
        off = pl.multiple_of(end - (j + 1) * BLOCK, CHUNK)
        return vt_ref[:, pl.ds(off, BLOCK)]

    @pl.when(safe)
    def _():
        p = jnp.exp2(causal(scores(0), heads)).astype(bf16)
        acc[...] = contract(values(0), p, 1, 0)

        def step(j, _):
            p = jnp.exp2(scores(j)).astype(bf16)
            acc[...] += contract(values(j), p, 1, 0)
            return 0

        lax.fori_loop(1, blocks, step, 0)
        top[...] = jnp.zeros_like(top)

    @pl.when(jnp.logical_not(safe))
    def _():
        s = causal(scores(0), heads)
        m = jnp.max(s, axis=0, keepdims=True)
        top[...] = m
        acc[...] = contract(values(0), jnp.exp2(s - m).astype(bf16), 1, 0)

        def step(j, _):
            s = scores(j)
            old = top[...]
            m = jnp.maximum(old, jnp.max(s, axis=0, keepdims=True))
            top[...] = m
            p = jnp.exp2(s - m).astype(bf16)
            acc[...] = acc[...] * jnp.exp2(old - m) + contract(values(j), p, 1, 0)
            return 0

        lax.fori_loop(1, blocks, step, 0)

    total = acc[head_dim : head_dim + 1, :]
    attended = tall(acc[:head_dim, :] / total, heads)
    o_ref[...] = attended.astype(bf16)
    rest_ref[...] = (attended - attended.astype(bf16).astype(f32)).astype(bf16)
    lse_ref[0] = top[...] + jnp.log2(total)


def feed_phase(
    att_ref, wo_hbm, tok_ref, cot_hbm, vecs, upb_ref, up_hbm, down_hbm,
    out_hbm, res_ref, gatt_ref, mat,
    up_buf, down_buf, normal, out_acc, gn_acc, wo_ref, cot_ref, out_ref, fetch, piece_done,
):
    tile = mat.shape[1] // 2
    tiles = up_hbm.shape[1] // tile
    width = up_hbm.shape[0]
    out_bias, gain, shift, down_bias = (line(ref) for ref in vecs)

    def fetches(t, slot):
        at = pl.ds(pl.multiple_of(t * tile, tile), tile)
        return (
            pltpu.make_async_copy(up_hbm.at[:, at], up_buf.at[slot], fetch.at[0, slot]),
            pltpu.make_async_copy(down_hbm.at[at], down_buf.at[slot], fetch.at[1, slot]),
        )

    wo_copy = pltpu.make_async_copy(wo_hbm, wo_ref, fetch.at[2, 0])
    cot_copy = pltpu.make_async_copy(cot_hbm, cot_ref, fetch.at[2, 1])
    wo_copy.start()
    for copy in fetches(0, 0):
        copy.start()
    cot_copy.start()
    wo_copy.wait()

    residual = tok_ref[...].astype(f32) + contract(att_ref[...], wo_ref[...], 0, 0) + out_bias
    res_ref[...] = residual
    normal[...] = normed(residual, gain, shift).astype(bf16)
    out_acc[...] = residual + down_bias
    gn_acc[...] = jnp.zeros_like(gn_acc)
    sums = mat.shape[0] - 1
    cot_copy.wait()

    def step(t, _):
        slot = t % 2
        for copy in fetches(t, slot):
            copy.wait()

        @pl.when(t + 1 < tiles)
        def _():
            for copy in fetches(t + 1, 1 - slot):
                copy.start()

        u = contract(normal[...], up_buf[slot], 1, 0) + upb_ref[t]
        square = u * u
        th = jnp.tanh(GELU * (u + 0.044715 * (u * square)))
        half = 0.5 * (1.0 + th)
        slope = half + (0.5 * GELU) * u * (1.0 - th * th) * (1.0 + 3 * 0.044715 * square)
        activated = (u * half).astype(bf16)
        out_acc[...] += contract(activated, down_buf[slot], 1, 0)
        mat[t, tile:, :] = contract(activated, cot_ref[...], 0, 0).astype(bf16)
        grad = (contract(cot_ref[...], down_buf[slot], 1, 1) * slope).astype(bf16)
        gn_acc[...] += contract(grad, up_buf[slot], 1, 1)
        mat[t, :tile, :] = contract(grad, normal[...], 0, 0).astype(bf16)
        upb_ref[t] = jnp.sum(grad.astype(f32), axis=0, keepdims=True)
        piece_done(t)
        return 0

    lax.fori_loop(0, tiles, step, 0)
    out_ref[...] = out_acc[...].astype(bf16)
    out_copy = pltpu.make_async_copy(out_ref, out_hbm, fetch.at[2, 0])
    out_copy.start()

    residual = res_ref[...]
    center = residual - jnp.mean(residual, axis=-1, keepdims=True)
    scale = lax.rsqrt(jnp.mean(center * center, axis=-1, keepdims=True) + epsilon)
    xhat = center * scale
    gn = gn_acc[...]
    q = gn * gain
    grad = scale * (
        q - jnp.mean(q, axis=-1, keepdims=True) - xhat * jnp.mean(q * xhat, axis=-1, keepdims=True)
    )
    cot = cot_ref[...].astype(f32)
    grad = cot + grad
    res_ref[...] = grad
    proj = grad.astype(bf16)
    mat[sums, :width, :] = contract(att_ref[...], proj, 1, 0).astype(bf16)
    rows = [cot, proj.astype(f32), gn * xhat, gn]
    rows = [jnp.sum(row, axis=0, keepdims=True) for row in rows]
    rows.append(jnp.zeros((16 - len(rows), width), f32))
    mat[sums, width : width + 16, :] = jnp.concatenate(rows, axis=0).astype(bf16)
    rows = [upb_ref[t] for t in range(tiles)] + [jnp.zeros((1, tile), f32)] * (16 - tiles)
    rows = jnp.concatenate([jnp.concatenate(rows, axis=0), jnp.zeros((16, width - tile), f32)], axis=1)
    mat[sums, width + 16 : width + 32, :] = rows.astype(bf16)
    rest = mat.shape[1] - width - 32
    mat[sums, width + 32 :, :] = jnp.zeros((rest, width), bf16)
    gatt_ref[...] = contract(wo_ref[...], proj, 1, 1).astype(bf16)
    out_copy.wait()


def back_phase(
    plan, heads, head_dim, me, talk, steps,
    q_hbm, k_hbm, v_hbm, kt_hbm, lse_ref, o_ref, rest_hbm, gatt_ref, dq_ref,
    low, inbox, kv_send, kv_recv,
    k_ref, v_ref, kt_ref, q_ref, q_mat, q_aug, g_aug, acc, total, rest_ref, fetch, prepared,
):
    shard_len = plan.shard_len
    copies = [
        pltpu.make_async_copy(src, dst, fetch.at[k])
        for k, (src, dst) in enumerate(
            [(q_hbm, q_ref), (rest_hbm, rest_ref), (k_hbm, k_ref), (v_hbm, v_ref), (kt_hbm, kt_ref)]
        )
    ]
    for copy in copies:
        copy.start()
    total[...] = jnp.zeros_like(total)
    acc[...] = jnp.zeros_like(acc)
    for copy in copies[:2]:
        copy.wait()
    for i in range(plan.per_dev):
        at = pl.ds(i * CHUNK, CHUNK)
        q = wide(q_ref[:, at], heads, head_dim)
        q_mat[i] = q
        row = plan.chunk(me, i) // plan.per_row
        q_aug[i] = scaled_queries(q, head_dim, hi_lo(-lse_ref[i], 3), row)
        g = wide(gatt_ref[:, at], heads, head_dim)
        o = wide(o_ref[:, at], heads, head_dim).astype(f32) + wide(rest_ref[:, at], heads, head_dim).astype(f32)
        delta = jnp.sum(g.astype(f32) * o, axis=0, keepdims=True)
        fill = jnp.zeros((head_dim - 3, heads * CHUNK), f32)
        marks = jnp.concatenate(hi_lo(-delta, 3) + [fill], axis=0).astype(bf16)
        g_aug[i] = jnp.concatenate([marks, g], axis=0)
    prepared()
    for copy in copies[2:]:
        copy.wait()

    def piece(off, source, holder):
        at = pl.ds(pl.multiple_of(plan.place(source, holder), CHUNK), shard_len)
        return remote(low.at[:, at], inbox.at[off - 1], kv_send.at[off - 1], kv_recv.at[off - 1], source)

    def block(i, at, place, diagonal):
        s = contract(k_ref[at, :], q_aug[i], 1, 0)
        if diagonal:
            key = lax.broadcasted_iota(jnp.int32, (BLOCK, heads * CHUNK), 0)
            query = lax.broadcasted_iota(jnp.int32, (BLOCK, heads * CHUNK), 1) % CHUNK
            s = jnp.where(key - query <= place % (BLOCK // CHUNK) * CHUNK, s, BIG)
        dp = contract(v_ref[at, :], g_aug[i], 1, 0)
        p = jnp.exp2(s)
        ds = (p * dp).astype(bf16)
        p = p.astype(bf16)
        acc[i] += contract(kt_ref[:, at], ds, 1, 0)
        total[:head_dim, at] += contract(q_mat[i], ds, 1, 1)
        total[head_dim:, at] += contract(g_aug[i, head_dim:, :], p, 1, 1)

    def key_step(b, n):
        at = pl.ds(pl.multiple_of(MARGIN + b * BLOCK, BLOCK), BLOCK)

        def chunk_step(i, n):
            place = plan.chunk(me, i)
            last = place // (BLOCK // CHUNK)
            active = (b <= last) & (b // (ROW // BLOCK) == place // plan.per_row)

            @pl.when(active)
            def _():
                talk(n)

            @pl.when(active & (b < last))
            def _():
                block(i, at, place, False)

            @pl.when(b == last)
            def _():
                block(i, at, place, True)

            return n + jnp.where(active, 1, 0)

        n = lax.fori_loop(0, plan.per_dev, chunk_step, n)
        for off in range(1, plan.reach + 1):
            end = plan.place(me - off, me) + shard_len - MARGIN

            @pl.when(plan.feeds(me - off, me) & (b == (end + BLOCK - 1) // BLOCK - 1))
            def _():
                at = pl.ds(pl.multiple_of(plan.place(me - off, me), CHUNK), shard_len)
                low[:head_dim, at] = (total[:head_dim, at] * head_dim ** (-0.5)).astype(bf16)
                low[head_dim:, at] = total[head_dim:, at].astype(bf16)
                piece(off, me - off, me).start()

        return n

    done = lax.fori_loop(0, plan.span // BLOCK, key_step, steps)
    for i in range(plan.per_dev):
        dq_ref[:, i * CHUNK : (i + 1) * CHUNK] = tall(acc[i] * head_dim ** (-0.5), heads).astype(bf16)
    own = pl.ds(pl.multiple_of(plan.place(me, me), CHUNK), shard_len)
    acc_kv = total[:, own]
    total[:, :shard_len] = jnp.concatenate(
        [acc_kv[:head_dim] * head_dim ** (-0.5), acc_kv[head_dim:]], axis=0
    )
    return done


def layer_kernel(
    plan, heads, head_dim,
    att_ref, tok_ref, ob_ref, gain_ref, shift_ref, db_ref, upb_ref, lse_ref, gain_one_ref,
    wo_hbm, cot_hbm, up_hbm, down_hbm, rest_hbm, q_hbm, k_hbm, v_hbm, kt_hbm, normal_hbm, wq_hbm, wkv_hbm,
    sum_ref, out_hbm, end_mat, res_ref,
    gatt_ref, low, inbox, mat, upb_mat, feed_fetch, back_fetch, kv_send, kv_recv, load, *summing,
):
    me = lax.axis_index("seq")
    shard_len, width = tok_ref.shape
    pieces, height, _ = mat.shape
    half = len(summing) // 2
    summed = Summing(plan, pieces, height, mat, *summing[:2], summing[2:half])
    ending = Summing(plan, *end_mat.shape[:2], end_mat, *summing[half : half + 2], summing[half + 2 :])
    starts = summed.starts(DELAYS)
    greet(plan, me, summed.partners())
    for t in range(upb_mat.shape[0]):
        wide_t = upb_mat.shape[2]
        upb_mat[t] = upb_ref[pl.ds(t * wide_t, wide_t)].reshape(1, wide_t)

    def store(p):
        pltpu.make_async_copy(mat.at[p], sum_ref.at[p], load.at[p]).start()

    def talk(n):
        summed.step(n, starts, None, store)

    def first(up_buf, down_buf, normal, out_acc, gn_acc, wo_ref, cot_ref, out_ref):
        feed_phase(
            att_ref, wo_hbm, tok_ref, cot_hbm, (ob_ref, gain_ref, shift_ref, db_ref), upb_mat, up_hbm, down_hbm,
            out_hbm, res_ref, gatt_ref, mat,
            up_buf, down_buf, normal, out_acc, gn_acc, wo_ref, cot_ref, out_ref, feed_fetch, talk,
        )

    tile = height // 2
    pl.run_scoped(
        first,
        pltpu.VMEM((2, width, tile), bf16),
        pltpu.VMEM((2, tile, width), bf16),
        pltpu.VMEM((shard_len, width), bf16),
        pltpu.VMEM((shard_len, width), f32),
        pltpu.VMEM((shard_len, width), f32),
        pltpu.VMEM((width, width), bf16),
        pltpu.VMEM((shard_len, width), bf16),
        pltpu.VMEM((shard_len, width), bf16),
    )
    talk(pieces - 1)
    window, columns = plan.window, heads * CHUNK
    chunks = plan.per_dev

    def second(k_ref, v_ref, kt_ref, q_ref, q_mat, q_aug, g_aug, acc, total, spare, wkv):
        copies = [
            pltpu.make_async_copy(src, dst, back_fetch.at[5 + k])
            for k, (src, dst) in enumerate([(normal_hbm, gatt_ref), (wq_hbm, spare), (wkv_hbm, wkv)])
        ]

        def later():
            for copy in copies:
                copy.start()

        done = back_phase(
            plan, heads, head_dim, me, talk, pieces,
            q_hbm, k_hbm, v_hbm, kt_hbm, lse_ref, att_ref, rest_hbm, gatt_ref, q_ref,
            low, inbox, kv_send, kv_recv,
            k_ref, v_ref, kt_ref, q_ref, q_mat, q_aug, g_aug, acc, total, spare, back_fetch, later,
        )

        for copy in copies:
            copy.wait()
        normal, wq = gatt_ref, spare
        end_height = end_mat.shape[1]
        grad = contract(normal[...], q_ref[...], 0, 1).astype(bf16)
        end_mat[0] = grad[:end_height]
        end_mat[1, : width - end_height, :] = grad[end_height:]
        ending.event(0, 0)
        grad_qb = jnp.sum(q_ref[...].astype(f32).T, axis=0, keepdims=True)
        gn = contract(q_ref[...], wq[...], 0, 1)

        def drain(n, _):
            talk(n)
            return 0

        lax.fori_loop(done, starts[-1] + pieces, drain, 0)
        for off in range(1, plan.reach + 1):

            @pl.when(plan.feeds(me, me + off))
            def _():
                at = pl.ds(pl.multiple_of(plan.place(me, me + off), CHUNK), shard_len)
                remote(
                    low.at[:, at], inbox.at[off - 1], kv_send.at[off - 1], kv_recv.at[off - 1], me + off
                ).wait_recv()
                total[:, :shard_len] += inbox[off - 1].astype(f32)

            @pl.when(plan.feeds(me - off, me))
            def _():
                at = pl.ds(pl.multiple_of(plan.place(me - off, me), CHUNK), shard_len)
                remote(
                    low.at[:, at], inbox.at[off - 1], kv_send.at[off - 1], kv_recv.at[off - 1], me - off
                ).wait_send()

        grad_kv = total[:, :shard_len].astype(bf16)
        gn = gn + contract(grad_kv, wkv[...], 0, 1)
        at = width - end_height
        end_mat[1, at : at + 2 * head_dim, :] = contract(grad_kv, normal[...], 1, 0).astype(bf16)
        grad_vb = jnp.sum(grad_kv.astype(f32).T, axis=0, keepdims=True)

        tok = tok_ref[...].astype(f32)
        center = tok - jnp.mean(tok, axis=-1, keepdims=True)
        scale = lax.rsqrt(jnp.mean(center * center, axis=-1, keepdims=True) + epsilon)
        xhat = center * scale
        grads = [gn * xhat, gn]
        rows = [jnp.sum(grad, axis=0, keepdims=True) for grad in grads] + [grad_qb]
        rows.append(jnp.concatenate([grad_vb, jnp.zeros((1, width - 2 * head_dim), f32)], axis=1))
        rows.append(jnp.zeros((16 - len(rows), width), f32))
        at = at + 2 * head_dim
        end_mat[1, at : at + 16, :] = jnp.concatenate(rows, axis=0).astype(bf16)
        end_mat[1, at + 16 :, :] = jnp.zeros((end_height - at - 16, width), bf16)
        ending.event(0, 1)
        q = gn * line(gain_one_ref)
        res_ref[...] += scale * (
            q - jnp.mean(q, axis=-1, keepdims=True) - xhat * jnp.mean(q * xhat, axis=-1, keepdims=True)
        )

        for stage in range(1, ending.stages + 1):
            for p in range(2):
                ending.event(stage, p)

    pl.run_scoped(
        second,
        pltpu.VMEM((window, 4 * head_dim), bf16),
        pltpu.VMEM((window, 2 * head_dim), bf16),
        pltpu.VMEM((head_dim, window), bf16),
        pltpu.VMEM((width, shard_len), bf16),
        pltpu.VMEM((chunks, head_dim, columns), bf16),
        pltpu.VMEM((chunks, 4 * head_dim, columns), bf16),
        pltpu.VMEM((chunks, 2 * head_dim, columns), bf16),
        pltpu.VMEM((chunks, head_dim, columns), f32),
        pltpu.VMEM((2 * head_dim, window), f32),
        pltpu.VMEM(wq_hbm.shape, bf16),
        pltpu.VMEM(wkv_hbm.shape, bf16),
    )
    for p in range(pieces):
        pltpu.make_async_copy(mat.at[p], sum_ref.at[p], load.at[p]).wait()


def final_kernel(
    head_dim,
    sum_ref, rest_ref, last_ref,
    up_ref, down_ref, out_ref, q_ref, kv_ref, upb_ref,
    db_ref, ob_ref, gain_two_ref, shift_two_ref, gain_one_ref, shift_one_ref, qb_ref, vb_ref,
):
    i = pl.program_id(0)
    tile, width = down_ref.shape
    up_ref[...] = sum_ref[0, :tile, :].astype(f32).T
    down_ref[...] = sum_ref[0, tile:, :].astype(f32)

    @pl.when(i == 0)
    def _():
        out_ref[...] = rest_ref[0, :width, :].astype(f32)
        q_ref[:tile, :] = last_ref[0].astype(f32)
        at = width - tile
        q_ref[tile:, :] = last_ref[1, :at, :].astype(f32)
        kv_ref[...] = last_ref[1, at : at + 2 * head_dim, :].astype(f32).T
        rows = rest_ref[0, width : width + 32, :].astype(f32)
        for k, ref in enumerate([db_ref, ob_ref, gain_two_ref, shift_two_ref]):
            ref[...] = rows[k : k + 1].reshape(width)
        for t in range(upb_ref.shape[0] // tile):
            upb_ref[pl.ds(t * tile, tile)] = rows[16 + t : 17 + t, :tile].reshape(tile)
        at = at + 2 * head_dim
        rows = last_ref[1, at : at + 16, :].astype(f32)
        for k, ref in enumerate([gain_one_ref, shift_one_ref, qb_ref]):
            ref[...] = rows[k : k + 1].reshape(width)
        vb_ref[...] = rows[3:4, head_dim : 2 * head_dim].reshape(head_dim)


def whole(shape):
    return pl.BlockSpec(shape, lambda i: (0,) * len(shape))


def column(height):
    return pl.BlockSpec((height, CHUNK), lambda i: (0, i))


def lead(shape):
    return pl.BlockSpec((1,) + shape, lambda i: (i,) + (0,) * len(shape))


def per_device(
    plan,
    tokens,
    lengths,
    cotangent,
    norm1_gain,
    norm1_shift,
    query_weight,
    query_bias,
    keyval_weight,
    value_bias,
    out_weight,
    out_bias,
    norm2_gain,
    norm2_shift,
    up_weight,
    up_bias,
    down_weight,
    down_bias,
):
    shard_len, width = tokens.shape[1:]
    head_dim = keyval_weight.shape[1] // 2
    heads = width // head_dim
    columns = heads * CHUNK
    chunks = plan.per_dev
    window = plan.window
    reach = plan.reach
    limit = dict(vmem_limit_bytes=63 * 2**20)
    vmem = pl.BlockSpec(memory_space=pltpu.VMEM)
    anywhere = pl.BlockSpec(memory_space=pl.ANY)
    dma = pltpu.SemaphoreType.DMA

    normal_one, queries, keyvals = pl.pallas_call(
        partial(gather_kernel, plan),
        in_specs=[vmem] * 7,
        out_specs=[vmem] * 3,
        out_shape=[
            jax.ShapeDtypeStruct((shard_len, width), bf16),
            jax.ShapeDtypeStruct((width, shard_len), bf16),
            jax.ShapeDtypeStruct((window, 2 * head_dim), bf16),
        ],
        scratch_shapes=[pltpu.VMEM((shard_len, 2 * head_dim), bf16)] + [dma((reach,))] * 2,
        compiler_params=pltpu.CompilerParams(collective_id=0, has_side_effects=True, **limit),
        name="gather",
    )(
        tokens[0],
        norm1_gain,
        norm1_shift,
        keyval_weight,
        value_bias,
        query_weight,
        query_bias,
    )

    attended, attended_low, lse, k_aug, v_aug, k_turned = pl.pallas_call(
        partial(attend_kernel, plan, heads, head_dim),
        grid_spec=pltpu.PrefetchScalarGridSpec(
            num_scalar_prefetch=0,
            grid=(chunks,),
            in_specs=[
                pl.BlockSpec(memory_space=pltpu.SMEM),
                column(width),
                whole((window, 2 * head_dim)),
            ],
            out_specs=[
                column(width),
                column(width),
                lead((1, columns)),
                whole((window, 4 * head_dim)),
                whole((window, 2 * head_dim)),
                whole((head_dim, window)),
            ],
            scratch_shapes=[
                pltpu.VMEM((head_dim + 16, window), bf16),
                pltpu.VMEM((head_dim + 16, columns), f32),
                pltpu.VMEM((1, columns), f32),
                pltpu.VMEM((1, 1), f32),
            ],
        ),
        out_shape=[
            jax.ShapeDtypeStruct((width, shard_len), bf16),
            jax.ShapeDtypeStruct((width, shard_len), bf16),
            jax.ShapeDtypeStruct((chunks, 1, columns), f32),
            jax.ShapeDtypeStruct((window, 4 * head_dim), bf16),
            jax.ShapeDtypeStruct((window, 2 * head_dim), bf16),
            jax.ShapeDtypeStruct((head_dim, window), bf16),
        ],
        compiler_params=pltpu.CompilerParams(**limit),
        name="attend",
    )(lengths, queries, keyvals)

    inputs = tokens[0].astype(f32)
    hidden = up_weight.shape[1]
    tile = PIECE // 2
    tiles = hidden // tile
    pieces = tiles + 1
    sums, outputs, last, grad_inputs = pl.pallas_call(
        partial(layer_kernel, plan, heads, head_dim),
        in_specs=[vmem] * 9 + [anywhere] * 12,
        out_specs=[anywhere] * 2 + [vmem] * 2,
        out_shape=[
            jax.ShapeDtypeStruct((pieces, PIECE, width), bf16),
            jax.ShapeDtypeStruct((shard_len, width), bf16),
            jax.ShapeDtypeStruct((2, tile, width), bf16),
            jax.ShapeDtypeStruct((shard_len, width), f32),
        ],
        scratch_shapes=[
            pltpu.VMEM((width, shard_len), bf16),
            pltpu.VMEM((2 * head_dim, window), bf16),
            pltpu.VMEM((reach, 2 * head_dim, shard_len), bf16),
            pltpu.VMEM((pieces, PIECE, width), bf16),
            pltpu.VMEM((tiles, 1, tile), f32),
            dma((3, 2)),
            dma((8,)),
            dma((reach,)),
            dma((reach,)),
            dma((pieces,)),
        ]
        + Summing.scratch(plan, pieces, PIECE, width)
        + Summing.scratch(plan, 2, tile, width),
        compiler_params=pltpu.CompilerParams(collective_id=1, has_side_effects=True, **limit),
        name="layer",
    )(
        attended,
        tokens[0],
        out_bias,
        norm2_gain,
        norm2_shift,
        down_bias,
        up_bias,
        lse,
        norm1_gain,
        out_weight,
        cotangent[0],
        up_weight,
        down_weight,
        attended_low,
        queries,
        k_aug,
        v_aug,
        k_turned,
        normal_one,
        query_weight,
        keyval_weight,
    )

    vector = jax.ShapeDtypeStruct((width,), f32)
    finals = pl.pallas_call(
        partial(final_kernel, head_dim),
        grid=(tiles,),
        in_specs=[
            lead((PIECE, width)),
            pl.BlockSpec((1, PIECE, width), lambda i: (tiles, 0, 0)),
            whole((2, tile, width)),
        ],
        out_specs=[
            pl.BlockSpec((width, tile), lambda i: (0, i)),
            pl.BlockSpec((tile, width), lambda i: (i, 0)),
            whole((width, width)),
            whole((width, width)),
            whole((width, 2 * head_dim)),
            whole((hidden,)),
        ]
        + [whole((width,))] * 7
        + [whole((head_dim,))],
        out_shape=[
            jax.ShapeDtypeStruct((width, hidden), f32),
            jax.ShapeDtypeStruct((hidden, width), f32),
            jax.ShapeDtypeStruct((width, width), f32),
            jax.ShapeDtypeStruct((width, width), f32),
            jax.ShapeDtypeStruct((width, 2 * head_dim), f32),
            jax.ShapeDtypeStruct((hidden,), f32),
        ]
        + [vector] * 7
        + [jax.ShapeDtypeStruct((head_dim,), f32)],
        compiler_params=pltpu.CompilerParams(**limit),
        name="finals",
    )(sums, sums, last)
    up_w, down_w, out_w, qw, kvw, up_b = finals[:6]
    down_b, out_b, gain_two, shift_two, gain_one, shift_one, qb, vb = finals[6:]
    return (
        outputs[None],
        grad_inputs[None],
        gain_one,
        shift_one,
        qw,
        qb,
        kvw,
        vb,
        out_w,
        out_b,
        gain_two,
        shift_two,
        up_w,
        up_b,
        down_w,
        down_b,
    )


def solution(mesh):
    split = P("dp", "seq", None)
    devices = mesh.shape["seq"]

    def run(*arrays):
        plan = Plan(devices, arrays[0].shape[1] // devices)
        return jax.shard_map(
            partial(per_device, plan),
            mesh=mesh,
            in_specs=(split, P("dp", None), split) + (P(),) * 14,
            out_specs=(split, split) + (P(),) * 14,
            check_vma=False,
        )(*arrays)

    return run
```

```python
from functools import partial

import jax
import jax.numpy as jnp
import numpy as np
from jax import lax
from jax.experimental import pallas as pl
from jax.experimental.pallas import tpu as pltpu
from jax.sharding import PartitionSpec as P

ROW = 4096
CHUNK = 128
BLOCK = 512
PAD = BLOCK - CHUNK
LOG2E = 1.4426950408889634
BIG = -1e30
MARGIN = BLOCK
PIECE = 1024
ORDERS = ((0, 1, 2), (2, 0, 1), (2, 0, 1), (1, 0, 2), (0, 2, 1), (2, 1, 0), (1, 0, 2))
TABLE = (
    (4, 5, 6, 8, 11, 12, 17),
    (8, 6, 10, 9, 13, 15, 21),
    (12, 11, 15, 24, 21, 26, 30),
    (15, 18, 19, 27, 31, 30, 35),
    (18, 25, 22, 31, 37, 34, 41),
    (23, 31, 26, 35, 42, 36, 44),
    (27, 36, 30, 39, 51, 45, 49),
    (42, 38, 36, 41, 57, 47, 59),
    (48, 42, 46, 44, 63, 61, 66),
    (56, 57, 54, 73, 77, 80, 81),
    (86, 70, 57, 75, 84, 88, 83),
)
LAST_ORDERS = ((0, 2, 1), (2, 0, 1), (1, 0, 2))
LAST_TABLE = (
    (49, 50, 51),
    (50, 52, 53),
    (55, 56, 57),
    (57, 58, 59),
    (59, 60, 64),
    (62, 65, 67),
    (69, 68, 70),
    (72, 71, 74),
    (78, 76, 79),
    (85, 82, 87),
    (89, 90, 91),
)
SAFE = 60.0
epsilon = 1e-05
GELU = 0.7978845608028654
bf16 = jnp.bfloat16
f32 = jnp.float32


HELP = (
    (4, 4, 0, 0), (4, 5, 0, 1), (3, 5, 1, 0), (10, 3, 6, 0), (9, 4, 6, 1), (9, 5, 7, 0),
    (15, 4, 11, 0), (15, 5, 11, 1), (14, 5, 12, 0),
)
UNIT = 16


class Plan:
    def __init__(self, devices, shard_len):
        self.devices = devices
        self.shard_len = shard_len
        self.per_dev = shard_len // CHUNK
        self.per_row = ROW // CHUNK
        assert shard_len % CHUNK == 0 and shard_len <= ROW
        ends = [(d + 1) * shard_len - self.first_row(d) * ROW for d in range(devices)]
        self.span = -(-max(ends) // BLOCK) * BLOCK
        self.window = MARGIN + self.span
        self.help = HELP if devices % UNIT == 0 and shard_len * UNIT == 3 * ROW else ()
        self.slots = 2
        self.top = {}
        for home, _, helper, _ in self.help:
            self.top[helper] = max(home, self.top.get(helper, 0))
        helpers = sorted(self.top)
        self.kinds = {helper: k % 2 for k, helper in enumerate(helpers)}
        self.reach = max(
            d - e for d in range(devices) for e in range(d + 1) if self.first_row(d) <= self.last_row(e)
        )
        self.skips = sorted({self.skip(d, h) for d in range(devices) for h in range(d, min(d + self.reach + 1, devices))
                             if self.first_row(h) <= self.last_row(d)})
        self.blocks = max(self.load(d) for d in range(devices))
        self.offsets = [o for o in range(-self.reach, self.reach + 1) if o != 0]
        self.inboxes = self.reach + 2

    def load(self, device):
        def blocks(d, i):
            return self.chunk(d, i) % self.per_row // (BLOCK // CHUNK) + 1

        unit, place = device // UNIT * UNIT, device % UNIT
        moved = {(home, i) for home, i, _, _ in self.help}
        total = sum(blocks(device, i) for i in range(self.per_dev) if (place, i) not in moved)
        return total + sum(blocks(unit + home, i) for home, i, helper, _ in self.help if helper == place)

    def first_row(self, device):
        return device * self.shard_len // ROW

    def last_row(self, device):
        return ((device + 1) * self.shard_len - 1) // ROW

    def lookup(self, device, table, default):
        place = device % UNIT
        value = default
        for key, entry in table.items():
            value = jnp.where(place == key, entry, value)
        return value

    def reaches(self, device):
        extra = {helper: top - helper for helper, top in self.top.items()}
        return device + self.lookup(device, extra, 0)

    def helps(self, device):
        return self.lookup(device, {helper: 1 for helper in self.top}, 0)

    def feeds(self, source, holder):
        return (
            (source >= 0)
            & (holder >= 0)
            & (source < self.devices)
            & (holder < self.devices)
            & (self.first_row(holder) <= self.last_row(source))
            & (source <= self.reaches(holder))
        )

    def given(self, device, i):
        place = device % UNIT
        found, helper, slot, order = 0, 0, 0, 0
        counts = {}
        for home, chunk, to, k in self.help:
            here = jnp.where((place == home) & (i == chunk), 1, 0)
            found, slot = found + here, slot + here * k
            helper = helper + here * (to - home)
            order = order + here * counts.get(home, 0)
            counts[home] = counts.get(home, 0) + 1
        return found, device + helper, slot, order

    def taken(self, device, k):
        place = device % UNIT
        found, home, i, order = 0, 0, 0, 0
        counts = {}
        for owner, chunk, helper, slot in self.help:
            here = jnp.where((place == helper) & (k == slot), 1, 0)
            found, i = found + here, i + here * chunk
            home = home + here * (owner - helper)
            order = order + here * counts.get(owner, 0)
            counts[owner] = counts.get(owner, 0) + 1
        return found, device + home, i, order

    def box(self, owner, off):
        return off - 1 if off > 0 else self.reach + self.lookup(owner + off, self.kinds, 0)

    def skip(self, source, holder):
        gap = self.first_row(holder) * ROW - source * self.shard_len
        return max(gap, 0) if isinstance(gap, int) else jnp.where(gap > 0, gap, 0)

    def pairs(self, source, holder):
        return [(self.feeds(source, holder) & (self.skip(source, holder) == left), left) for left in self.skips]

    def place(self, source, holder):
        return MARGIN + source * self.shard_len - self.first_row(holder) * ROW

    def chunk(self, device, i, holder=None):
        return device * self.per_dev + i - self.first_row(device if holder is None else holder) * self.per_row


class Summing:
    def __init__(self, plan, orders, table, height, mat, inbox, extra, sems):
        self.pieces, self.height, self.orders = len(orders), height, orders
        self.mat, self.inbox, self.extra = mat, inbox, extra
        self.out_send, self.out_recv, self.back_send, self.back_recv, self.free = sems
        self.bits = plan.devices.bit_length() - 1
        self.halvings = 1 + min(self.bits, 4)
        self.swaps = self.bits + 1 - self.halvings
        self.stages = 2 * self.halvings + self.swaps
        if len(table) != self.stages + 1:
            table = [[start + 3 * s for start in table[0]] for s in range(self.stages + 1)]
        self.table = table
        self.end = max(max(row) for row in table) + 1
        self.seq, self.dp = lax.axis_index("seq"), lax.axis_index("dp")

    @staticmethod
    def scratch(plan, pieces, height, width):
        bits = plan.devices.bit_length() - 1
        halvings = 1 + min(bits, 4)
        swaps = bits + 1 - halvings
        last = height >> halvings
        dma = pltpu.SemaphoreType.DMA
        return [
            pltpu.VMEM((pieces, height - last, width), bf16),
            pltpu.VMEM((max(swaps, 1), pieces, last, width), bf16),
            dma((halvings + swaps, pieces)),
            dma((halvings + swaps, pieces)),
            dma((halvings, pieces)),
            dma((halvings, pieces)),
            pltpu.SemaphoreType.REGULAR((halvings, pieces)),
        ]

    def partners(self):
        bits = [(self.seq >> b) & 1 for b in range(self.bits)]
        return [(self.seq, 1 - self.dp)] + [
            (self.seq + (1 - 2 * bit) * (1 << b), self.dp) for b, bit in enumerate(bits)
        ]

    def spots(self, p, count):
        spots, starts, at = [], [0], 0
        for t in range(count):
            if t == 0:
                bit, device = self.dp, {"seq": self.seq, "dp": 1 - self.dp}
            else:
                if t < 4:
                    word = sum(order[t - 1] << (2 * k) for k, order in enumerate(self.orders))
                    axis = lax.shift_right_logical(np.int32(word), 2 * p) & 3
                else:
                    axis = t - 1
                bit = lax.shift_right_logical(self.seq, axis) & 1
                step = lax.shift_left(np.int32(1), axis) if t < 4 else 1 << axis
                device = {"seq": self.seq + (1 - 2 * bit) * step, "dp": self.dp}
            spots.append((bit, device))
            at = at + bit * (self.height >> (t + 1))
            starts.append(at)
        return spots, starts

    def rows(self, start, size):
        return pl.ds(pl.multiple_of(start, size), size)

    def remote(self, src, dst, sems, device):
        return pltpu.make_async_remote_copy(
            src_ref=src,
            dst_ref=dst,
            send_sem=sems[0],
            recv_sem=sems[1],
            device_id=device,
            device_id_type=pl.DeviceIdType.MESH,
        )

    def sems(self, stage, p):
        if stage < self.halvings + self.swaps:
            return self.out_send.at[stage, p], self.out_recv.at[stage, p]
        t = self.stages - 1 - stage
        return self.back_send.at[t, p], self.back_recv.at[t, p]

    def size(self, stage):
        h, w = self.halvings, self.swaps
        t = stage if stage < h else h - 1 if stage < h + w else self.stages - 1 - stage
        return self.height >> (t + 1)

    def event(self, stage, p):
        h, w, last = self.halvings, self.swaps, self.stages
        depth = min(stage + 1, h + w) if stage < h + w else last - stage
        spots, starts = self.spots(p, max(depth, 1))
        if stage > 0:
            before = stage - 1
            size = self.size(before)
            some = self.mat.at[p, pl.ds(0, size)]
            wait = self.remote(some, some, self.sems(before, p), spots[0][1])
            wait.wait()
            if before < h:
                at = self.rows(starts[before + 1], size)
                self.mat[p, at, :] = self.mat[p, at, :] + self.inbox[p, pl.ds(self.height - 2 * size, size), :]
                pl.semaphore_signal(
                    self.free.at[before, p],
                    inc=1,
                    device_id=spots[before][1],
                    device_id_type=pl.DeviceIdType.MESH,
                )
            elif before < h + w:
                at = self.rows(starts[h], size)
                self.mat[p, at, :] = self.mat[p, at, :] + self.extra[before - h, p]
        if stage < h:
            size = self.size(stage)
            bit, device = spots[stage]
            src = self.mat.at[p, self.rows(starts[stage] + (1 - bit) * size, size)]
            dst = self.inbox.at[p, pl.ds(self.height - 2 * size, size)]
            self.remote(src, dst, self.sems(stage, p), device).start()
        elif stage < h + w:
            src = self.mat.at[p, self.rows(starts[h], self.size(stage))]
            self.remote(src, self.extra.at[stage - h, p], self.sems(stage, p), spots[stage][1]).start()
        elif stage < last:
            t = last - 1 - stage
            pl.semaphore_wait(self.free.at[t, p], 1)
            src = self.mat.at[p, self.rows(starts[t + 1], self.size(stage))]
            self.remote(src, src, self.sems(stage, p), spots[t][1]).start()

    def step(self, n, last=None):
        for stage in range(self.stages, -1, -1):
            p = -1
            for k, step in enumerate(self.table[stage]):
                p = jnp.where(n == step, k, p)

            @pl.when(p >= 0)
            def _():
                self.event(stage, p)
                if stage == self.stages and last is not None:
                    last(p)


def line(ref):
    return ref[...].reshape(1, ref.shape[0])


def remote(src, dst, send, recv, device):
    return pltpu.make_async_remote_copy(
        src_ref=src,
        dst_ref=dst,
        send_sem=send,
        recv_sem=recv,
        device_id={"seq": device},
        device_id_type=pl.DeviceIdType.MESH,
    )


def greet(plan, me, others=()):
    barrier = pltpu.get_barrier_semaphore()
    count = len(others)
    for seq, dp in others:
        pl.semaphore_signal(
            barrier, inc=1, device_id={"seq": seq, "dp": dp}, device_id_type=pl.DeviceIdType.MESH
        )
    for off in plan.offsets:
        there = plan.feeds(me, me + off) | plan.feeds(me + off, me)
        count = count + jnp.where(there, 1, 0)

        @pl.when(there)
        def _():
            pl.semaphore_signal(
                barrier, inc=1, device_id={"seq": me + off}, device_id_type=pl.DeviceIdType.MESH
            )

    pl.semaphore_wait(barrier, count)


def gather_kernel(
    plan,
    tok_ref, gain_ref, shift_ref, wkv_ref, kvb_ref, wq_ref, qb_ref,
    normal_ref, q_ref, win_ref, taken_ref,
    kv_ref, kv_send, kv_recv, q_send, q_recv,
):
    me = lax.axis_index("seq")
    greet(plan, me)

    def copy(k, source, holder, left, device):
        size = plan.shard_len - left
        at = pl.multiple_of(plan.place(source, holder) + left, CHUNK)
        return remote(
            kv_ref.at[pl.ds(left, size)], win_ref.at[pl.ds(at, size)], kv_send.at[k], kv_recv.at[k], device
        )

    givable = sorted({entry[1] for entry in plan.help})

    def handed(i):
        found, helper, slot, order = plan.given(me, i)
        return found > 0, remote(
            q_ref.at[:, pl.ds(i * CHUNK, CHUNK)], taken_ref.at[slot], q_send.at[order], q_recv.at[slot], helper
        )

    normal = normed(tok_ref[...].astype(f32), line(gain_ref), line(shift_ref)).astype(bf16)
    normal_ref[...] = normal
    bias = line(kvb_ref)
    bias = jnp.concatenate([jnp.zeros_like(bias), bias], axis=1)
    kv_ref[...] = (contract(normal, wkv_ref[...], 1, 0) + bias).astype(bf16)
    for k, off in enumerate(plan.offsets):

        for there, left in plan.pairs(me, me + off):

            @pl.when(there)
            def _():
                copy(k, me, me + off, left, me + off).start()

    own = pl.multiple_of(plan.place(me, me), CHUNK)
    win_ref[pl.ds(own, plan.shard_len), :] = kv_ref[...]
    q_ref[...] = (contract(normal, wq_ref[...], 1, 0) + line(qb_ref)).T.astype(bf16)
    for i in givable:
        there, hand = handed(i)

        @pl.when(there)
        def _():
            hand.start()

    for k, off in enumerate(plan.offsets):
        for there, left in plan.pairs(me, me + off):

            @pl.when(there)
            def _():
                copy(k, me, me + off, left, me + off).wait_send()

        for there, left in plan.pairs(me - off, me):

            @pl.when(there)
            def _():
                copy(k, me - off, me, left, me - off).wait_recv()

    for i in givable:
        there, hand = handed(i)

        @pl.when(there)
        def _():
            hand.wait_send()

    for k in range(plan.slots):
        found, home, _, _ = plan.taken(me, k)

        @pl.when(found > 0)
        def _():
            remote(taken_ref.at[k], taken_ref.at[k], q_send.at[k], q_recv.at[k], home).wait_recv()


def normed(values, gains, shifts):
    center = values - jnp.mean(values, axis=-1, keepdims=True)
    spread = jnp.mean(center * center, axis=-1, keepdims=True)
    return center * lax.rsqrt(spread + epsilon) * gains + shifts


def contract(left_op, right_op, left_dim, right_dim):
    return lax.dot_general(
        left_op, right_op, (((left_dim,), (right_dim,)), ((), ())), preferred_element_type=f32
    )


def wide(block, heads, head_dim):
    return jnp.concatenate([block[h * head_dim : (h + 1) * head_dim] for h in range(heads)], axis=1)


def tall(block, heads):
    return jnp.concatenate([block[:, h * CHUNK : (h + 1) * CHUNK] for h in range(heads)], axis=0)


def hi_lo(value, count):
    parts = []
    for _ in range(count):
        part = value.astype(bf16)
        parts.append(part.astype(f32))
        value = value - parts[-1]
    return parts


def scaled_queries(q, head_dim, lse_parts, row):
    width = q.shape[1]
    hi, lo = hi_lo(q.astype(f32) * (LOG2E * head_dim ** (-0.5)), 2)
    first = jnp.broadcast_to(jnp.where(row == 0, 1.0, 0.0), (1, width))
    fill = jnp.zeros((2 * head_dim - 5, width), f32)
    return jnp.concatenate([hi, lo] + lse_parts + [first, 1.0 - first, fill], axis=0).astype(bf16)


def triangle(heads):
    key = lax.broadcasted_iota(jnp.int32, (CHUNK, heads * CHUNK), 0)
    query = lax.broadcasted_iota(jnp.int32, (CHUNK, heads * CHUNK), 1) % CHUNK
    return key <= query


def causal(s, heads):
    return jnp.concatenate([s[:PAD], jnp.where(triangle(heads), s[PAD:], BIG)], axis=0)


def attend_kernel(
    plan, heads, head_dim, len_ref, q_ref, win_ref, o_ref, rest_ref, lse_ref, k_ref, v_ref, kt_ref, vt_ref, acc, top, norm
):
    i = pl.program_id(0)
    me = lax.axis_index("seq")
    place = plan.chunk(me, i)
    row = place // (ROW // CHUNK)
    end = MARGIN + (place + 1) * CHUNK
    blocks = place % (ROW // CHUNK) // (BLOCK // CHUNK) + 1

    @pl.when(i == 0)
    def _():
        first, second = len_ref[0, plan.first_row(me)], len_ref[0, plan.last_row(me)]
        filled = plan.place(plan.reaches(me), me) + plan.shard_len - MARGIN
        lane = lax.broadcasted_iota(jnp.int32, (BLOCK, 2 * head_dim), 1)
        vt_ref[head_dim:, :] = jnp.where(
            lax.broadcasted_iota(jnp.int32, (16, vt_ref.shape[1]), 0) == 0, 1.0, 0.0
        ).astype(bf16)
        norm[...] = jnp.zeros_like(norm)

        def fill(b, _):
            at = pl.ds(pl.multiple_of(b * BLOCK, BLOCK), BLOCK)
            pos = b * BLOCK - MARGIN + lax.broadcasted_iota(jnp.int32, (BLOCK, 2 * head_dim), 0)
            inside = (pos >= 0) & (pos < filled)
            both = jnp.where(inside, win_ref[at, :].astype(f32), 0.0)
            swapped = pltpu.roll(both, head_dim, 1)
            k_ref[at, : 2 * head_dim] = jnp.where(lane < head_dim, both, swapped).astype(bf16)
            one = (pos >= 0) & (pos < first)
            two = (pos >= ROW) & (pos < ROW + second)
            bias = jnp.where(lane == 3, jnp.where(one, 0.0, BIG), jnp.where(two, 0.0, BIG))
            marks = jnp.where(lane < 3, 1.0, jnp.where(lane < 5, bias, 0.0))
            k_ref[at, 2 * head_dim :] = marks.astype(bf16)
            v_ref[at, :] = jnp.where(
                lane >= head_dim, both, jnp.where(lane < 3, 1.0, 0.0)
            ).astype(bf16)
            turned = both.T
            kt_ref[:, at] = turned[:head_dim].astype(bf16)
            vt_ref[:head_dim, at] = turned[head_dim:].astype(bf16)
            norm[...] = jnp.maximum(
                norm[...],
                jnp.max(jnp.sum(jnp.square(turned[:head_dim]), axis=0, keepdims=True), axis=1, keepdims=True),
            )
            return 0

        lax.fori_loop(0, k_ref.shape[0] // BLOCK, fill, 0)

    zero = jnp.zeros((1, heads * CHUNK), f32)
    q = wide(q_ref[...], heads, head_dim)
    q_aug = scaled_queries(q, head_dim, [zero, zero, zero], row)
    q_norm = jnp.max(jnp.sum(jnp.square(q.astype(f32)), axis=0, keepdims=True), axis=1, keepdims=True)
    limit = (SAFE / LOG2E) ** 2 * head_dim
    safe = jnp.max(jnp.where(q_norm * norm[...] < limit, 1, 0)) > 0

    def scores(j):
        off = pl.multiple_of(end - (j + 1) * BLOCK, CHUNK)
        return contract(k_ref[pl.ds(off, BLOCK), :], q_aug, 1, 0)

    def values(j):
        off = pl.multiple_of(end - (j + 1) * BLOCK, CHUNK)
        return vt_ref[:, pl.ds(off, BLOCK)]

    @pl.when(safe)
    def _():
        p = jnp.exp2(causal(scores(0), heads)).astype(bf16)
        acc[...] = contract(values(0), p, 1, 0)

        def twice(k, _):
            one, two = scores(2 * k + 1), scores(2 * k + 2)
            mixed = contract(values(2 * k + 1), jnp.exp2(one).astype(bf16), 1, 0)
            acc[...] += mixed + contract(values(2 * k + 2), jnp.exp2(two).astype(bf16), 1, 0)
            return 0

        lax.fori_loop(0, (blocks - 1) // 2, twice, 0)

        @pl.when(blocks % 2 == 0)
        def _():
            acc[...] += contract(values(blocks - 1), jnp.exp2(scores(blocks - 1)).astype(bf16), 1, 0)

        top[...] = jnp.zeros_like(top)

    @pl.when(jnp.logical_not(safe))
    def _():
        s = causal(scores(0), heads)
        m = jnp.max(s, axis=0, keepdims=True)
        top[...] = m
        acc[...] = contract(values(0), jnp.exp2(s - m).astype(bf16), 1, 0)

        def step(j, _):
            s = scores(j)
            old = top[...]
            m = jnp.maximum(old, jnp.max(s, axis=0, keepdims=True))
            top[...] = m
            p = jnp.exp2(s - m).astype(bf16)
            acc[...] = acc[...] * jnp.exp2(old - m) + contract(values(j), p, 1, 0)
            return 0

        lax.fori_loop(1, blocks, step, 0)

    total = acc[head_dim : head_dim + 1, :]
    attended = tall(acc[:head_dim, :] / total, heads)
    o_ref[...] = attended.astype(bf16)
    rest_ref[...] = (attended - attended.astype(bf16).astype(f32)).astype(bf16)
    lse_ref[0] = top[...] + jnp.log2(total)


def feed_phase(
    att_ref, wo_hbm, tok_ref, cot_hbm, vecs, upb_ref, up_hbm, down_hbm,
    out_hbm, res_ref, gatt_ref, mat,
    up_buf, down_buf, normal, out_acc, gn_acc, wo_ref, cot_ref, out_ref, fetch, talk,
):
    tile = mat.shape[1] // 2
    tiles = up_hbm.shape[1] // tile
    width = up_hbm.shape[0]
    out_bias, gain, shift, down_bias = (line(ref) for ref in vecs)

    def fetches(t, slot):
        at = pl.ds(pl.multiple_of(t * tile, tile), tile)
        return (
            pltpu.make_async_copy(up_hbm.at[:, at], up_buf.at[slot], fetch.at[0, slot]),
            pltpu.make_async_copy(down_hbm.at[at], down_buf.at[slot], fetch.at[1, slot]),
        )

    wo_copy = pltpu.make_async_copy(wo_hbm, wo_ref, fetch.at[2, 0])
    cot_copy = pltpu.make_async_copy(cot_hbm, cot_ref, fetch.at[2, 1])
    wo_copy.start()
    for copy in fetches(0, 0):
        copy.start()
    cot_copy.start()
    wo_copy.wait()

    residual = tok_ref[...].astype(f32) + contract(att_ref[...], wo_ref[...], 0, 0) + out_bias
    res_ref[...] = residual
    normal[...] = normed(residual, gain, shift).astype(bf16)
    out_acc[...] = residual + down_bias
    gn_acc[...] = jnp.zeros_like(gn_acc)
    sums = mat.shape[0] - 1
    cot_copy.wait()

    def step(t, _):
        slot = t % 2
        for copy in fetches(t, slot):
            copy.wait()

        @pl.when(t + 1 < tiles)
        def _():
            for copy in fetches(t + 1, 1 - slot):
                copy.start()

        u = contract(normal[...], up_buf[slot], 1, 0) + upb_ref[t]
        square = u * u
        th = jnp.tanh(GELU * (u + 0.044715 * (u * square)))
        half = 0.5 * (1.0 + th)
        slope = half + (0.5 * GELU) * u * (1.0 - th * th) * (1.0 + 3 * 0.044715 * square)
        activated = (u * half).astype(bf16)
        out_acc[...] += contract(activated, down_buf[slot], 1, 0)
        mat[t, tile:, :] = contract(activated, cot_ref[...], 0, 0).astype(bf16)
        talk(2 * t + 1)
        grad = (contract(cot_ref[...], down_buf[slot], 1, 1) * slope).astype(bf16)
        gn_acc[...] += contract(grad, up_buf[slot], 1, 1)
        mat[t, :tile, :] = contract(grad, normal[...], 0, 0).astype(bf16)
        upb_ref[t] = jnp.sum(grad.astype(f32), axis=0, keepdims=True)
        talk(2 * t + 2)
        return 0

    lax.fori_loop(0, tiles, step, 0)
    out_ref[...] = out_acc[...].astype(bf16)
    out_copy = pltpu.make_async_copy(out_ref, out_hbm, fetch.at[2, 0])
    out_copy.start()

    residual = res_ref[...]
    center = residual - jnp.mean(residual, axis=-1, keepdims=True)
    scale = lax.rsqrt(jnp.mean(center * center, axis=-1, keepdims=True) + epsilon)
    xhat = center * scale
    gn = gn_acc[...]
    q = gn * gain
    grad = scale * (
        q - jnp.mean(q, axis=-1, keepdims=True) - xhat * jnp.mean(q * xhat, axis=-1, keepdims=True)
    )
    cot = cot_ref[...].astype(f32)
    grad = cot + grad
    res_ref[...] = grad
    proj = grad.astype(bf16)
    talk(2 * tiles + 1)
    mat[sums, :width, :] = contract(att_ref[...], proj, 1, 0).astype(bf16)
    rows = [cot, proj.astype(f32), gn * xhat, gn]
    rows = [jnp.sum(row, axis=0, keepdims=True) for row in rows]
    rows.append(jnp.zeros((16 - len(rows), width), f32))
    mat[sums, width : width + 16, :] = jnp.concatenate(rows, axis=0).astype(bf16)
    rows = [upb_ref[t] for t in range(tiles)] + [jnp.zeros((1, tile), f32)] * (16 - tiles)
    rows = jnp.concatenate([jnp.concatenate(rows, axis=0), jnp.zeros((16, width - tile), f32)], axis=1)
    mat[sums, width + 16 : width + 32, :] = rows.astype(bf16)
    rest = mat.shape[1] - width - 32
    mat[sums, width + 32 :, :] = jnp.zeros((rest, width), bf16)
    gatt_ref[...] = contract(wo_ref[...], proj, 1, 1).astype(bf16)
    out_copy.wait()


def back_phase(
    plan, heads, head_dim, me, talk, steps,
    q_hbm, taken_hbm, k_hbm, v_hbm, kt_hbm, lse_ref, o_ref, rest_hbm, gatt_ref, dq_ref,
    low, inbox, land_q, land_g, land_s, give_s, kv_send, kv_recv, help_send, help_recv,
    k_ref, v_ref, kt_ref, q_ref, q_aug, g_aug, acc, total, rest_ref, fetch, prepared,
):
    shard_len = plan.shard_len
    copies = [
        pltpu.make_async_copy(src, dst, fetch.at[k])
        for k, (src, dst) in enumerate(
            [(q_hbm, q_ref), (rest_hbm, rest_ref), (k_hbm, k_ref), (v_hbm, v_ref), (kt_hbm, kt_ref), (taken_hbm, land_q)]
        )
    ]
    for copy in copies:
        copy.start()
    total[...] = jnp.zeros_like(total)
    acc[...] = jnp.zeros_like(acc)
    for copy in copies[:2]:
        copy.wait()

    def prepare(i, q, g, lse, delta, place):
        q_aug[i] = scaled_queries(wide(q, heads, head_dim), head_dim, hi_lo(-lse, 3), place // plan.per_row)
        fill = jnp.zeros((head_dim - 3, heads * CHUNK), f32)
        marks = jnp.concatenate(hi_lo(-delta, 3) + [fill], axis=0).astype(bf16)
        g_aug[i] = jnp.concatenate([marks, wide(g, heads, head_dim)], axis=0)

    def sends(i):
        found, helper, slot, order = plan.given(me, i)
        return found > 0, [
            remote(gatt_ref.at[:, pl.ds(i * CHUNK, CHUNK)], land_g.at[slot], help_send.at[1, order], help_recv.at[1, slot], helper),
            remote(give_s.at[order], land_s.at[slot], help_send.at[2, order], help_recv.at[2, slot], helper),
        ]

    givable = sorted({entry[1] for entry in plan.help})
    for i in range(plan.per_dev):
        if i in (2, 4):
            talk(steps + i // 2 - 1)
        at = pl.ds(i * CHUNK, CHUNK)
        g = gatt_ref[:, at]
        o = o_ref[:, at].astype(f32) + rest_ref[:, at].astype(f32)
        delta = jnp.sum(wide(g.astype(f32) * o, heads, head_dim), axis=0, keepdims=True)
        prepare(i, q_ref[:, at], g, lse_ref[i], delta, plan.chunk(me, i))
        if i in givable:
            there, copies_out = sends(i)

            @pl.when(there)
            def _():
                order = plan.given(me, i)[3]
                give_s[order, :1, :] = lse_ref[i]
                give_s[order, 1:2, :] = delta
                for copy in copies_out:
                    copy.start()

    for copy in copies[2:]:
        copy.wait()

    def piece(k, off, left):
        at = pl.ds(pl.multiple_of(plan.place(me + off, me) + left, CHUNK), shard_len - left)
        box = plan.box(me + off, -off)
        land = inbox.at[box, :, pl.ds(left, shard_len - left)]
        return remote(low.at[:, at], land, kv_send.at[k], kv_recv.at[box], me + off)

    def block(i, at, place, diagonal):
        s = contract(k_ref[at, :], q_aug[i], 1, 0)
        if diagonal:
            key = lax.broadcasted_iota(jnp.int32, (BLOCK, heads * CHUNK), 0)
            query = lax.broadcasted_iota(jnp.int32, (BLOCK, heads * CHUNK), 1) % CHUNK
            s = jnp.where(key - query <= place % (BLOCK // CHUNK) * CHUNK, s, BIG)
        dp = contract(v_ref[at, :], g_aug[i], 1, 0)
        p = jnp.exp2(s)
        ds = (p * dp).astype(bf16)
        p = p.astype(bf16)
        acc[i] += contract(kt_ref[:, at], ds, 1, 0)
        dk = contract(q_aug[i, : 2 * head_dim, :], ds, 1, 1)
        total[:head_dim, at] += dk[:head_dim] + dk[head_dim:]
        total[head_dim:, at] += contract(g_aug[i, head_dim:, :], p, 1, 1)

    def walk(count, locate, turn, n):
        def key_step(b, n):
            at = pl.ds(pl.multiple_of(MARGIN + b * BLOCK, BLOCK), BLOCK)

            def chunk_step(i, n):
                there, place = locate(i)
                last = place // (BLOCK // CHUNK)
                active = there & (b <= last) & (b // (ROW // BLOCK) == place // plan.per_row)

                @pl.when(active)
                def _():
                    talk(n)

                @pl.when(active & (b < last))
                def _():
                    block(i, at, place, False)

                @pl.when(active & (b == last))
                def _():
                    block(i, at, place, True)

                return n + jnp.where(active, 1, 0)

            n = lax.fori_loop(0, count, chunk_step, n)
            for k, off in enumerate(plan.offsets):
                end = plan.place(me + off, me) + shard_len - MARGIN

                for there, left in plan.pairs(me + off, me):

                    @pl.when(there & (b == (end + BLOCK - 1) // BLOCK - 1) & (plan.helps(me) == turn))
                    def _():
                        at = pl.ds(pl.multiple_of(plan.place(me + off, me), CHUNK), shard_len)
                        low[:head_dim, at] = (total[:head_dim, at] * (1.0 / LOG2E)).astype(bf16)
                        low[head_dim:, at] = total[head_dim:, at].astype(bf16)
                        piece(k, off, left).start()

            return n

        return lax.fori_loop(0, plan.span // BLOCK, key_step, n)

    def own(i):
        return plan.given(me, i)[0] == 0, plan.chunk(me, i)

    n = walk(plan.per_dev, own, 0, steps + 2)
    for i in range(plan.per_dev):
        dq_ref[:, i * CHUNK : (i + 1) * CHUNK] = tall(acc[i] * head_dim ** (-0.5), heads).astype(bf16)

    def taken(k):
        found, home, i, _ = plan.taken(me, k)
        return found > 0, plan.chunk(home, i, me)

    for k in range(plan.slots):
        there, place = taken(k)
        home = plan.taken(me, k)[1]

        @pl.when(there)
        def _():
            for part, land in ((1, land_g), (2, land_s)):
                remote(land.at[k], land.at[k], help_send.at[part, 0], help_recv.at[part, k], home).wait_recv()
            prepare(k, land_q[k], land_g[k], land_s[k, :1, :], land_s[k, 1:2, :], place)
            acc[k] = jnp.zeros_like(acc[k])

    for i in givable:
        there, copies_out = sends(i)

        @pl.when(there)
        def _():
            for copy in copies_out:
                copy.wait_send()

    prepared()
    n = walk(plan.slots, taken, 1, n)
    for k in range(plan.slots):
        there, _ = taken(k)
        _, home, _, order = plan.taken(me, k)

        @pl.when(there)
        def _():
            land_q[k] = tall(acc[k] * head_dim ** (-0.5), heads).astype(bf16)
            remote(land_q.at[k], land_g.at[order], help_send.at[3, k], help_recv.at[3, order], home).start()

    mine = pl.ds(pl.multiple_of(plan.place(me, me), CHUNK), shard_len)
    acc_kv = total[:, mine]
    total[:, :shard_len] = jnp.concatenate(
        [acc_kv[:head_dim] * (1.0 / LOG2E), acc_kv[head_dim:]], axis=0
    )
    return n


def layer_kernel(
    plan, heads, head_dim,
    att_ref, tok_ref, ob_ref, gain_ref, shift_ref, db_ref, upb_ref, lse_ref, gain_one_ref,
    wo_hbm, cot_hbm, up_hbm, down_hbm, rest_hbm, q_hbm, taken_hbm, k_hbm, v_hbm, kt_hbm, normal_hbm, wq_hbm, wkv_hbm,
    sum_ref, out_hbm, end_mat, res_ref,
    gatt_ref, low, inbox, land_q, land_g, land_s, give_s, mat, upb_mat,
    feed_fetch, back_fetch, kv_send, kv_recv, help_send, help_recv, load, *summing,
):
    me = lax.axis_index("seq")
    shard_len, width = tok_ref.shape
    pieces, height, _ = mat.shape
    half = len(summing) // 2
    summed = Summing(plan, ORDERS, TABLE, height, mat, *summing[:2], summing[2:half])
    ending = Summing(
        plan, LAST_ORDERS, LAST_TABLE, end_mat.shape[1], end_mat, *summing[half : half + 2], summing[half + 2 :]
    )
    greet(plan, me, summed.partners())
    givable = sorted({entry[1] for entry in plan.help})
    for t in range(upb_mat.shape[0]):
        wide_t = upb_mat.shape[2]
        upb_mat[t] = upb_ref[pl.ds(t * wide_t, wide_t)].reshape(1, wide_t)

    def store(p):
        pltpu.make_async_copy(mat.at[p], sum_ref.at[p], load.at[p]).start()

    def talk(n):
        summed.step(n, store)

    def first(up_buf, down_buf, normal, out_acc, gn_acc, wo_ref, cot_ref, out_ref):
        feed_phase(
            att_ref, wo_hbm, tok_ref, cot_hbm, (ob_ref, gain_ref, shift_ref, db_ref), upb_mat, up_hbm, down_hbm,
            out_hbm, res_ref, gatt_ref, mat,
            up_buf, down_buf, normal, out_acc, gn_acc, wo_ref, cot_ref, out_ref, feed_fetch, talk,
        )

    tile = height // 2
    pl.run_scoped(
        first,
        pltpu.VMEM((2, width, tile), bf16),
        pltpu.VMEM((2, tile, width), bf16),
        pltpu.VMEM((shard_len, width), bf16),
        pltpu.VMEM((shard_len, width), f32),
        pltpu.VMEM((shard_len, width), f32),
        pltpu.VMEM((width, width), bf16),
        pltpu.VMEM((shard_len, width), bf16),
        pltpu.VMEM((shard_len, width), bf16),
    )
    talk(2 * pieces)
    window, columns = plan.window, heads * CHUNK
    chunks = plan.per_dev

    def second(k_ref, v_ref, kt_ref, q_ref, q_aug, g_aug, acc, total, spare, wkv):
        copies = [
            pltpu.make_async_copy(src, dst, back_fetch.at[6 + k])
            for k, (src, dst) in enumerate([(normal_hbm, gatt_ref), (wq_hbm, spare), (wkv_hbm, wkv)])
        ]

        def later():
            for copy in copies:
                copy.start()

        done = back_phase(
            plan, heads, head_dim, me, talk, 2 * pieces + 1,
            q_hbm, taken_hbm, k_hbm, v_hbm, kt_hbm, lse_ref, att_ref, rest_hbm, gatt_ref, q_ref,
            low, inbox, land_q, land_g, land_s, give_s, kv_send, kv_recv, help_send, help_recv,
            k_ref, v_ref, kt_ref, q_ref, q_aug, g_aug, acc, total, spare, back_fetch, later,
        )

        def drain(n, _):
            talk(n)
            return 0

        busy = 2 * pieces + 3 + plan.blocks
        lax.fori_loop(done, busy, drain, 0)
        for i in givable:
            found, helper, _, order = plan.given(me, i)

            @pl.when(found > 0)
            def _():
                land = land_g.at[order]
                remote(land, land, help_send.at[3, 0], help_recv.at[3, order], helper).wait_recv()
                q_ref[:, i * CHUNK : (i + 1) * CHUNK] = land_g[order]

        for copy in copies:
            copy.wait()
        normal, wq = gatt_ref, spare
        tall_part = end_mat.shape[1]
        grad = contract(normal[...], q_ref[...], 0, 1).astype(bf16)
        wide_part = width - tall_part
        end_mat[0] = grad[:tall_part, :tall_part]
        end_mat[1, :wide_part, :] = grad[tall_part:, :tall_part]
        end_mat[1, wide_part:, :wide_part] = grad[:wide_part, tall_part:]
        end_mat[1, wide_part:, wide_part:] = grad[wide_part:tall_part, tall_part:]
        end_mat[2, :wide_part, :wide_part] = grad[tall_part:, tall_part:]
        talk(busy)
        ending.step(busy)
        grad_qb = jnp.sum(q_ref[...].astype(f32).T, axis=0, keepdims=True)
        gn = contract(q_ref[...], wq[...], 0, 1)

        for k, off in enumerate(plan.offsets):

            for there, left in plan.pairs(me, me + off):

                @pl.when(there)
                def _():
                    box = plan.box(me, off)
                    part = pl.ds(left, shard_len - left)
                    land = inbox.at[box, :, part]
                    remote(land, land, kv_send.at[0], kv_recv.at[box], me + off).wait_recv()
                    total[:, part] += inbox[box, :, part].astype(f32)

            for there, left in plan.pairs(me + off, me):

                @pl.when(there)
                def _():
                    some = inbox.at[0, :, pl.ds(left, shard_len - left)]
                    remote(some, some, kv_send.at[k], kv_recv.at[0], me + off).wait_send()

        for k in range(plan.slots):
            found, home, _, order = plan.taken(me, k)

            @pl.when(found > 0)
            def _():
                remote(
                    land_q.at[k], land_g.at[order], help_send.at[3, k], help_recv.at[3, order], home
                ).wait_send()

        grad_kv = total[:, :shard_len].astype(bf16)
        gn = gn + contract(grad_kv, wkv[...], 0, 1)
        grad = contract(grad_kv, normal[...], 1, 0).astype(bf16)
        pair = 2 * head_dim
        end_mat[2, :pair, wide_part:] = grad[:, :wide_part]
        end_mat[2, pair : 2 * pair, wide_part:] = grad[:, wide_part : 2 * wide_part]
        end_mat[2, wide_part : wide_part + pair, :wide_part] = grad[:, 2 * wide_part :]
        grad_vb = jnp.sum(grad_kv.astype(f32).T, axis=0, keepdims=True)

        tok = tok_ref[...].astype(f32)
        center = tok - jnp.mean(tok, axis=-1, keepdims=True)
        scale = lax.rsqrt(jnp.mean(center * center, axis=-1, keepdims=True) + epsilon)
        xhat = center * scale
        grads = [gn * xhat, gn]
        rows = [jnp.sum(grad, axis=0, keepdims=True) for grad in grads] + [grad_qb]
        rows.append(jnp.concatenate([grad_vb, jnp.zeros((1, width - 2 * head_dim), f32)], axis=1))
        rows.append(jnp.zeros((16 - len(rows), width), f32))
        rows = jnp.concatenate(rows, axis=0).astype(bf16)
        for k in range(3):
            at = wide_part + 16 * k
            end_mat[2, at : at + 16, wide_part:] = rows[:, k * wide_part : (k + 1) * wide_part]
        end_mat[2, wide_part + 48 : wide_part + pair, wide_part:] = jnp.zeros((pair - 48, wide_part), bf16)
        end_mat[2, wide_part + pair :, :] = jnp.zeros((tall_part - wide_part - pair, tall_part), bf16)
        talk(busy + 1)
        ending.step(busy + 1)
        q = gn * line(gain_one_ref)
        res_ref[...] += scale * (
            q - jnp.mean(q, axis=-1, keepdims=True) - xhat * jnp.mean(q * xhat, axis=-1, keepdims=True)
        )


        def finish(n, _):
            talk(n)
            ending.step(n)
            return 0

        lax.fori_loop(busy + 2, max(summed.end, ending.end), finish, 0)

    pl.run_scoped(
        second,
        pltpu.VMEM((window, 4 * head_dim), bf16),
        pltpu.VMEM((window, 2 * head_dim), bf16),
        pltpu.VMEM((head_dim, window), bf16),
        pltpu.VMEM((width, shard_len), bf16),
        pltpu.VMEM((chunks, 4 * head_dim, columns), bf16),
        pltpu.VMEM((chunks, 2 * head_dim, columns), bf16),
        pltpu.VMEM((chunks, head_dim, columns), f32),
        pltpu.VMEM((2 * head_dim, window), f32),
        pltpu.VMEM(wq_hbm.shape, bf16),
        pltpu.VMEM(wkv_hbm.shape, bf16),
    )
    for p in range(pieces):
        pltpu.make_async_copy(mat.at[p], sum_ref.at[p], load.at[p]).wait()


def final_kernel(
    head_dim,
    sum_ref, rest_ref, last_ref, tok_ref, grad_ref,
    tok_out, grad_out, up_ref, down_ref, out_ref, q_ref, kv_ref, upb_ref,
    db_ref, ob_ref, gain_two_ref, shift_two_ref, gain_one_ref, shift_one_ref, qb_ref, vb_ref,
):
    tok_out[...] = tok_ref[...]
    grad_out[...] = grad_ref[...]
    i = pl.program_id(0)
    tile, width = down_ref.shape
    up_ref[...] = sum_ref[0, :tile, :].astype(f32).T
    down_ref[...] = sum_ref[0, tile:, :].astype(f32)

    @pl.when(i == 0)
    def _():
        out_ref[...] = rest_ref[0, :width, :].astype(f32)
        side, pair = width - tile, 2 * head_dim
        last = [last_ref[k].astype(f32) for k in range(3)]
        q_ref[:tile, :tile] = last[0]
        q_ref[tile:, :tile] = last[1][:side]
        q_ref[:side, tile:] = last[1][side:, :side]
        q_ref[side:tile, tile:] = last[1][side:, side:]
        q_ref[tile:, tile:] = last[2][:side, :side]
        kv = [last[2][:pair, side:], last[2][pair : 2 * pair, side:], last[2][side : side + pair, :side]]
        kv_ref[...] = jnp.concatenate(kv, axis=1).T
        rows = rest_ref[0, width : width + 32, :].astype(f32)
        for k, ref in enumerate([db_ref, ob_ref, gain_two_ref, shift_two_ref]):
            ref[...] = rows[k : k + 1].reshape(width)
        for t in range(upb_ref.shape[0] // tile):
            upb_ref[pl.ds(t * tile, tile)] = rows[16 + t : 17 + t, :tile].reshape(tile)
        rows = jnp.concatenate([last[2][side + 16 * k : side + 16 * k + 16, side:] for k in range(3)], axis=1)
        for k, ref in enumerate([gain_one_ref, shift_one_ref, qb_ref]):
            ref[...] = rows[k : k + 1].reshape(width)
        vb_ref[...] = rows[3:4, head_dim : 2 * head_dim].reshape(head_dim)


def whole(shape):
    return pl.BlockSpec(shape, lambda i: (0,) * len(shape))


def column(height):
    return pl.BlockSpec((height, CHUNK), lambda i: (0, i))


def lead(shape):
    return pl.BlockSpec((1,) + shape, lambda i: (i,) + (0,) * len(shape))


def per_device(
    plan,
    tokens,
    lengths,
    cotangent,
    norm1_gain,
    norm1_shift,
    query_weight,
    query_bias,
    keyval_weight,
    value_bias,
    out_weight,
    out_bias,
    norm2_gain,
    norm2_shift,
    up_weight,
    up_bias,
    down_weight,
    down_bias,
):
    shard_len, width = tokens.shape[1:]
    head_dim = keyval_weight.shape[1] // 2
    heads = width // head_dim
    columns = heads * CHUNK
    chunks = plan.per_dev
    window = plan.window
    limit = dict(vmem_limit_bytes=63 * 2**20)
    vmem = pl.BlockSpec(memory_space=pltpu.VMEM)
    anywhere = pl.BlockSpec(memory_space=pl.ANY)
    dma = pltpu.SemaphoreType.DMA

    normal_one, queries, keyvals, taken = pl.pallas_call(
        partial(gather_kernel, plan),
        in_specs=[vmem] * 7,
        out_specs=[vmem] * 4,
        out_shape=[
            jax.ShapeDtypeStruct((shard_len, width), bf16),
            jax.ShapeDtypeStruct((width, shard_len), bf16),
            jax.ShapeDtypeStruct((window, 2 * head_dim), bf16),
            jax.ShapeDtypeStruct((plan.slots, width, CHUNK), bf16),
        ],
        scratch_shapes=[pltpu.VMEM((shard_len, 2 * head_dim), bf16)]
        + [dma((len(plan.offsets),))] * 2
        + [dma((plan.slots,))] * 2,
        compiler_params=pltpu.CompilerParams(collective_id=0, has_side_effects=True, **limit),
        name="gather",
    )(
        tokens[0],
        norm1_gain,
        norm1_shift,
        keyval_weight,
        value_bias,
        query_weight,
        query_bias,
    )

    attended, attended_low, lse, k_aug, v_aug, k_turned = pl.pallas_call(
        partial(attend_kernel, plan, heads, head_dim),
        grid_spec=pltpu.PrefetchScalarGridSpec(
            num_scalar_prefetch=0,
            grid=(chunks,),
            in_specs=[
                pl.BlockSpec(memory_space=pltpu.SMEM),
                column(width),
                whole((window, 2 * head_dim)),
            ],
            out_specs=[
                column(width),
                column(width),
                lead((1, columns)),
                whole((window, 4 * head_dim)),
                whole((window, 2 * head_dim)),
                whole((head_dim, window)),
            ],
            scratch_shapes=[
                pltpu.VMEM((head_dim + 16, window), bf16),
                pltpu.VMEM((head_dim + 16, columns), f32),
                pltpu.VMEM((1, columns), f32),
                pltpu.VMEM((1, 1), f32),
            ],
        ),
        out_shape=[
            jax.ShapeDtypeStruct((width, shard_len), bf16),
            jax.ShapeDtypeStruct((width, shard_len), bf16),
            jax.ShapeDtypeStruct((chunks, 1, columns), f32),
            jax.ShapeDtypeStruct((window, 4 * head_dim), bf16),
            jax.ShapeDtypeStruct((window, 2 * head_dim), bf16),
            jax.ShapeDtypeStruct((head_dim, window), bf16),
        ],
        compiler_params=pltpu.CompilerParams(**limit),
        name="attend",
    )(lengths, queries, keyvals)

    inputs = tokens[0].astype(f32)
    hidden = up_weight.shape[1]
    tile = PIECE // 2
    tiles = hidden // tile
    pieces = tiles + 1
    assert pieces == len(ORDERS) and 2 * (width - tile) == tile and 4 * head_dim == width - tile
    sums, outputs, last, grad_inputs = pl.pallas_call(
        partial(layer_kernel, plan, heads, head_dim),
        in_specs=[vmem] * 9 + [anywhere] * 13,
        out_specs=[anywhere] * 2 + [vmem] * 2,
        out_shape=[
            jax.ShapeDtypeStruct((pieces, PIECE, width), bf16),
            jax.ShapeDtypeStruct((shard_len, width), bf16),
            jax.ShapeDtypeStruct((len(LAST_ORDERS), tile, tile), bf16),
            jax.ShapeDtypeStruct((shard_len, width), f32),
        ],
        scratch_shapes=[
            pltpu.VMEM((width, shard_len), bf16),
            pltpu.VMEM((2 * head_dim, window), bf16),
            pltpu.VMEM((plan.inboxes, 2 * head_dim, shard_len), bf16),
            pltpu.VMEM((plan.slots, width, CHUNK), bf16),
            pltpu.VMEM((plan.slots, width, CHUNK), bf16),
            pltpu.VMEM((plan.slots, 8, columns), f32),
            pltpu.VMEM((plan.slots, 8, columns), f32),
            pltpu.VMEM((pieces, PIECE, width), bf16),
            pltpu.VMEM((tiles, 1, tile), f32),
            dma((3, 2)),
            dma((9,)),
            dma((len(plan.offsets),)),
            dma((plan.inboxes,)),
            dma((4, plan.slots)),
            dma((4, plan.slots)),
            dma((pieces,)),
        ]
        + Summing.scratch(plan, pieces, PIECE, width)
        + Summing.scratch(plan, len(LAST_ORDERS), tile, tile),
        compiler_params=pltpu.CompilerParams(collective_id=1, has_side_effects=True, **limit),
        name="layer",
    )(
        attended,
        tokens[0],
        out_bias,
        norm2_gain,
        norm2_shift,
        down_bias,
        up_bias,
        lse,
        norm1_gain,
        out_weight,
        cotangent[0],
        up_weight,
        down_weight,
        attended_low,
        queries,
        taken,
        k_aug,
        v_aug,
        k_turned,
        normal_one,
        query_weight,
        keyval_weight,
    )

    vector = jax.ShapeDtypeStruct((width,), f32)
    finals = pl.pallas_call(
        partial(final_kernel, head_dim),
        grid=(tiles,),
        in_specs=[
            lead((PIECE, width)),
            pl.BlockSpec((1, PIECE, width), lambda i: (tiles, 0, 0)),
            whole((len(LAST_ORDERS), tile, tile)),
            pl.BlockSpec((shard_len // tiles, width), lambda i: (i, 0)),
            pl.BlockSpec((shard_len // tiles, width), lambda i: (i, 0)),
        ],
        out_specs=[
            pl.BlockSpec((shard_len // tiles, width), lambda i: (i, 0)),
            pl.BlockSpec((shard_len // tiles, width), lambda i: (i, 0)),
            pl.BlockSpec((width, tile), lambda i: (0, i)),
            pl.BlockSpec((tile, width), lambda i: (i, 0)),
            whole((width, width)),
            whole((width, width)),
            whole((width, 2 * head_dim)),
            whole((hidden,)),
        ]
        + [whole((width,))] * 7
        + [whole((head_dim,))],
        out_shape=[
            jax.ShapeDtypeStruct((shard_len, width), bf16),
            jax.ShapeDtypeStruct((shard_len, width), f32),
            jax.ShapeDtypeStruct((width, hidden), f32),
            jax.ShapeDtypeStruct((hidden, width), f32),
            jax.ShapeDtypeStruct((width, width), f32),
            jax.ShapeDtypeStruct((width, width), f32),
            jax.ShapeDtypeStruct((width, 2 * head_dim), f32),
            jax.ShapeDtypeStruct((hidden,), f32),
        ]
        + [vector] * 7
        + [jax.ShapeDtypeStruct((head_dim,), f32)],
        compiler_params=pltpu.CompilerParams(**limit),
        name="finals",
    )(sums, sums, last, outputs, grad_inputs)
    outputs, grad_inputs, up_w, down_w, out_w, qw, kvw, up_b = finals[:8]
    down_b, out_b, gain_two, shift_two, gain_one, shift_one, qb, vb = finals[8:]
    return (
        outputs[None],
        grad_inputs[None],
        gain_one,
        shift_one,
        qw,
        qb,
        kvw,
        vb,
        out_w,
        out_b,
        gain_two,
        shift_two,
        up_w,
        up_b,
        down_w,
        down_b,
    )


def solution(mesh):
    split = P("dp", "seq", None)
    devices = mesh.shape["seq"]

    def run(*arrays):
        plan = Plan(devices, arrays[0].shape[1] // devices)
        return jax.shard_map(
            partial(per_device, plan),
            mesh=mesh,
            in_specs=(split, P("dp", None), split) + (P(),) * 14,
            out_specs=(split, split) + (P(),) * 14,
            check_vma=False,
        )(*arrays)

    return run
```

```python
from functools import partial

import jax
import jax.numpy as jnp
import numpy as np
from jax import lax
from jax.experimental import pallas as pl
from jax.experimental.pallas import tpu as pltpu
from jax.sharding import PartitionSpec as P

ROW = 4096
CHUNK = 128
BLOCK = 512
PAD = BLOCK - CHUNK
LOG2E = 1.4426950408889634
BIG = -1e30
MARGIN = BLOCK
PIECE = 1024
ORDERS = ((0, 1, 2), (1, 0, 2), (2, 1, 0), (2, 0, 1), (1, 0, 2), (0, 1, 2), (1, 0, 2))
TABLE = (
    (2, 4, 6, 8, 10, 12, 14),
    (3, 5, 7, 9, 11, 13, 15),
    (9, 11, 13, 15, 17, 19, 21),
    (14, 16, 18, 20, 22, 24, 26),
    (18, 20, 22, 24, 26, 28, 30),
    (22, 24, 26, 28, 30, 32, 34),
    (25, 27, 29, 31, 33, 35, 37),
    (29, 31, 33, 35, 37, 39, 41),
    (35, 39, 41, 43, 45, 47, 49),
    (41, 45, 47, 49, 51, 50, 55),
    (44, 48, 50, 52, 54, 56, 58),
)
LAST_ORDERS = ((0, 1, 2), (1, 0, 2), (2, 0, 1))
LAST_TABLE = (
    (49, 50, 51),
    (52, 53, 54),
    (55, 56, 57),
    (58, 59, 60),
    (61, 62, 63),
    (64, 65, 66),
    (67, 68, 69),
    (70, 71, 72),
    (73, 74, 75),
    (76, 77, 78),
    (79, 80, 81),
)
TINY_ORDERS = ((0, 1, 2),)
TINY_TABLE = ((53,), (55,), (58,), (61,), (64,), (67,), (70,), (73,), (76,), (78,), (81,))
SAFE = 60.0
epsilon = 1e-05
GELU = 0.7978845608028654
bf16 = jnp.bfloat16
f32 = jnp.float32


HELP = (
    (4, 4, 0, 0), (4, 5, 0, 1), (3, 5, 1, 0), (10, 3, 6, 0), (9, 4, 6, 1), (9, 5, 7, 0),
    (15, 4, 11, 0), (15, 5, 11, 1), (14, 5, 12, 0),
)
UNIT = 16


class Plan:
    def __init__(self, devices, shard_len):
        self.devices = devices
        self.shard_len = shard_len
        self.per_dev = shard_len // CHUNK
        self.per_row = ROW // CHUNK
        assert shard_len % CHUNK == 0 and shard_len <= ROW
        ends = [(d + 1) * shard_len - self.first_row(d) * ROW for d in range(devices)]
        self.span = -(-max(ends) // BLOCK) * BLOCK
        self.window = MARGIN + self.span
        self.help = HELP if devices % UNIT == 0 and shard_len * UNIT == 3 * ROW else ()
        self.slots = 2
        self.top = {}
        for home, _, helper, _ in self.help:
            self.top[helper] = max(home, self.top.get(helper, 0))
        helpers = sorted(self.top)
        self.kinds = {helper: k % 2 for k, helper in enumerate(helpers)}
        self.reach = max(
            d - e for d in range(devices) for e in range(d + 1) if self.first_row(d) <= self.last_row(e)
        )
        self.skips = sorted({self.skip(d, h) for d in range(devices) for h in range(d, min(d + self.reach + 1, devices))
                             if self.first_row(h) <= self.last_row(d)})
        self.blocks = max(self.load(d) for d in range(devices))
        self.offsets = [o for o in range(-self.reach, self.reach + 1) if o != 0]
        self.inboxes = self.reach + 2

    def load(self, device):
        def blocks(d, i):
            return self.chunk(d, i) % self.per_row // (BLOCK // CHUNK) + 1

        unit, place = device // UNIT * UNIT, device % UNIT
        moved = {(home, i) for home, i, _, _ in self.help}
        total = sum(blocks(device, i) for i in range(self.per_dev) if (place, i) not in moved)
        return total + sum(blocks(unit + home, i) for home, i, helper, _ in self.help if helper == place)

    def first_row(self, device):
        return device * self.shard_len // ROW

    def last_row(self, device):
        return ((device + 1) * self.shard_len - 1) // ROW

    def lookup(self, device, table, default):
        place = device % UNIT
        value = default
        for key, entry in table.items():
            value = jnp.where(place == key, entry, value)
        return value

    def reaches(self, device):
        extra = {helper: top - helper for helper, top in self.top.items()}
        return device + self.lookup(device, extra, 0)

    def helps(self, device):
        return self.lookup(device, {helper: 1 for helper in self.top}, 0)

    def feeds(self, source, holder):
        return (
            (source >= 0)
            & (holder >= 0)
            & (source < self.devices)
            & (holder < self.devices)
            & (self.first_row(holder) <= self.last_row(source))
            & (source <= self.reaches(holder))
        )

    def given(self, device, i):
        place = device % UNIT
        found, helper, slot, order = 0, 0, 0, 0
        counts = {}
        for home, chunk, to, k in self.help:
            here = jnp.where((place == home) & (i == chunk), 1, 0)
            found, slot = found + here, slot + here * k
            helper = helper + here * (to - home)
            order = order + here * counts.get(home, 0)
            counts[home] = counts.get(home, 0) + 1
        return found, device + helper, slot, order

    def taken(self, device, k):
        place = device % UNIT
        found, home, i, order = 0, 0, 0, 0
        counts = {}
        for owner, chunk, helper, slot in self.help:
            here = jnp.where((place == helper) & (k == slot), 1, 0)
            found, i = found + here, i + here * chunk
            home = home + here * (owner - helper)
            order = order + here * counts.get(owner, 0)
            counts[owner] = counts.get(owner, 0) + 1
        return found, device + home, i, order

    def box(self, owner, off):
        return off - 1 if off > 0 else self.reach + self.lookup(owner + off, self.kinds, 0)

    def skip(self, source, holder):
        gap = self.first_row(holder) * ROW - source * self.shard_len
        return max(gap, 0) if isinstance(gap, int) else jnp.where(gap > 0, gap, 0)

    def pairs(self, source, holder):
        return [(self.feeds(source, holder) & (self.skip(source, holder) == left), left) for left in self.skips]

    def place(self, source, holder):
        return MARGIN + source * self.shard_len - self.first_row(holder) * ROW

    def chunk(self, device, i, holder=None):
        return device * self.per_dev + i - self.first_row(device if holder is None else holder) * self.per_row


class Summing:
    def __init__(self, plan, orders, table, height, mat, inbox, extra, sems):
        self.pieces, self.height, self.orders = len(orders), height, orders
        self.mat, self.inbox, self.extra = mat, inbox, extra
        self.out_send, self.out_recv, self.back_send, self.back_recv, self.free = sems
        self.bits = plan.devices.bit_length() - 1
        self.halvings = 1 + min(self.bits, 4)
        self.swaps = self.bits + 1 - self.halvings
        self.stages = 2 * self.halvings + self.swaps
        if len(table) != self.stages + 1:
            table = [[start + 3 * s for start in table[0]] for s in range(self.stages + 1)]
        self.table = table
        self.end = max(max(row) for row in table) + 1
        self.seq, self.dp = lax.axis_index("seq"), lax.axis_index("dp")

    @staticmethod
    def scratch(plan, pieces, height, width):
        bits = plan.devices.bit_length() - 1
        halvings = 1 + min(bits, 4)
        swaps = bits + 1 - halvings
        last = height >> halvings
        dma = pltpu.SemaphoreType.DMA
        return [
            pltpu.VMEM((pieces, height - last, width), bf16),
            pltpu.VMEM((max(swaps, 1), pieces, last, width), bf16),
            dma((halvings + swaps, pieces)),
            dma((halvings + swaps, pieces)),
            dma((halvings, pieces)),
            dma((halvings, pieces)),
            pltpu.SemaphoreType.REGULAR((halvings, pieces)),
        ]

    def partners(self):
        bits = [(self.seq >> b) & 1 for b in range(self.bits)]
        return [(self.seq, 1 - self.dp)] + [
            (self.seq + (1 - 2 * bit) * (1 << b), self.dp) for b, bit in enumerate(bits)
        ]

    def spots(self, p, count):
        spots, starts, at = [], [0], 0
        for t in range(count):
            if t == 0:
                bit, device = self.dp, {"seq": self.seq, "dp": 1 - self.dp}
            else:
                if t < 4:
                    word = sum(order[t - 1] << (2 * k) for k, order in enumerate(self.orders))
                    axis = lax.shift_right_logical(np.int32(word), 2 * p) & 3
                else:
                    axis = t - 1
                bit = lax.shift_right_logical(self.seq, axis) & 1
                step = lax.shift_left(np.int32(1), axis) if t < 4 else 1 << axis
                device = {"seq": self.seq + (1 - 2 * bit) * step, "dp": self.dp}
            spots.append((bit, device))
            at = at + bit * (self.height >> (t + 1))
            starts.append(at)
        return spots, starts

    def rows(self, start, size):
        return pl.ds(pl.multiple_of(start, size), size)

    def remote(self, src, dst, sems, device):
        return pltpu.make_async_remote_copy(
            src_ref=src,
            dst_ref=dst,
            send_sem=sems[0],
            recv_sem=sems[1],
            device_id=device,
            device_id_type=pl.DeviceIdType.MESH,
        )

    def sems(self, stage, p):
        if stage < self.halvings + self.swaps:
            return self.out_send.at[stage, p], self.out_recv.at[stage, p]
        t = self.stages - 1 - stage
        return self.back_send.at[t, p], self.back_recv.at[t, p]

    def size(self, stage):
        h, w = self.halvings, self.swaps
        t = stage if stage < h else h - 1 if stage < h + w else self.stages - 1 - stage
        return self.height >> (t + 1)

    def event(self, stage, p):
        h, w, last = self.halvings, self.swaps, self.stages
        depth = min(stage + 1, h + w) if stage < h + w else last - stage
        spots, starts = self.spots(p, max(depth, 1))
        if stage > 0:
            before = stage - 1
            size = self.size(before)
            some = self.mat.at[p, pl.ds(0, size)]
            wait = self.remote(some, some, self.sems(before, p), spots[0][1])
            wait.wait()
            if before < h:
                at = self.rows(starts[before + 1], size)
                self.mat[p, at, :] = self.mat[p, at, :] + self.inbox[p, pl.ds(self.height - 2 * size, size), :]
                pl.semaphore_signal(
                    self.free.at[before, p],
                    inc=1,
                    device_id=spots[before][1],
                    device_id_type=pl.DeviceIdType.MESH,
                )
            elif before < h + w:
                at = self.rows(starts[h], size)
                self.mat[p, at, :] = self.mat[p, at, :] + self.extra[before - h, p]
        if stage < h:
            size = self.size(stage)
            bit, device = spots[stage]
            src = self.mat.at[p, self.rows(starts[stage] + (1 - bit) * size, size)]
            dst = self.inbox.at[p, pl.ds(self.height - 2 * size, size)]
            self.remote(src, dst, self.sems(stage, p), device).start()
        elif stage < h + w:
            src = self.mat.at[p, self.rows(starts[h], self.size(stage))]
            self.remote(src, self.extra.at[stage - h, p], self.sems(stage, p), spots[stage][1]).start()
        elif stage < last:
            t = last - 1 - stage
            pl.semaphore_wait(self.free.at[t, p], 1)
            src = self.mat.at[p, self.rows(starts[t + 1], self.size(stage))]
            self.remote(src, src, self.sems(stage, p), spots[t][1]).start()

    def step(self, n, last=None):
        for stage in range(self.stages, -1, -1):
            p = -1
            for k, step in enumerate(self.table[stage]):
                p = jnp.where(n == step, k, p)

            @pl.when(p >= 0)
            def _():
                self.event(stage, p)
                if stage == self.stages and last is not None:
                    last(p)


def line(ref):
    return ref[...].reshape(1, ref.shape[0])


def remote(src, dst, send, recv, device):
    return pltpu.make_async_remote_copy(
        src_ref=src,
        dst_ref=dst,
        send_sem=send,
        recv_sem=recv,
        device_id={"seq": device},
        device_id_type=pl.DeviceIdType.MESH,
    )


def rows(index, count):
    return pl.ds(pl.multiple_of(index * count, count), count)


def greet(plan, me, others=()):
    barrier = pltpu.get_barrier_semaphore()
    count = len(others)
    for seq, dp in others:
        pl.semaphore_signal(
            barrier, inc=1, device_id={"seq": seq, "dp": dp}, device_id_type=pl.DeviceIdType.MESH
        )
    for off in plan.offsets:
        there = plan.feeds(me, me + off) | plan.feeds(me + off, me)
        count = count + jnp.where(there, 1, 0)

        @pl.when(there)
        def _():
            pl.semaphore_signal(
                barrier, inc=1, device_id={"seq": me + off}, device_id_type=pl.DeviceIdType.MESH
            )

    pl.semaphore_wait(barrier, count)


def gather_kernel(
    plan,
    tok_ref, gain_ref, shift_ref, wkv_ref, kvb_ref, wq_ref, qb_ref, cot_hbm, down_hbm,
    normal_ref, q_ref, win_ref, taken_ref, act_hbm,
    kv_ref, cot_ref, down_ref, act_ref, kv_send, kv_recv, q_send, q_recv, fetch,
):
    me = lax.axis_index("seq")
    fetches = [
        pltpu.make_async_copy(cot_hbm, cot_ref, fetch.at[0]),
        pltpu.make_async_copy(down_hbm, down_ref, fetch.at[1]),
    ]
    for fetched in fetches:
        fetched.start()
    greet(plan, me)

    def copy(k, source, holder, left, device):
        size = plan.shard_len - left
        at = pl.multiple_of(plan.place(source, holder) + left, CHUNK)
        return remote(
            kv_ref.at[pl.ds(left, size)], win_ref.at[pl.ds(at, size)], kv_send.at[k], kv_recv.at[k], device
        )

    givable = sorted({entry[1] for entry in plan.help})

    def handed(i):
        found, helper, slot, order = plan.given(me, i)
        return found > 0, remote(
            q_ref.at[:, pl.ds(i * CHUNK, CHUNK)], taken_ref.at[slot], q_send.at[order], q_recv.at[slot], helper
        )

    normal = normed(tok_ref[...].astype(f32), line(gain_ref), line(shift_ref)).astype(bf16)
    normal_ref[...] = normal
    bias = line(kvb_ref)
    bias = jnp.concatenate([jnp.zeros_like(bias), bias], axis=1)
    kv_ref[...] = (contract(normal, wkv_ref[...], 1, 0) + bias).astype(bf16)
    for k, off in enumerate(plan.offsets):

        for there, left in plan.pairs(me, me + off):

            @pl.when(there)
            def _():
                copy(k, me, me + off, left, me + off).start()

    own = pl.multiple_of(plan.place(me, me), CHUNK)
    win_ref[pl.ds(own, plan.shard_len), :] = kv_ref[...]
    q_ref[...] = (contract(normal, wq_ref[...], 1, 0) + line(qb_ref)).T.astype(bf16)
    for i in givable:
        there, hand = handed(i)

        @pl.when(there)
        def _():
            hand.start()

    for fetched in fetches:
        fetched.wait()
    tile = act_ref.shape[2]
    tiles = act_hbm.shape[0]

    def put(t, slot):
        return pltpu.make_async_copy(act_ref.at[slot], act_hbm.at[t], fetch.at[slot])

    def back(t, _):
        slot = t % 2

        @pl.when(t >= 2)
        def _():
            put(t - 2, slot).wait()

        act_ref[slot] = contract(cot_ref[...], down_ref[rows(t, tile), :], 1, 1)
        put(t, slot).start()
        return 0

    lax.fori_loop(0, tiles, back, 0)
    for t in range(tiles - 2, tiles):
        put(t, t % 2).wait()

    for k, off in enumerate(plan.offsets):
        for there, left in plan.pairs(me, me + off):

            @pl.when(there)
            def _():
                copy(k, me, me + off, left, me + off).wait_send()

        for there, left in plan.pairs(me - off, me):

            @pl.when(there)
            def _():
                copy(k, me - off, me, left, me - off).wait_recv()

    for i in givable:
        there, hand = handed(i)

        @pl.when(there)
        def _():
            hand.wait_send()

    for k in range(plan.slots):
        found, home, _, _ = plan.taken(me, k)

        @pl.when(found > 0)
        def _():
            remote(taken_ref.at[k], taken_ref.at[k], q_send.at[k], q_recv.at[k], home).wait_recv()


def normed(values, gains, shifts):
    center = values - jnp.mean(values, axis=-1, keepdims=True)
    spread = jnp.mean(center * center, axis=-1, keepdims=True)
    return center * lax.rsqrt(spread + epsilon) * gains + shifts


def contract(left_op, right_op, left_dim, right_dim):
    return lax.dot_general(
        left_op, right_op, (((left_dim,), (right_dim,)), ((), ())), preferred_element_type=f32
    )


def wide(block, heads, head_dim):
    return jnp.concatenate([block[h * head_dim : (h + 1) * head_dim] for h in range(heads)], axis=1)


def tall(block, heads):
    return jnp.concatenate([block[:, h * CHUNK : (h + 1) * CHUNK] for h in range(heads)], axis=0)


def hi_lo(value, count):
    parts = []
    for _ in range(count):
        part = value.astype(bf16)
        parts.append(part.astype(f32))
        value = value - parts[-1]
    return parts


def scaled_queries(q, head_dim, lse_parts, row):
    width = q.shape[1]
    hi, lo = hi_lo(q.astype(f32) * (LOG2E * head_dim ** (-0.5)), 2)
    first = jnp.broadcast_to(jnp.where(row == 0, 1.0, 0.0), (1, width))
    fill = jnp.zeros((2 * head_dim - 5, width), f32)
    return jnp.concatenate([hi, lo] + lse_parts + [first, 1.0 - first, fill], axis=0).astype(bf16)


def triangle(heads):
    key = lax.broadcasted_iota(jnp.int32, (CHUNK, heads * CHUNK), 0)
    query = lax.broadcasted_iota(jnp.int32, (CHUNK, heads * CHUNK), 1) % CHUNK
    return key <= query


def causal(s, heads):
    return jnp.concatenate([s[:PAD], jnp.where(triangle(heads), s[PAD:], BIG)], axis=0)


def attend_kernel(
    plan, heads, head_dim, len_ref, q_ref, win_ref, o_ref, rest_ref, lse_ref, k_ref, v_ref, kt_ref, vt_ref, acc, top, norm
):
    i = pl.program_id(0)
    me = lax.axis_index("seq")
    place = plan.chunk(me, i)
    row = place // (ROW // CHUNK)
    end = MARGIN + (place + 1) * CHUNK
    blocks = place % (ROW // CHUNK) // (BLOCK // CHUNK) + 1

    @pl.when(i == 0)
    def _():
        first, second = len_ref[0, plan.first_row(me)], len_ref[0, plan.last_row(me)]
        filled = plan.place(plan.reaches(me), me) + plan.shard_len - MARGIN
        lane = lax.broadcasted_iota(jnp.int32, (BLOCK, 2 * head_dim), 1)
        vt_ref[head_dim:, :] = jnp.where(
            lax.broadcasted_iota(jnp.int32, (16, vt_ref.shape[1]), 0) == 0, 1.0, 0.0
        ).astype(bf16)
        norm[...] = jnp.zeros_like(norm)

        def fill(b, _):
            at = pl.ds(pl.multiple_of(b * BLOCK, BLOCK), BLOCK)
            pos = b * BLOCK - MARGIN + lax.broadcasted_iota(jnp.int32, (BLOCK, 2 * head_dim), 0)
            inside = (pos >= 0) & (pos < filled)
            both = jnp.where(inside, win_ref[at, :].astype(f32), 0.0)
            swapped = pltpu.roll(both, head_dim, 1)
            k_ref[at, : 2 * head_dim] = jnp.where(lane < head_dim, both, swapped).astype(bf16)
            one = (pos >= 0) & (pos < first)
            two = (pos >= ROW) & (pos < ROW + second)
            bias = jnp.where(lane == 3, jnp.where(one, 0.0, BIG), jnp.where(two, 0.0, BIG))
            marks = jnp.where(lane < 3, 1.0, jnp.where(lane < 5, bias, 0.0))
            k_ref[at, 2 * head_dim :] = marks.astype(bf16)
            v_ref[at, :] = jnp.where(
                lane >= head_dim, both, jnp.where(lane < 3, 1.0, 0.0)
            ).astype(bf16)
            turned = both.T
            kt_ref[:, at] = turned[:head_dim].astype(bf16)
            vt_ref[:head_dim, at] = turned[head_dim:].astype(bf16)
            norm[...] = jnp.maximum(
                norm[...],
                jnp.max(jnp.sum(jnp.square(turned[:head_dim]), axis=0, keepdims=True), axis=1, keepdims=True),
            )
            return 0

        lax.fori_loop(0, k_ref.shape[0] // BLOCK, fill, 0)

    zero = jnp.zeros((1, heads * CHUNK), f32)
    q = wide(q_ref[...], heads, head_dim)
    q_aug = scaled_queries(q, head_dim, [zero, zero, zero], row)
    q_norm = jnp.max(jnp.sum(jnp.square(q.astype(f32)), axis=0, keepdims=True), axis=1, keepdims=True)
    limit = (SAFE / LOG2E) ** 2 * head_dim
    safe = jnp.max(jnp.where(q_norm * norm[...] < limit, 1, 0)) > 0

    def scores(j):
        off = pl.multiple_of(end - (j + 1) * BLOCK, CHUNK)
        return contract(k_ref[pl.ds(off, BLOCK), :], q_aug, 1, 0)

    def values(j):
        off = pl.multiple_of(end - (j + 1) * BLOCK, CHUNK)
        return vt_ref[:, pl.ds(off, BLOCK)]

    @pl.when(safe)
    def _():
        p = jnp.exp2(causal(scores(0), heads)).astype(bf16)
        acc[...] = contract(values(0), p, 1, 0)

        def twice(k, _):
            one, two = scores(2 * k + 1), scores(2 * k + 2)
            mixed = contract(values(2 * k + 1), jnp.exp2(one).astype(bf16), 1, 0)
            acc[...] += mixed + contract(values(2 * k + 2), jnp.exp2(two).astype(bf16), 1, 0)
            return 0

        lax.fori_loop(0, (blocks - 1) // 2, twice, 0)

        @pl.when(blocks % 2 == 0)
        def _():
            acc[...] += contract(values(blocks - 1), jnp.exp2(scores(blocks - 1)).astype(bf16), 1, 0)

        top[...] = jnp.zeros_like(top)

    @pl.when(jnp.logical_not(safe))
    def _():
        s = causal(scores(0), heads)
        m = jnp.max(s, axis=0, keepdims=True)
        top[...] = m
        acc[...] = contract(values(0), jnp.exp2(s - m).astype(bf16), 1, 0)

        def step(j, _):
            s = scores(j)
            old = top[...]
            m = jnp.maximum(old, jnp.max(s, axis=0, keepdims=True))
            top[...] = m
            p = jnp.exp2(s - m).astype(bf16)
            acc[...] = acc[...] * jnp.exp2(old - m) + contract(values(j), p, 1, 0)
            return 0

        lax.fori_loop(1, blocks, step, 0)

    total = acc[head_dim : head_dim + 1, :]
    attended = tall(acc[:head_dim, :] / total, heads)
    o_ref[...] = attended.astype(bf16)
    rest_ref[...] = (attended - attended.astype(bf16).astype(f32)).astype(bf16)
    lse_ref[0] = top[...] + jnp.log2(total)


def feed_phase(
    att_ref, wo_hbm, tok_ref, cot_hbm, vecs, upb_ref, up_hbm, down_hbm, act_hbm,
    out_hbm, res_ref, gatt_ref, mat,
    up_buf, down_buf, act_buf, normal, out_acc, gn_acc, wo_ref, cot_ref, out_ref, fetch, talk,
):
    tile = mat.shape[1] // 2
    tiles = up_hbm.shape[1] // tile
    width = up_hbm.shape[0]
    out_bias, gain, shift, down_bias = (line(ref) for ref in vecs)

    def fetches(t, slot):
        at = pl.ds(pl.multiple_of(t * tile, tile), tile)
        return (
            pltpu.make_async_copy(up_hbm.at[:, at], up_buf.at[slot], fetch.at[0, slot]),
            pltpu.make_async_copy(down_hbm.at[at], down_buf.at[slot], fetch.at[1, slot]),
            pltpu.make_async_copy(act_hbm.at[t], act_buf.at[slot], fetch.at[3, slot]),
        )

    wo_copy = pltpu.make_async_copy(wo_hbm, wo_ref, fetch.at[2, 0])
    cot_copy = pltpu.make_async_copy(cot_hbm, cot_ref, fetch.at[2, 1])
    wo_copy.start()
    for copy in fetches(0, 0):
        copy.start()
    cot_copy.start()
    wo_copy.wait()

    residual = tok_ref[...].astype(f32) + contract(att_ref[...], wo_ref[...], 0, 0) + out_bias
    res_ref[...] = residual
    normal[...] = normed(residual, gain, shift).astype(bf16)
    out_acc[...] = residual + down_bias
    gn_acc[...] = jnp.zeros_like(gn_acc)
    sums = mat.shape[0] - 1
    cot_copy.wait()

    def step(t, _):
        slot = t % 2
        for copy in fetches(t, slot):
            copy.wait()

        @pl.when(t + 1 < tiles)
        def _():
            for copy in fetches(t + 1, 1 - slot):
                copy.start()

        u = contract(normal[...], up_buf[slot], 1, 0) + upb_ref[t]
        square = u * u
        th = jnp.tanh(GELU * (u + 0.044715 * (u * square)))
        half = 0.5 * (1.0 + th)
        slope = half + (0.5 * GELU) * u * (1.0 - th * th) * (1.0 + 3 * 0.044715 * square)
        activated = (u * half).astype(bf16)
        out_acc[...] += contract(activated, down_buf[slot], 1, 0)
        mat[t, tile:, :] = contract(activated, cot_ref[...], 0, 0).astype(bf16)
        talk(2 * t + 1)
        grad = (act_buf[slot] * slope).astype(bf16)
        gn_acc[...] += contract(grad, up_buf[slot], 1, 1)
        mat[t, :tile, :] = contract(grad, normal[...], 0, 0).astype(bf16)
        upb_ref[t] = jnp.sum(grad.astype(f32), axis=0, keepdims=True)
        talk(2 * t + 2)
        return 0

    lax.fori_loop(0, tiles, step, 0)
    out_ref[...] = out_acc[...].astype(bf16)
    out_copy = pltpu.make_async_copy(out_ref, out_hbm, fetch.at[2, 0])
    out_copy.start()

    residual = res_ref[...]
    center = residual - jnp.mean(residual, axis=-1, keepdims=True)
    scale = lax.rsqrt(jnp.mean(center * center, axis=-1, keepdims=True) + epsilon)
    xhat = center * scale
    gn = gn_acc[...]
    q = gn * gain
    grad = scale * (
        q - jnp.mean(q, axis=-1, keepdims=True) - xhat * jnp.mean(q * xhat, axis=-1, keepdims=True)
    )
    cot = cot_ref[...].astype(f32)
    grad = cot + grad
    res_ref[...] = grad
    proj = grad.astype(bf16)
    talk(2 * tiles + 1)
    mat[sums, :width, :] = contract(att_ref[...], proj, 1, 0).astype(bf16)
    rows = [cot, proj.astype(f32), gn * xhat, gn]
    rows = [jnp.sum(row, axis=0, keepdims=True) for row in rows]
    rows.append(jnp.zeros((16 - len(rows), width), f32))
    mat[sums, width : width + 16, :] = jnp.concatenate(rows, axis=0).astype(bf16)
    rows = [upb_ref[t] for t in range(tiles)] + [jnp.zeros((1, tile), f32)] * (16 - tiles)
    rows = jnp.concatenate([jnp.concatenate(rows, axis=0), jnp.zeros((16, width - tile), f32)], axis=1)
    mat[sums, width + 16 : width + 32, :] = rows.astype(bf16)
    rest = mat.shape[1] - width - 32
    mat[sums, width + 32 :, :] = jnp.zeros((rest, width), bf16)
    gatt_ref[...] = contract(wo_ref[...], proj, 1, 1).astype(bf16)
    out_copy.wait()


def back_phase(
    plan, heads, head_dim, me, talk, steps,
    q_hbm, taken_hbm, k_hbm, v_hbm, kt_hbm, lse_ref, o_ref, rest_hbm, gatt_ref, dq_ref,
    low, inbox, land_q, land_g, land_s, give_s, kv_send, kv_recv, help_send, help_recv,
    k_ref, v_ref, kt_ref, q_ref, q_aug, g_aug, acc, total, rest_ref, fetch, prepared,
):
    shard_len = plan.shard_len
    copies = [
        pltpu.make_async_copy(src, dst, fetch.at[k])
        for k, (src, dst) in enumerate(
            [(q_hbm, q_ref), (rest_hbm, rest_ref), (k_hbm, k_ref), (v_hbm, v_ref), (kt_hbm, kt_ref), (taken_hbm, land_q)]
        )
    ]
    for copy in copies:
        copy.start()
    total[...] = jnp.zeros_like(total)
    acc[...] = jnp.zeros_like(acc)
    for copy in copies[:2]:
        copy.wait()

    def prepare(i, q, g, lse, delta, place):
        q_aug[i] = scaled_queries(wide(q, heads, head_dim), head_dim, hi_lo(-lse, 3), place // plan.per_row)
        fill = jnp.zeros((head_dim - 3, heads * CHUNK), f32)
        marks = jnp.concatenate(hi_lo(-delta, 3) + [fill], axis=0).astype(bf16)
        g_aug[i] = jnp.concatenate([marks, wide(g, heads, head_dim)], axis=0)

    def sends(i):
        found, helper, slot, order = plan.given(me, i)
        return found > 0, [
            remote(gatt_ref.at[:, pl.ds(i * CHUNK, CHUNK)], land_g.at[slot], help_send.at[1, order], help_recv.at[1, slot], helper),
            remote(give_s.at[order], land_s.at[slot], help_send.at[2, order], help_recv.at[2, slot], helper),
        ]

    givable = sorted({entry[1] for entry in plan.help})
    for i in range(plan.per_dev):
        if i in (2, 4):
            talk(steps + i // 2 - 1)
        at = pl.ds(i * CHUNK, CHUNK)
        g = gatt_ref[:, at]
        o = o_ref[:, at].astype(f32) + rest_ref[:, at].astype(f32)
        delta = jnp.sum(wide(g.astype(f32) * o, heads, head_dim), axis=0, keepdims=True)
        prepare(i, q_ref[:, at], g, lse_ref[i], delta, plan.chunk(me, i))
        if i in givable:
            there, copies_out = sends(i)

            @pl.when(there)
            def _():
                order = plan.given(me, i)[3]
                give_s[order, :1, :] = lse_ref[i]
                give_s[order, 1:2, :] = delta
                for copy in copies_out:
                    copy.start()

    for copy in copies[2:]:
        copy.wait()

    def piece(k, off, left):
        at = pl.ds(pl.multiple_of(plan.place(me + off, me) + left, CHUNK), shard_len - left)
        box = plan.box(me + off, -off)
        land = inbox.at[box, :, pl.ds(left, shard_len - left)]
        return remote(low.at[:, at], land, kv_send.at[k], kv_recv.at[box], me + off)

    def block(i, at, place, diagonal):
        s = contract(k_ref[at, :], q_aug[i], 1, 0)
        if diagonal:
            key = lax.broadcasted_iota(jnp.int32, (BLOCK, heads * CHUNK), 0)
            query = lax.broadcasted_iota(jnp.int32, (BLOCK, heads * CHUNK), 1) % CHUNK
            s = jnp.where(key - query <= place % (BLOCK // CHUNK) * CHUNK, s, BIG)
        dp = contract(v_ref[at, :], g_aug[i], 1, 0)
        p = jnp.exp2(s)
        ds = (p * dp).astype(bf16)
        p = p.astype(bf16)
        acc[i] += contract(kt_ref[:, at], ds, 1, 0)
        dk = contract(q_aug[i, : 2 * head_dim, :], ds, 1, 1)
        total[:head_dim, at] += dk[:head_dim] + dk[head_dim:]
        total[head_dim:, at] += contract(g_aug[i, head_dim:, :], p, 1, 1)

    def walk(count, locate, turn, n):
        def key_step(b, n):
            at = pl.ds(pl.multiple_of(MARGIN + b * BLOCK, BLOCK), BLOCK)

            def chunk_step(i, n):
                there, place = locate(i)
                last = place // (BLOCK // CHUNK)
                active = there & (b <= last) & (b // (ROW // BLOCK) == place // plan.per_row)

                @pl.when(active)
                def _():
                    talk(n)

                @pl.when(active & (b < last))
                def _():
                    block(i, at, place, False)

                @pl.when(active & (b == last))
                def _():
                    block(i, at, place, True)

                return n + jnp.where(active, 1, 0)

            n = lax.fori_loop(0, count, chunk_step, n)
            for k, off in enumerate(plan.offsets):
                end = plan.place(me + off, me) + shard_len - MARGIN

                for there, left in plan.pairs(me + off, me):

                    @pl.when(there & (b == (end + BLOCK - 1) // BLOCK - 1) & (plan.helps(me) == turn))
                    def _():
                        at = pl.ds(pl.multiple_of(plan.place(me + off, me), CHUNK), shard_len)
                        low[:head_dim, at] = (total[:head_dim, at] * (1.0 / LOG2E)).astype(bf16)
                        low[head_dim:, at] = total[head_dim:, at].astype(bf16)
                        piece(k, off, left).start()

            return n

        return lax.fori_loop(0, plan.span // BLOCK, key_step, n)

    def own(i):
        return plan.given(me, i)[0] == 0, plan.chunk(me, i)

    n = walk(plan.per_dev, own, 0, steps + 2)
    for i in range(plan.per_dev):
        dq_ref[:, i * CHUNK : (i + 1) * CHUNK] = tall(acc[i] * head_dim ** (-0.5), heads).astype(bf16)

    def taken(k):
        found, home, i, _ = plan.taken(me, k)
        return found > 0, plan.chunk(home, i, me)

    for k in range(plan.slots):
        there, place = taken(k)
        home = plan.taken(me, k)[1]

        @pl.when(there)
        def _():
            for part, land in ((1, land_g), (2, land_s)):
                remote(land.at[k], land.at[k], help_send.at[part, 0], help_recv.at[part, k], home).wait_recv()
            prepare(k, land_q[k], land_g[k], land_s[k, :1, :], land_s[k, 1:2, :], place)
            acc[k] = jnp.zeros_like(acc[k])

    for i in givable:
        there, copies_out = sends(i)

        @pl.when(there)
        def _():
            for copy in copies_out:
                copy.wait_send()

    prepared()
    n = walk(plan.slots, taken, 1, n)
    for k in range(plan.slots):
        there, _ = taken(k)
        _, home, _, order = plan.taken(me, k)

        @pl.when(there)
        def _():
            land_q[k] = tall(acc[k] * head_dim ** (-0.5), heads).astype(bf16)
            remote(land_q.at[k], land_g.at[order], help_send.at[3, k], help_recv.at[3, order], home).start()

    mine = pl.ds(pl.multiple_of(plan.place(me, me), CHUNK), shard_len)
    acc_kv = total[:, mine]
    total[:, :shard_len] = jnp.concatenate(
        [acc_kv[:head_dim] * (1.0 / LOG2E), acc_kv[head_dim:]], axis=0
    )
    return n


def layer_kernel(
    plan, heads, head_dim,
    att_ref, tok_ref, ob_ref, gain_ref, shift_ref, db_ref, upb_ref, lse_ref, gain_one_ref,
    wo_hbm, cot_hbm, up_hbm, down_hbm, act_hbm, rest_hbm, q_hbm, taken_hbm, k_hbm, v_hbm, kt_hbm, normal_hbm, wq_hbm, wkv_hbm,
    sum_ref, out_hbm, end_mat, tiny_mat, res_ref,
    gatt_ref, low, inbox, land_q, land_g, land_s, give_s, mat, upb_mat,
    feed_fetch, back_fetch, kv_send, kv_recv, help_send, help_recv, load, *summing,
):
    me = lax.axis_index("seq")
    shard_len, width = tok_ref.shape
    pieces, height, _ = mat.shape
    third = len(summing) // 3
    refs = [summing[k * third : (k + 1) * third] for k in range(3)]
    summed = Summing(plan, ORDERS, TABLE, height, mat, *refs[0][:2], refs[0][2:])
    ending = Summing(plan, LAST_ORDERS, LAST_TABLE, end_mat.shape[1], end_mat, *refs[1][:2], refs[1][2:])
    tiny = Summing(plan, TINY_ORDERS, TINY_TABLE, tiny_mat.shape[1], tiny_mat, *refs[2][:2], refs[2][2:])
    greet(plan, me, summed.partners())
    givable = sorted({entry[1] for entry in plan.help})
    for t in range(upb_mat.shape[0]):
        wide_t = upb_mat.shape[2]
        upb_mat[t] = upb_ref[pl.ds(t * wide_t, wide_t)].reshape(1, wide_t)

    def store(p):
        pltpu.make_async_copy(mat.at[p], sum_ref.at[p], load.at[p]).start()

    def talk(n):
        summed.step(n, store)

    def first(up_buf, down_buf, act_buf, normal, out_acc, gn_acc, wo_ref, cot_ref, out_ref):
        feed_phase(
            att_ref, wo_hbm, tok_ref, cot_hbm, (ob_ref, gain_ref, shift_ref, db_ref), upb_mat, up_hbm, down_hbm, act_hbm,
            out_hbm, res_ref, gatt_ref, mat,
            up_buf, down_buf, act_buf, normal, out_acc, gn_acc, wo_ref, cot_ref, out_ref, feed_fetch, talk,
        )

    tile = height // 2
    pl.run_scoped(
        first,
        pltpu.VMEM((2, width, tile), bf16),
        pltpu.VMEM((2, tile, width), bf16),
        pltpu.VMEM((2, shard_len, tile), f32),
        pltpu.VMEM((shard_len, width), bf16),
        pltpu.VMEM((shard_len, width), f32),
        pltpu.VMEM((shard_len, width), f32),
        pltpu.VMEM((width, width), bf16),
        pltpu.VMEM((shard_len, width), bf16),
        pltpu.VMEM((shard_len, width), bf16),
    )
    talk(2 * pieces)
    window, columns = plan.window, heads * CHUNK
    chunks = plan.per_dev

    def second(k_ref, v_ref, kt_ref, q_ref, q_aug, g_aug, acc, total, spare, wkv):
        copies = [
            pltpu.make_async_copy(src, dst, back_fetch.at[6 + k])
            for k, (src, dst) in enumerate([(normal_hbm, gatt_ref), (wq_hbm, spare), (wkv_hbm, wkv)])
        ]

        def later():
            for copy in copies:
                copy.start()

        done = back_phase(
            plan, heads, head_dim, me, talk, 2 * pieces + 1,
            q_hbm, taken_hbm, k_hbm, v_hbm, kt_hbm, lse_ref, att_ref, rest_hbm, gatt_ref, q_ref,
            low, inbox, land_q, land_g, land_s, give_s, kv_send, kv_recv, help_send, help_recv,
            k_ref, v_ref, kt_ref, q_ref, q_aug, g_aug, acc, total, spare, back_fetch, later,
        )

        def drain(n, _):
            talk(n)
            return 0

        busy = 2 * pieces + 3 + plan.blocks
        lax.fori_loop(done, busy, drain, 0)
        for i in givable:
            found, helper, _, order = plan.given(me, i)

            @pl.when(found > 0)
            def _():
                land = land_g.at[order]
                remote(land, land, help_send.at[3, 0], help_recv.at[3, order], helper).wait_recv()
                q_ref[:, i * CHUNK : (i + 1) * CHUNK] = land_g[order]

        for copy in copies:
            copy.wait()
        normal, wq = gatt_ref, spare
        tall_part, wide_part = end_mat.shape[1:]
        grad = contract(normal[...], q_ref[...], 0, 1).astype(bf16)
        rest = width - tall_part
        for k in range(2):
            at = slice(k * wide_part, (k + 1) * wide_part)
            end_mat[k] = grad[:tall_part, at]
            end_mat[2, k * rest : (k + 1) * rest, :] = grad[tall_part:, at]

        def joint(n):
            talk(n)
            ending.step(n)
            tiny.step(n)

        for k in range(3):
            joint(busy + k)
        grad_qb = jnp.sum(q_ref[...].astype(f32).T, axis=0, keepdims=True)
        gn = contract(q_ref[...], wq[...], 0, 1)
        joint(busy + 3)

        for k, off in enumerate(plan.offsets):

            for there, left in plan.pairs(me, me + off):

                @pl.when(there)
                def _():
                    box = plan.box(me, off)
                    part = pl.ds(left, shard_len - left)
                    land = inbox.at[box, :, part]
                    remote(land, land, kv_send.at[0], kv_recv.at[box], me + off).wait_recv()
                    total[:, part] += inbox[box, :, part].astype(f32)

            for there, left in plan.pairs(me + off, me):

                @pl.when(there)
                def _():
                    some = inbox.at[0, :, pl.ds(left, shard_len - left)]
                    remote(some, some, kv_send.at[k], kv_recv.at[0], me + off).wait_send()

        for k in range(plan.slots):
            found, home, _, order = plan.taken(me, k)

            @pl.when(found > 0)
            def _():
                remote(
                    land_q.at[k], land_g.at[order], help_send.at[3, k], help_recv.at[3, order], home
                ).wait_send()

        grad_kv = total[:, :shard_len].astype(bf16)
        gn = gn + contract(grad_kv, wkv[...], 0, 1)
        grad = contract(grad_kv, normal[...], 1, 0).astype(bf16)
        pair, piece = 2 * head_dim, tiny_mat.shape[2]
        parts = width // piece
        for k in range(parts):
            tiny_mat[0, k * pair : (k + 1) * pair, :] = grad[:, k * piece : (k + 1) * piece]
        grad_vb = jnp.sum(grad_kv.astype(f32).T, axis=0, keepdims=True)

        tok = tok_ref[...].astype(f32)
        center = tok - jnp.mean(tok, axis=-1, keepdims=True)
        scale = lax.rsqrt(jnp.mean(center * center, axis=-1, keepdims=True) + epsilon)
        xhat = center * scale
        grads = [gn * xhat, gn]
        rows = [jnp.sum(grad, axis=0, keepdims=True) for grad in grads] + [grad_qb]
        rows.append(jnp.concatenate([grad_vb, jnp.zeros((1, width - 2 * head_dim), f32)], axis=1))
        rows.append(jnp.zeros((16 - len(rows), width), f32))
        rows = jnp.concatenate(rows, axis=0).astype(bf16)
        for k in range(parts):
            at = parts * pair + 16 * k
            tiny_mat[0, at : at + 16, :] = rows[:, k * piece : (k + 1) * piece]
        at = parts * (pair + 16)
        tiny_mat[0, at:, :] = jnp.zeros((tiny_mat.shape[1] - at, piece), bf16)
        joint(busy + 4)
        q = gn * line(gain_one_ref)
        res_ref[...] += scale * (
            q - jnp.mean(q, axis=-1, keepdims=True) - xhat * jnp.mean(q * xhat, axis=-1, keepdims=True)
        )


        def finish(n, _):
            joint(n)
            return 0

        lax.fori_loop(busy + 5, max(summed.end, ending.end, tiny.end), finish, 0)

    pl.run_scoped(
        second,
        pltpu.VMEM((window, 4 * head_dim), bf16),
        pltpu.VMEM((window, 2 * head_dim), bf16),
        pltpu.VMEM((head_dim, window), bf16),
        pltpu.VMEM((width, shard_len), bf16),
        pltpu.VMEM((chunks, 4 * head_dim, columns), bf16),
        pltpu.VMEM((chunks, 2 * head_dim, columns), bf16),
        pltpu.VMEM((chunks, head_dim, columns), f32),
        pltpu.VMEM((2 * head_dim, window), f32),
        pltpu.VMEM(wq_hbm.shape, bf16),
        pltpu.VMEM(wkv_hbm.shape, bf16),
    )
    for p in range(pieces):
        pltpu.make_async_copy(mat.at[p], sum_ref.at[p], load.at[p]).wait()


def final_kernel(
    head_dim,
    sum_ref, rest_ref, last_ref, small_ref, tok_ref, grad_ref,
    tok_out, grad_out, up_ref, down_ref, out_ref, q_ref, kv_ref, upb_ref,
    db_ref, ob_ref, gain_two_ref, shift_two_ref, gain_one_ref, shift_one_ref, qb_ref, vb_ref,
):
    tok_out[...] = tok_ref[...]
    grad_out[...] = grad_ref[...]
    i = pl.program_id(0)
    tile, width = down_ref.shape
    up_ref[...] = sum_ref[0, :tile, :].astype(f32).T
    down_ref[...] = sum_ref[0, tile:, :].astype(f32)

    @pl.when(i == 0)
    def _():
        out_ref[...] = rest_ref[0, :width, :].astype(f32)
        half, side, pair = width // 2, width - tile, 2 * head_dim
        for k in range(2):
            at = slice(k * half, (k + 1) * half)
            q_ref[:tile, at] = last_ref[k].astype(f32)
            q_ref[tile:, at] = last_ref[2, k * side : (k + 1) * side, :].astype(f32)
        small = small_ref[0].astype(f32)
        parts = width // small.shape[1]
        kv_ref[...] = jnp.concatenate([small[k * pair : (k + 1) * pair] for k in range(parts)], axis=1).T
        rows = rest_ref[0, width : width + 32, :].astype(f32)
        for k, ref in enumerate([db_ref, ob_ref, gain_two_ref, shift_two_ref]):
            ref[...] = rows[k : k + 1].reshape(width)
        for t in range(upb_ref.shape[0] // tile):
            upb_ref[pl.ds(t * tile, tile)] = rows[16 + t : 17 + t, :tile].reshape(tile)
        rows = [small[parts * pair + 16 * k : parts * pair + 16 * (k + 1)] for k in range(parts)]
        rows = jnp.concatenate(rows, axis=1)
        for k, ref in enumerate([gain_one_ref, shift_one_ref, qb_ref]):
            ref[...] = rows[k : k + 1].reshape(width)
        vb_ref[...] = rows[3:4, head_dim : 2 * head_dim].reshape(head_dim)


def whole(shape):
    return pl.BlockSpec(shape, lambda i: (0,) * len(shape))


def column(height):
    return pl.BlockSpec((height, CHUNK), lambda i: (0, i))


def lead(shape):
    return pl.BlockSpec((1,) + shape, lambda i: (i,) + (0,) * len(shape))


def per_device(
    plan,
    tokens,
    lengths,
    cotangent,
    norm1_gain,
    norm1_shift,
    query_weight,
    query_bias,
    keyval_weight,
    value_bias,
    out_weight,
    out_bias,
    norm2_gain,
    norm2_shift,
    up_weight,
    up_bias,
    down_weight,
    down_bias,
):
    shard_len, width = tokens.shape[1:]
    head_dim = keyval_weight.shape[1] // 2
    heads = width // head_dim
    columns = heads * CHUNK
    chunks = plan.per_dev
    window = plan.window
    limit = dict(vmem_limit_bytes=63 * 2**20)
    vmem = pl.BlockSpec(memory_space=pltpu.VMEM)
    anywhere = pl.BlockSpec(memory_space=pl.ANY)
    dma = pltpu.SemaphoreType.DMA

    hidden = up_weight.shape[1]
    tile = PIECE // 2
    tiles = hidden // tile
    normal_one, queries, keyvals, taken, grad_act = pl.pallas_call(
        partial(gather_kernel, plan),
        in_specs=[vmem] * 7 + [anywhere] * 2,
        out_specs=[vmem] * 4 + [anywhere],
        out_shape=[
            jax.ShapeDtypeStruct((shard_len, width), bf16),
            jax.ShapeDtypeStruct((width, shard_len), bf16),
            jax.ShapeDtypeStruct((window, 2 * head_dim), bf16),
            jax.ShapeDtypeStruct((plan.slots, width, CHUNK), bf16),
            jax.ShapeDtypeStruct((tiles, shard_len, tile), f32),
        ],
        scratch_shapes=[
            pltpu.VMEM((shard_len, 2 * head_dim), bf16),
            pltpu.VMEM((shard_len, width), bf16),
            pltpu.VMEM((hidden, width), bf16),
            pltpu.VMEM((2, shard_len, tile), f32),
        ]
        + [dma((len(plan.offsets),))] * 2
        + [dma((plan.slots,))] * 2
        + [dma((2,))],
        compiler_params=pltpu.CompilerParams(collective_id=0, has_side_effects=True, **limit),
        name="gather",
    )(
        tokens[0],
        norm1_gain,
        norm1_shift,
        keyval_weight,
        value_bias,
        query_weight,
        query_bias,
        cotangent[0],
        down_weight,
    )

    attended, attended_low, lse, k_aug, v_aug, k_turned = pl.pallas_call(
        partial(attend_kernel, plan, heads, head_dim),
        grid_spec=pltpu.PrefetchScalarGridSpec(
            num_scalar_prefetch=0,
            grid=(chunks,),
            in_specs=[
                pl.BlockSpec(memory_space=pltpu.SMEM),
                column(width),
                whole((window, 2 * head_dim)),
            ],
            out_specs=[
                column(width),
                column(width),
                lead((1, columns)),
                whole((window, 4 * head_dim)),
                whole((window, 2 * head_dim)),
                whole((head_dim, window)),
            ],
            scratch_shapes=[
                pltpu.VMEM((head_dim + 16, window), bf16),
                pltpu.VMEM((head_dim + 16, columns), f32),
                pltpu.VMEM((1, columns), f32),
                pltpu.VMEM((1, 1), f32),
            ],
        ),
        out_shape=[
            jax.ShapeDtypeStruct((width, shard_len), bf16),
            jax.ShapeDtypeStruct((width, shard_len), bf16),
            jax.ShapeDtypeStruct((chunks, 1, columns), f32),
            jax.ShapeDtypeStruct((window, 4 * head_dim), bf16),
            jax.ShapeDtypeStruct((window, 2 * head_dim), bf16),
            jax.ShapeDtypeStruct((head_dim, window), bf16),
        ],
        compiler_params=pltpu.CompilerParams(**limit),
        name="attend",
    )(lengths, queries, keyvals)

    inputs = tokens[0].astype(f32)
    pieces = tiles + 1
    assert pieces == len(ORDERS) and 2 * (width - tile) == tile and 3 * (2 * head_dim + 16) <= tile
    sums, outputs, last, small, grad_inputs = pl.pallas_call(
        partial(layer_kernel, plan, heads, head_dim),
        in_specs=[vmem] * 9 + [anywhere] * 14,
        out_specs=[anywhere] * 2 + [vmem] * 3,
        out_shape=[
            jax.ShapeDtypeStruct((pieces, PIECE, width), bf16),
            jax.ShapeDtypeStruct((shard_len, width), bf16),
            jax.ShapeDtypeStruct((3, tile, width // 2), bf16),
            jax.ShapeDtypeStruct((1, tile, width // 3), bf16),
            jax.ShapeDtypeStruct((shard_len, width), f32),
        ],
        scratch_shapes=[
            pltpu.VMEM((width, shard_len), bf16),
            pltpu.VMEM((2 * head_dim, window), bf16),
            pltpu.VMEM((plan.inboxes, 2 * head_dim, shard_len), bf16),
            pltpu.VMEM((plan.slots, width, CHUNK), bf16),
            pltpu.VMEM((plan.slots, width, CHUNK), bf16),
            pltpu.VMEM((plan.slots, 8, columns), f32),
            pltpu.VMEM((plan.slots, 8, columns), f32),
            pltpu.VMEM((pieces, PIECE, width), bf16),
            pltpu.VMEM((tiles, 1, tile), f32),
            dma((4, 2)),
            dma((9,)),
            dma((len(plan.offsets),)),
            dma((plan.inboxes,)),
            dma((4, plan.slots)),
            dma((4, plan.slots)),
            dma((pieces,)),
        ]
        + Summing.scratch(plan, pieces, PIECE, width)
        + Summing.scratch(plan, 3, tile, width // 2)
        + Summing.scratch(plan, 1, tile, width // 3),
        compiler_params=pltpu.CompilerParams(collective_id=1, has_side_effects=True, **limit),
        name="layer",
    )(
        attended,
        tokens[0],
        out_bias,
        norm2_gain,
        norm2_shift,
        down_bias,
        up_bias,
        lse,
        norm1_gain,
        out_weight,
        cotangent[0],
        up_weight,
        down_weight,
        grad_act,
        attended_low,
        queries,
        taken,
        k_aug,
        v_aug,
        k_turned,
        normal_one,
        query_weight,
        keyval_weight,
    )

    vector = jax.ShapeDtypeStruct((width,), f32)
    finals = pl.pallas_call(
        partial(final_kernel, head_dim),
        grid=(tiles,),
        in_specs=[
            lead((PIECE, width)),
            pl.BlockSpec((1, PIECE, width), lambda i: (tiles, 0, 0)),
            whole((3, tile, width // 2)),
            whole((1, tile, width // 3)),
            pl.BlockSpec((shard_len // tiles, width), lambda i: (i, 0)),
            pl.BlockSpec((shard_len // tiles, width), lambda i: (i, 0)),
        ],
        out_specs=[
            pl.BlockSpec((shard_len // tiles, width), lambda i: (i, 0)),
            pl.BlockSpec((shard_len // tiles, width), lambda i: (i, 0)),
            pl.BlockSpec((width, tile), lambda i: (0, i)),
            pl.BlockSpec((tile, width), lambda i: (i, 0)),
            whole((width, width)),
            whole((width, width)),
            whole((width, 2 * head_dim)),
            whole((hidden,)),
        ]
        + [whole((width,))] * 7
        + [whole((head_dim,))],
        out_shape=[
            jax.ShapeDtypeStruct((shard_len, width), bf16),
            jax.ShapeDtypeStruct((shard_len, width), f32),
            jax.ShapeDtypeStruct((width, hidden), f32),
            jax.ShapeDtypeStruct((hidden, width), f32),
            jax.ShapeDtypeStruct((width, width), f32),
            jax.ShapeDtypeStruct((width, width), f32),
            jax.ShapeDtypeStruct((width, 2 * head_dim), f32),
            jax.ShapeDtypeStruct((hidden,), f32),
        ]
        + [vector] * 7
        + [jax.ShapeDtypeStruct((head_dim,), f32)],
        compiler_params=pltpu.CompilerParams(**limit),
        name="finals",
    )(sums, sums, last, small, outputs, grad_inputs)
    outputs, grad_inputs, up_w, down_w, out_w, qw, kvw, up_b = finals[:8]
    down_b, out_b, gain_two, shift_two, gain_one, shift_one, qb, vb = finals[8:]
    return (
        outputs[None],
        grad_inputs[None],
        gain_one,
        shift_one,
        qw,
        qb,
        kvw,
        vb,
        out_w,
        out_b,
        gain_two,
        shift_two,
        up_w,
        up_b,
        down_w,
        down_b,
    )


def solution(mesh):
    split = P("dp", "seq", None)
    devices = mesh.shape["seq"]

    def run(*arrays):
        plan = Plan(devices, arrays[0].shape[1] // devices)
        return jax.shard_map(
            partial(per_device, plan),
            mesh=mesh,
            in_specs=(split, P("dp", None), split) + (P(),) * 14,
            out_specs=(split, split) + (P(),) * 14,
            check_vma=False,
        )(*arrays)

    return run
```

```python
from functools import partial

import jax
import jax.numpy as jnp
import numpy as np
from jax import lax
from jax.experimental import pallas as pl
from jax.experimental.pallas import tpu as pltpu
from jax.sharding import PartitionSpec as P

ROW = 4096
CHUNK = 128
BLOCK = 512
PAD = BLOCK - CHUNK
LOG2E = 1.4426950408889634
BIG = -1e30
MARGIN = BLOCK
PIECE = 1024
ORDERS = ((0, 1, 2), (1, 0, 2), (2, 1, 0), (2, 0, 1), (1, 0, 2), (0, 1, 2), (1, 0, 2))
TABLE = (
    (2, 4, 6, 8, 10, 12, 14),
    (4, 6, 8, 10, 12, 14, 16),
    (10, 12, 14, 16, 18, 20, 21),
    (15, 17, 19, 21, 23, 25, 26),
    (19, 21, 23, 25, 27, 29, 30),
    (23, 25, 27, 29, 31, 33, 34),
    (26, 28, 30, 32, 34, 36, 37),
    (30, 32, 34, 36, 38, 40, 41),
    (36, 40, 42, 44, 46, 48, 49),
    (42, 46, 48, 50, 52, 51, 55),
    (45, 49, 51, 53, 55, 57, 58),
)
LAST_ORDERS = ((0, 1, 2), (1, 0, 2), (0, 1, 2))
LAST_TABLE = (
    (49, 50, 51),
    (52, 53, 54),
    (55, 56, 57),
    (58, 59, 60),
    (62, 63, 64),
    (65, 66, 67),
    (68, 69, 70),
    (71, 72, 73),
    (74, 75, 76),
)
TINY_ORDERS = ((1, 0, 2),)
TINY_TABLE = ((53,), (55,), (58,), (61,), (65,), (68,), (71,), (74,), (77,))
SAFE = 60.0
epsilon = 1e-05
GELU = 0.7978845608028654
bf16 = jnp.bfloat16
f32 = jnp.float32


HELP = (
    (4, 4, 0, 0), (4, 5, 0, 1), (3, 5, 1, 0), (10, 3, 6, 0), (9, 4, 6, 1), (9, 5, 7, 0),
    (15, 4, 11, 0), (15, 5, 11, 1), (14, 5, 12, 0),
)
UNIT = 16


class Plan:
    def __init__(self, devices, shard_len):
        self.devices = devices
        self.shard_len = shard_len
        self.per_dev = shard_len // CHUNK
        self.per_row = ROW // CHUNK
        assert shard_len % CHUNK == 0 and shard_len <= ROW
        ends = [(d + 1) * shard_len - self.first_row(d) * ROW for d in range(devices)]
        self.span = -(-max(ends) // BLOCK) * BLOCK
        self.window = MARGIN + self.span
        self.help = HELP if devices % UNIT == 0 and shard_len * UNIT == 3 * ROW else ()
        self.slots = 2
        self.top = {}
        for home, _, helper, _ in self.help:
            self.top[helper] = max(home, self.top.get(helper, 0))
        helpers = sorted(self.top)
        self.kinds = {helper: k % 2 for k, helper in enumerate(helpers)}
        self.reach = max(
            d - e for d in range(devices) for e in range(d + 1) if self.first_row(d) <= self.last_row(e)
        )
        self.skips = sorted({self.skip(d, h) for d in range(devices) for h in range(d, min(d + self.reach + 1, devices))
                             if self.first_row(h) <= self.last_row(d)})
        self.blocks = max(self.load(d) for d in range(devices))
        self.offsets = [o for o in range(-self.reach, self.reach + 1) if o != 0]
        self.inboxes = self.reach + 2

    def load(self, device):
        def blocks(d, i):
            return self.chunk(d, i) % self.per_row // (BLOCK // CHUNK) + 1

        unit, place = device // UNIT * UNIT, device % UNIT
        moved = {(home, i) for home, i, _, _ in self.help}
        total = sum(blocks(device, i) for i in range(self.per_dev) if (place, i) not in moved)
        return total + sum(blocks(unit + home, i) for home, i, helper, _ in self.help if helper == place)

    def first_row(self, device):
        return device * self.shard_len // ROW

    def last_row(self, device):
        return ((device + 1) * self.shard_len - 1) // ROW

    def lookup(self, device, table, default):
        place = device % UNIT
        value = default
        for key, entry in table.items():
            value = jnp.where(place == key, entry, value)
        return value

    def reaches(self, device):
        extra = {helper: top - helper for helper, top in self.top.items()}
        return device + self.lookup(device, extra, 0)

    def helps(self, device):
        return self.lookup(device, {helper: 1 for helper in self.top}, 0)

    def feeds(self, source, holder):
        return (
            (source >= 0)
            & (holder >= 0)
            & (source < self.devices)
            & (holder < self.devices)
            & (self.first_row(holder) <= self.last_row(source))
            & (source <= self.reaches(holder))
        )

    def given(self, device, i):
        place = device % UNIT
        found, helper, slot, order = 0, 0, 0, 0
        counts = {}
        for home, chunk, to, k in self.help:
            here = jnp.where((place == home) & (i == chunk), 1, 0)
            found, slot = found + here, slot + here * k
            helper = helper + here * (to - home)
            order = order + here * counts.get(home, 0)
            counts[home] = counts.get(home, 0) + 1
        return found, device + helper, slot, order

    def taken(self, device, k):
        place = device % UNIT
        found, home, i, order = 0, 0, 0, 0
        counts = {}
        for owner, chunk, helper, slot in self.help:
            here = jnp.where((place == helper) & (k == slot), 1, 0)
            found, i = found + here, i + here * chunk
            home = home + here * (owner - helper)
            order = order + here * counts.get(owner, 0)
            counts[owner] = counts.get(owner, 0) + 1
        return found, device + home, i, order

    def box(self, owner, off):
        return off - 1 if off > 0 else self.reach + self.lookup(owner + off, self.kinds, 0)

    def skip(self, source, holder):
        gap = self.first_row(holder) * ROW - source * self.shard_len
        return max(gap, 0) if isinstance(gap, int) else jnp.where(gap > 0, gap, 0)

    def pairs(self, source, holder):
        return [(self.feeds(source, holder) & (self.skip(source, holder) == left), left) for left in self.skips]

    def place(self, source, holder):
        return MARGIN + source * self.shard_len - self.first_row(holder) * ROW

    def chunk(self, device, i, holder=None):
        return device * self.per_dev + i - self.first_row(device if holder is None else holder) * self.per_row


class Summing:
    def __init__(self, plan, orders, table, height, mat, inbox, extra, sems):
        self.pieces, self.height, self.orders = len(orders), height, orders
        self.mat, self.inbox, self.extra = mat, inbox, extra
        self.out_send, self.out_recv, self.back_send, self.back_recv, self.free = sems
        self.bits = plan.devices.bit_length() - 1
        self.halvings = 1 + min(self.bits, 4)
        self.swaps = self.bits + 1 - self.halvings
        self.stages = 2 * self.halvings + self.swaps
        if table is not None:
            self.schedule(table)
        self.seq, self.dp = lax.axis_index("seq"), lax.axis_index("dp")

    def schedule(self, table):
        if len(table) != self.stages + 1:
            table = [[start + 3 * s for start in table[0]] for s in range(self.stages + 1)]
        self.table = table
        self.end = max(max(row) for row in table) + 1

    @staticmethod
    def scratch(plan, pieces, height, width):
        bits = plan.devices.bit_length() - 1
        halvings = 1 + min(bits, 4)
        swaps = bits + 1 - halvings
        last = height >> halvings
        dma = pltpu.SemaphoreType.DMA
        return [
            pltpu.VMEM((pieces, height - last, width), bf16),
            pltpu.VMEM((max(swaps, 1), pieces, last, width), bf16),
            dma((6 + swaps, pieces)),
            dma((6 + swaps, pieces)),
            dma((6, pieces)),
            dma((6, pieces)),
            pltpu.SemaphoreType.REGULAR((6, pieces)),
        ]

    def partners(self):
        bits = [(self.seq >> b) & 1 for b in range(self.bits)]
        steps = [(1 - 2 * bit) * (1 << b) for b, bit in enumerate(bits)]
        if self.bits >= 4:
            steps.append(steps[2] + steps[3])
        return [(self.seq, 1 - self.dp)] + [(self.seq + step, self.dp) for step in steps]

    def spots(self, p, count):
        spots, starts, at = [], [0], 0
        for t in range(count):
            if t == 0:
                bit, device = self.dp, {"seq": self.seq, "dp": 1 - self.dp}
            else:
                if t < 4:
                    word = sum(order[t - 1] << (2 * k) for k, order in enumerate(self.orders))
                    axis = lax.shift_right_logical(np.int32(word), 2 * p) & 3
                else:
                    axis = t - 1
                bit = lax.shift_right_logical(self.seq, axis) & 1
                step = lax.shift_left(np.int32(1), axis) if t < 4 else 1 << axis
                device = {"seq": self.seq + (1 - 2 * bit) * step, "dp": self.dp}
            spots.append((bit, device))
            at = at + bit * (self.height >> (t + 1))
            starts.append(at)
        return spots, starts

    def rows(self, start, size):
        return pl.ds(pl.multiple_of(start, size), size)

    def remote(self, src, dst, sems, device):
        return pltpu.make_async_remote_copy(
            src_ref=src,
            dst_ref=dst,
            send_sem=sems[0],
            recv_sem=sems[1],
            device_id=device,
            device_id_type=pl.DeviceIdType.MESH,
        )

    def sems(self, stage, p):
        if stage < self.halvings + self.swaps:
            return self.out_send.at[stage, p], self.out_recv.at[stage, p]
        t = self.stages - 1 - stage
        return self.back_send.at[t, p], self.back_recv.at[t, p]

    def size(self, stage):
        h, w = self.halvings, self.swaps
        t = stage if stage < h else h - 1 if stage < h + w else self.stages - 1 - stage
        return self.height >> (t + 1)

    def event(self, stage, p):
        h, w, last = self.halvings, self.swaps, self.stages
        depth = min(stage + 1, h + w) if stage < h + w else last - stage
        spots, starts = self.spots(p, max(depth, 1))
        if stage > 0:
            before = stage - 1
            size = self.size(before)
            some = self.mat.at[p, pl.ds(0, size)]
            wait = self.remote(some, some, self.sems(before, p), spots[0][1])
            wait.wait()
            if before < h:
                at = self.rows(starts[before + 1], size)
                self.mat[p, at, :] = self.mat[p, at, :] + self.inbox[p, pl.ds(self.height - 2 * size, size), :]
                pl.semaphore_signal(
                    self.free.at[before, p],
                    inc=1,
                    device_id=spots[before][1],
                    device_id_type=pl.DeviceIdType.MESH,
                )
            elif before < h + w:
                at = self.rows(starts[h], size)
                self.mat[p, at, :] = self.mat[p, at, :] + self.extra[before - h, p]
        if stage < h:
            size = self.size(stage)
            bit, device = spots[stage]
            src = self.mat.at[p, self.rows(starts[stage] + (1 - bit) * size, size)]
            dst = self.inbox.at[p, pl.ds(self.height - 2 * size, size)]
            self.remote(src, dst, self.sems(stage, p), device).start()
        elif stage < h + w:
            src = self.mat.at[p, self.rows(starts[h], self.size(stage))]
            self.remote(src, self.extra.at[stage - h, p], self.sems(stage, p), spots[stage][1]).start()
        elif stage < last:
            t = last - 1 - stage
            pl.semaphore_wait(self.free.at[t, p], 1)
            src = self.mat.at[p, self.rows(starts[t + 1], self.size(stage))]
            self.remote(src, src, self.sems(stage, p), spots[t][1]).start()

    def step(self, n, last=None):
        for stage in range(self.stages, -1, -1):
            p = -1
            for k, step in enumerate(self.table[stage]):
                p = jnp.where(n == step, k, p)

            @pl.when(p >= 0)
            def _():
                self.event(stage, p)
                if stage == self.stages and last is not None:
                    last(p)


class FlatSumming(Summing):
    def __init__(self, plan, orders, table, height, mat, inbox, extra, sems):
        super().__init__(plan, orders, None, height, mat, inbox, extra, sems)
        self.halvings = 3
        self.stages = 2 * self.halvings + self.swaps + 2
        self.schedule(table)
        place = lax.shift_right_logical(self.seq, 2) & 3
        flip, flop = 1 - 2 * (place & 1), 2 - 4 * lax.shift_right_logical(place, 1)
        self.place = place
        self.others = [place + flip, place + flop, place + flip + flop]

    def quarter(self, start, index):
        size = self.height >> 5
        return pl.ds(pl.multiple_of(start + index * size, size), size)

    def peer(self, index):
        return {"seq": self.seq + 4 * (index - self.place), "dp": self.dp}

    def exchange(self, p, sems, d):
        some = self.mat.at[p, pl.ds(0, self.height >> 5)]
        self.remote(some, some, (sems[0].at[3 + d, p], sems[1].at[3 + d, p]), self.peer(self.others[d])).wait()

    def event(self, stage, p):
        h, w, last = self.halvings, self.swaps, self.stages
        spots, starts = self.spots(p, h)
        base = starts[h]
        out, back = (self.out_send, self.out_recv), (self.back_send, self.back_recv)
        before = stage - 1
        if before >= 0 and before < h:
            size = self.height >> (before + 1)
            some = self.mat.at[p, pl.ds(0, size)]
            self.remote(some, some, (out[0].at[before, p], out[1].at[before, p]), spots[0][1]).wait()
            at = self.rows(starts[before + 1], size)
            self.mat[p, at, :] = self.mat[p, at, :] + self.inbox[p, pl.ds(self.height - 2 * size, size), :]
            pl.semaphore_signal(
                self.free.at[before, p], inc=1, device_id=spots[before][1], device_id_type=pl.DeviceIdType.MESH
            )
        elif before == h:
            at, first = self.quarter(base, self.place), self.height - (self.height >> h)
            size = self.height >> 5
            total = self.mat[p, at, :].astype(f32)
            for d in range(3):
                self.exchange(p, out, d)
                total = total + self.inbox[p, pl.ds(first + d * size, size), :].astype(f32)
                pl.semaphore_signal(
                    self.free.at[3 + d, p],
                    inc=1,
                    device_id=self.peer(self.others[d]),
                    device_id_type=pl.DeviceIdType.MESH,
                )
            self.mat[p, at, :] = total.astype(bf16)
        elif h < before <= h + w:
            some = self.mat.at[p, pl.ds(0, self.height >> 5)]
            row = before + 2
            self.remote(some, some, (out[0].at[row, p], out[1].at[row, p]), spots[0][1]).wait()
            at = self.quarter(base, self.place)
            self.mat[p, at, :] = self.mat[p, at, :] + self.extra[before - h - 1, p]
        elif before == h + w + 1:
            for d in range(3):
                self.exchange(p, back, d)
        elif before > h + w + 1:
            t = last - 1 - before
            some = self.mat.at[p, pl.ds(0, self.height >> (t + 1))]
            self.remote(some, some, (back[0].at[t, p], back[1].at[t, p]), spots[0][1]).wait()
        if stage < h:
            size = self.height >> (stage + 1)
            bit, device = spots[stage]
            part = self.mat.at[p, self.rows(starts[stage] + (1 - bit) * size, size)]
            land = self.inbox.at[p, pl.ds(self.height - 2 * size, size)]
            self.remote(part, land, (out[0].at[stage, p], out[1].at[stage, p]), device).start()
        elif stage == h:
            first, size = self.height - (self.height >> h), self.height >> 5
            for d in range(3):
                part = self.mat.at[p, self.quarter(base, self.others[d])]
                land = self.inbox.at[p, pl.ds(first + d * size, size)]
                sems = out[0].at[3 + d, p], out[1].at[3 + d, p]
                self.remote(part, land, sems, self.peer(self.others[d])).start()
        elif stage <= h + w:
            axis, row = stage, stage + 2
            bit = lax.shift_right_logical(self.seq, axis) & 1
            device = {"seq": self.seq + (1 - 2 * bit) * (1 << axis), "dp": self.dp}
            part = self.mat.at[p, self.quarter(base, self.place)]
            sems = out[0].at[row, p], out[1].at[row, p]
            self.remote(part, self.extra.at[stage - h - 1, p], sems, device).start()
        elif stage == h + w + 1:
            for d in range(3):
                pl.semaphore_wait(self.free.at[3 + d, p], 1)
                part = self.mat.at[p, self.quarter(base, self.place)]
                sems = back[0].at[3 + d, p], back[1].at[3 + d, p]
                self.remote(part, part, sems, self.peer(self.others[d])).start()
        elif stage < last:
            t = last - 1 - stage
            pl.semaphore_wait(self.free.at[t, p], 1)
            part = self.mat.at[p, self.rows(starts[t + 1], self.height >> (t + 1))]
            self.remote(part, part, (back[0].at[t, p], back[1].at[t, p]), spots[t][1]).start()


def line(ref):
    return ref[...].reshape(1, ref.shape[0])


def remote(src, dst, send, recv, device):
    return pltpu.make_async_remote_copy(
        src_ref=src,
        dst_ref=dst,
        send_sem=send,
        recv_sem=recv,
        device_id={"seq": device},
        device_id_type=pl.DeviceIdType.MESH,
    )


def rows(index, count):
    return pl.ds(pl.multiple_of(index * count, count), count)


def greet(plan, me, others=()):
    barrier = pltpu.get_barrier_semaphore()
    count = len(others)
    for seq, dp in others:
        pl.semaphore_signal(
            barrier, inc=1, device_id={"seq": seq, "dp": dp}, device_id_type=pl.DeviceIdType.MESH
        )
    for off in plan.offsets:
        there = plan.feeds(me, me + off) | plan.feeds(me + off, me)
        count = count + jnp.where(there, 1, 0)

        @pl.when(there)
        def _():
            pl.semaphore_signal(
                barrier, inc=1, device_id={"seq": me + off}, device_id_type=pl.DeviceIdType.MESH
            )

    pl.semaphore_wait(barrier, count)


def gather_kernel(
    plan,
    tok_ref, gain_ref, shift_ref, wkv_ref, kvb_ref, wq_ref, qb_ref, cot_hbm, down_hbm,
    normal_ref, q_ref, win_ref, taken_ref, act_hbm,
    kv_ref, cot_ref, down_ref, act_ref, kv_send, kv_recv, q_send, q_recv, fetch,
):
    me = lax.axis_index("seq")
    fetches = [
        pltpu.make_async_copy(cot_hbm, cot_ref, fetch.at[0]),
        pltpu.make_async_copy(down_hbm, down_ref, fetch.at[1]),
    ]
    for fetched in fetches:
        fetched.start()
    greet(plan, me)

    def copy(k, source, holder, left, device):
        size = plan.shard_len - left
        at = pl.multiple_of(plan.place(source, holder) + left, CHUNK)
        return remote(
            kv_ref.at[pl.ds(left, size)], win_ref.at[pl.ds(at, size)], kv_send.at[k], kv_recv.at[k], device
        )

    givable = sorted({entry[1] for entry in plan.help})

    def handed(i):
        found, helper, slot, order = plan.given(me, i)
        return found > 0, remote(
            q_ref.at[:, pl.ds(i * CHUNK, CHUNK)], taken_ref.at[slot], q_send.at[order], q_recv.at[slot], helper
        )

    normal = normed(tok_ref[...].astype(f32), line(gain_ref), line(shift_ref)).astype(bf16)
    normal_ref[...] = normal
    bias = line(kvb_ref)
    bias = jnp.concatenate([jnp.zeros_like(bias), bias], axis=1)
    kv_ref[...] = (contract(normal, wkv_ref[...], 1, 0) + bias).astype(bf16)
    for k, off in enumerate(plan.offsets):

        for there, left in plan.pairs(me, me + off):

            @pl.when(there)
            def _():
                copy(k, me, me + off, left, me + off).start()

    own = pl.multiple_of(plan.place(me, me), CHUNK)
    win_ref[pl.ds(own, plan.shard_len), :] = kv_ref[...]
    q_ref[...] = (contract(normal, wq_ref[...], 1, 0) + line(qb_ref)).T.astype(bf16)
    for i in givable:
        there, hand = handed(i)

        @pl.when(there)
        def _():
            hand.start()

    for fetched in fetches:
        fetched.wait()
    tile = act_ref.shape[2]
    tiles = act_hbm.shape[0]

    def put(t, slot):
        return pltpu.make_async_copy(act_ref.at[slot], act_hbm.at[t], fetch.at[slot])

    def back(t, _):
        slot = t % 2

        @pl.when(t >= 2)
        def _():
            put(t - 2, slot).wait()

        act_ref[slot] = contract(cot_ref[...], down_ref[rows(t, tile), :], 1, 1)
        put(t, slot).start()
        return 0

    lax.fori_loop(0, tiles, back, 0)
    for t in range(tiles - 2, tiles):
        put(t, t % 2).wait()

    for k, off in enumerate(plan.offsets):
        for there, left in plan.pairs(me, me + off):

            @pl.when(there)
            def _():
                copy(k, me, me + off, left, me + off).wait_send()

        for there, left in plan.pairs(me - off, me):

            @pl.when(there)
            def _():
                copy(k, me - off, me, left, me - off).wait_recv()

    for i in givable:
        there, hand = handed(i)

        @pl.when(there)
        def _():
            hand.wait_send()

    for k in range(plan.slots):
        found, home, _, _ = plan.taken(me, k)

        @pl.when(found > 0)
        def _():
            remote(taken_ref.at[k], taken_ref.at[k], q_send.at[k], q_recv.at[k], home).wait_recv()


def normed(values, gains, shifts):
    center = values - jnp.mean(values, axis=-1, keepdims=True)
    spread = jnp.mean(center * center, axis=-1, keepdims=True)
    return center * lax.rsqrt(spread + epsilon) * gains + shifts


def contract(left_op, right_op, left_dim, right_dim):
    return lax.dot_general(
        left_op, right_op, (((left_dim,), (right_dim,)), ((), ())), preferred_element_type=f32
    )


def wide(block, heads, head_dim):
    return jnp.concatenate([block[h * head_dim : (h + 1) * head_dim] for h in range(heads)], axis=1)


def tall(block, heads):
    return jnp.concatenate([block[:, h * CHUNK : (h + 1) * CHUNK] for h in range(heads)], axis=0)


def hi_lo(value, count):
    parts = []
    for _ in range(count):
        part = value.astype(bf16)
        parts.append(part.astype(f32))
        value = value - parts[-1]
    return parts


def scaled_queries(q, head_dim, lse_parts, row):
    width = q.shape[1]
    hi, lo = hi_lo(q.astype(f32) * (LOG2E * head_dim ** (-0.5)), 2)
    first = jnp.broadcast_to(jnp.where(row == 0, 1.0, 0.0), (1, width))
    fill = jnp.zeros((2 * head_dim - 5, width), f32)
    return jnp.concatenate([hi, lo] + lse_parts + [first, 1.0 - first, fill], axis=0).astype(bf16)


def triangle(heads):
    key = lax.broadcasted_iota(jnp.int32, (CHUNK, heads * CHUNK), 0)
    query = lax.broadcasted_iota(jnp.int32, (CHUNK, heads * CHUNK), 1) % CHUNK
    return key <= query


def causal(s, heads):
    return jnp.concatenate([s[:PAD], jnp.where(triangle(heads), s[PAD:], BIG)], axis=0)


def attend_kernel(
    plan, heads, head_dim, len_ref, q_ref, win_ref, o_ref, rest_ref, lse_ref, k_ref, v_ref, kt_ref, vt_ref, acc, top, norm
):
    i = pl.program_id(0)
    me = lax.axis_index("seq")
    place = plan.chunk(me, i)
    row = place // (ROW // CHUNK)
    end = MARGIN + (place + 1) * CHUNK
    blocks = place % (ROW // CHUNK) // (BLOCK // CHUNK) + 1

    @pl.when(i == 0)
    def _():
        first, second = len_ref[0, plan.first_row(me)], len_ref[0, plan.last_row(me)]
        filled = plan.place(plan.reaches(me), me) + plan.shard_len - MARGIN
        lane = lax.broadcasted_iota(jnp.int32, (BLOCK, 2 * head_dim), 1)
        vt_ref[head_dim:, :] = jnp.where(
            lax.broadcasted_iota(jnp.int32, (16, vt_ref.shape[1]), 0) == 0, 1.0, 0.0
        ).astype(bf16)
        norm[...] = jnp.zeros_like(norm)

        def fill(b, _):
            at = pl.ds(pl.multiple_of(b * BLOCK, BLOCK), BLOCK)
            pos = b * BLOCK - MARGIN + lax.broadcasted_iota(jnp.int32, (BLOCK, 2 * head_dim), 0)
            inside = (pos >= 0) & (pos < filled)
            both = jnp.where(inside, win_ref[at, :].astype(f32), 0.0)
            swapped = pltpu.roll(both, head_dim, 1)
            k_ref[at, : 2 * head_dim] = jnp.where(lane < head_dim, both, swapped).astype(bf16)
            one = (pos >= 0) & (pos < first)
            two = (pos >= ROW) & (pos < ROW + second)
            bias = jnp.where(lane == 3, jnp.where(one, 0.0, BIG), jnp.where(two, 0.0, BIG))
            marks = jnp.where(lane < 3, 1.0, jnp.where(lane < 5, bias, 0.0))
            k_ref[at, 2 * head_dim :] = marks.astype(bf16)
            v_ref[at, :] = jnp.where(
                lane >= head_dim, both, jnp.where(lane < 3, 1.0, 0.0)
            ).astype(bf16)
            turned = both.T
            kt_ref[:, at] = turned[:head_dim].astype(bf16)
            vt_ref[:head_dim, at] = turned[head_dim:].astype(bf16)
            norm[...] = jnp.maximum(
                norm[...],
                jnp.max(jnp.sum(jnp.square(turned[:head_dim]), axis=0, keepdims=True), axis=1, keepdims=True),
            )
            return 0

        lax.fori_loop(0, k_ref.shape[0] // BLOCK, fill, 0)

    zero = jnp.zeros((1, heads * CHUNK), f32)
    q = wide(q_ref[...], heads, head_dim)
    q_aug = scaled_queries(q, head_dim, [zero, zero, zero], row)
    q_norm = jnp.max(jnp.sum(jnp.square(q.astype(f32)), axis=0, keepdims=True), axis=1, keepdims=True)
    limit = (SAFE / LOG2E) ** 2 * head_dim
    safe = jnp.max(jnp.where(q_norm * norm[...] < limit, 1, 0)) > 0

    def scores(j):
        off = pl.multiple_of(end - (j + 1) * BLOCK, CHUNK)
        return contract(k_ref[pl.ds(off, BLOCK), :], q_aug, 1, 0)

    def values(j):
        off = pl.multiple_of(end - (j + 1) * BLOCK, CHUNK)
        return vt_ref[:, pl.ds(off, BLOCK)]

    @pl.when(safe)
    def _():
        p = jnp.exp2(causal(scores(0), heads)).astype(bf16)
        acc[...] = contract(values(0), p, 1, 0)

        def several(first, count):
            s = [scores(first + k) for k in range(count)]
            mixed = [contract(values(first + k), jnp.exp2(s[k]).astype(bf16), 1, 0) for k in range(count)]
            acc[...] += sum(mixed)

        def four(k, _):
            several(4 * k + 1, 4)
            return 0

        left = (blocks - 1) % 4
        lax.fori_loop(0, (blocks - 1) // 4, four, 0)

        @pl.when(left >= 2)
        def _():
            several(blocks - left, 2)

        @pl.when(left % 2 == 1)
        def _():
            several(blocks - 1, 1)

        top[...] = jnp.zeros_like(top)

    @pl.when(jnp.logical_not(safe))
    def _():
        s = causal(scores(0), heads)
        m = jnp.max(s, axis=0, keepdims=True)
        top[...] = m
        acc[...] = contract(values(0), jnp.exp2(s - m).astype(bf16), 1, 0)

        def step(j, _):
            s = scores(j)
            old = top[...]
            m = jnp.maximum(old, jnp.max(s, axis=0, keepdims=True))
            top[...] = m
            p = jnp.exp2(s - m).astype(bf16)
            acc[...] = acc[...] * jnp.exp2(old - m) + contract(values(j), p, 1, 0)
            return 0

        lax.fori_loop(1, blocks, step, 0)

    total = acc[head_dim : head_dim + 1, :]
    attended = tall(acc[:head_dim, :] / total, heads)
    o_ref[...] = attended.astype(bf16)
    rest_ref[...] = (attended - attended.astype(bf16).astype(f32)).astype(bf16)
    lse_ref[0] = top[...] + jnp.log2(total)


def feed_phase(
    att_ref, wo_hbm, tok_ref, cot_hbm, vecs, upb_ref, up_hbm, down_hbm, act_hbm,
    out_hbm, res_ref, gatt_ref, mat,
    up_buf, down_buf, act_buf, normal, out_acc, gn_acc, wo_ref, cot_ref, out_ref, fetch, talk,
):
    tile = mat.shape[1] // 2
    tiles = up_hbm.shape[1] // tile
    width = up_hbm.shape[0]
    out_bias, gain, shift, down_bias = (line(ref) for ref in vecs)

    def fetches(t, slot):
        at = pl.ds(pl.multiple_of(t * tile, tile), tile)
        return (
            pltpu.make_async_copy(up_hbm.at[:, at], up_buf.at[slot], fetch.at[0, slot]),
            pltpu.make_async_copy(down_hbm.at[at], down_buf.at[slot], fetch.at[1, slot]),
            pltpu.make_async_copy(act_hbm.at[t], act_buf.at[slot], fetch.at[3, slot]),
        )

    wo_copy = pltpu.make_async_copy(wo_hbm, wo_ref, fetch.at[2, 0])
    cot_copy = pltpu.make_async_copy(cot_hbm, cot_ref, fetch.at[2, 1])
    wo_copy.start()
    for copy in fetches(0, 0):
        copy.start()
    cot_copy.start()
    wo_copy.wait()

    residual = tok_ref[...].astype(f32) + contract(att_ref[...], wo_ref[...], 0, 0) + out_bias
    res_ref[...] = residual
    normal[...] = normed(residual, gain, shift).astype(bf16)
    out_acc[...] = residual + down_bias
    gn_acc[...] = jnp.zeros_like(gn_acc)
    sums = mat.shape[0] - 1
    cot_copy.wait()

    def step(t, _):
        slot = t % 2
        for copy in fetches(t, slot):
            copy.wait()

        @pl.when(t + 1 < tiles)
        def _():
            for copy in fetches(t + 1, 1 - slot):
                copy.start()

        u = contract(normal[...], up_buf[slot], 1, 0) + upb_ref[t]
        square = u * u
        th = jnp.tanh(GELU * (u + 0.044715 * (u * square)))
        half = 0.5 * (1.0 + th)
        slope = half + (0.5 * GELU) * u * (1.0 - th * th) * (1.0 + 3 * 0.044715 * square)
        activated = (u * half).astype(bf16)
        out_acc[...] += contract(activated, down_buf[slot], 1, 0)
        mat[t, tile:, :] = contract(activated, cot_ref[...], 0, 0).astype(bf16)
        talk(2 * t + 1)
        grad = (act_buf[slot] * slope).astype(bf16)
        gn_acc[...] += contract(grad, up_buf[slot], 1, 1)
        mat[t, :tile, :] = contract(grad, normal[...], 0, 0).astype(bf16)
        upb_ref[t] = jnp.sum(grad.astype(f32), axis=0, keepdims=True)
        talk(2 * t + 2)
        return 0

    lax.fori_loop(0, tiles, step, 0)
    out_ref[...] = out_acc[...].astype(bf16)
    out_copy = pltpu.make_async_copy(out_ref, out_hbm, fetch.at[2, 0])
    out_copy.start()

    residual = res_ref[...]
    center = residual - jnp.mean(residual, axis=-1, keepdims=True)
    scale = lax.rsqrt(jnp.mean(center * center, axis=-1, keepdims=True) + epsilon)
    xhat = center * scale
    gn = gn_acc[...]
    q = gn * gain
    grad = scale * (
        q - jnp.mean(q, axis=-1, keepdims=True) - xhat * jnp.mean(q * xhat, axis=-1, keepdims=True)
    )
    cot = cot_ref[...].astype(f32)
    grad = cot + grad
    res_ref[...] = grad
    proj = grad.astype(bf16)
    talk(2 * tiles + 1)
    mat[sums, :width, :] = contract(att_ref[...], proj, 1, 0).astype(bf16)
    rows = [cot, proj.astype(f32), gn * xhat, gn]
    rows = [jnp.sum(row, axis=0, keepdims=True) for row in rows]
    rows.append(jnp.zeros((16 - len(rows), width), f32))
    mat[sums, width : width + 16, :] = jnp.concatenate(rows, axis=0).astype(bf16)
    rows = [upb_ref[t] for t in range(tiles)] + [jnp.zeros((1, tile), f32)] * (16 - tiles)
    rows = jnp.concatenate([jnp.concatenate(rows, axis=0), jnp.zeros((16, width - tile), f32)], axis=1)
    mat[sums, width + 16 : width + 32, :] = rows.astype(bf16)
    rest = mat.shape[1] - width - 32
    mat[sums, width + 32 :, :] = jnp.zeros((rest, width), bf16)
    gatt_ref[...] = contract(wo_ref[...], proj, 1, 1).astype(bf16)
    out_copy.wait()


def back_phase(
    plan, heads, head_dim, me, talk, steps,
    q_hbm, taken_hbm, k_hbm, v_hbm, kt_hbm, lse_ref, o_ref, rest_hbm, gatt_ref, dq_ref,
    low, inbox, land_q, land_g, land_s, give_s, kv_send, kv_recv, help_send, help_recv,
    k_ref, v_ref, kt_ref, q_ref, q_aug, g_aug, acc, total, rest_ref, fetch, prepared,
):
    shard_len = plan.shard_len
    pairs = [(q_hbm, q_ref), (rest_hbm, rest_ref), (k_hbm, k_ref), (v_hbm, v_ref), (kt_hbm, kt_ref), (taken_hbm, land_q)]
    copies = [pltpu.make_async_copy(src, dst, fetch.at[k]) for k, (src, dst) in enumerate(pairs)]
    for copy in copies[2:5]:
        copy.start()
    total[...] = jnp.zeros_like(total)
    acc[...] = jnp.zeros_like(acc)
    for copy in copies[:2]:
        copy.wait()

    def prepare(i, q, g, lse, delta, place):
        q_aug[i] = scaled_queries(wide(q, heads, head_dim), head_dim, hi_lo(-lse, 3), place // plan.per_row)
        fill = jnp.zeros((head_dim - 3, heads * CHUNK), f32)
        marks = jnp.concatenate(hi_lo(-delta, 3) + [fill], axis=0).astype(bf16)
        g_aug[i] = jnp.concatenate([marks, wide(g, heads, head_dim)], axis=0)

    def sends(i):
        found, helper, slot, order = plan.given(me, i)
        return found > 0, [
            remote(gatt_ref.at[:, pl.ds(i * CHUNK, CHUNK)], land_g.at[slot], help_send.at[1, order], help_recv.at[1, slot], helper),
            remote(give_s.at[order], land_s.at[slot], help_send.at[2, order], help_recv.at[2, slot], helper),
        ]

    givable = sorted({entry[1] for entry in plan.help})
    for i in range(plan.per_dev):
        if i in (2, 4):
            talk(steps + i // 2 - 1)
        at = pl.ds(i * CHUNK, CHUNK)
        g = gatt_ref[:, at]
        o = o_ref[:, at].astype(f32) + rest_ref[:, at].astype(f32)
        delta = jnp.sum(wide(g.astype(f32) * o, heads, head_dim), axis=0, keepdims=True)
        prepare(i, q_ref[:, at], g, lse_ref[i], delta, plan.chunk(me, i))
        if i in givable:
            there, copies_out = sends(i)

            @pl.when(there)
            def _():
                order = plan.given(me, i)[3]
                give_s[order, :1, :] = lse_ref[i]
                give_s[order, 1:2, :] = delta
                for copy in copies_out:
                    copy.start()

    for copy in copies[2:]:
        copy.wait()

    def piece(k, off, left):
        at = pl.ds(pl.multiple_of(plan.place(me + off, me) + left, CHUNK), shard_len - left)
        box = plan.box(me + off, -off)
        land = inbox.at[box, :, pl.ds(left, shard_len - left)]
        return remote(low.at[:, at], land, kv_send.at[k], kv_recv.at[box], me + off)

    def block(i, at, place, diagonal):
        s = contract(k_ref[at, :], q_aug[i], 1, 0)
        if diagonal:
            key = lax.broadcasted_iota(jnp.int32, (BLOCK, heads * CHUNK), 0)
            query = lax.broadcasted_iota(jnp.int32, (BLOCK, heads * CHUNK), 1) % CHUNK
            s = jnp.where(key - query <= place % (BLOCK // CHUNK) * CHUNK, s, BIG)
        dp = contract(v_ref[at, :], g_aug[i], 1, 0)
        p = jnp.exp2(s)
        ds = (p * dp).astype(bf16)
        p = p.astype(bf16)
        acc[i] += contract(kt_ref[:, at], ds, 1, 0)
        dk = contract(q_aug[i, : 2 * head_dim, :], ds, 1, 1)
        total[:head_dim, at] += dk[:head_dim] + dk[head_dim:]
        total[head_dim:, at] += contract(g_aug[i, head_dim:, :], p, 1, 1)

    def walk(count, locate, turn, n):
        def key_step(b, n):
            at = pl.ds(pl.multiple_of(MARGIN + b * BLOCK, BLOCK), BLOCK)

            def chunk_step(i, n):
                there, place = locate(i)
                last = place // (BLOCK // CHUNK)
                active = there & (b <= last) & (b // (ROW // BLOCK) == place // plan.per_row)

                @pl.when(active)
                def _():
                    talk(n)

                @pl.when(active & (b < last))
                def _():
                    block(i, at, place, False)

                @pl.when(active & (b == last))
                def _():
                    block(i, at, place, True)

                return n + jnp.where(active, 1, 0)

            n = lax.fori_loop(0, count, chunk_step, n)
            for k, off in enumerate(plan.offsets):
                end = plan.place(me + off, me) + shard_len - MARGIN

                for there, left in plan.pairs(me + off, me):

                    @pl.when(there & (b == (end + BLOCK - 1) // BLOCK - 1) & (plan.helps(me) == turn))
                    def _():
                        at = pl.ds(pl.multiple_of(plan.place(me + off, me), CHUNK), shard_len)
                        low[:head_dim, at] = (total[:head_dim, at] * (1.0 / LOG2E)).astype(bf16)
                        low[head_dim:, at] = total[head_dim:, at].astype(bf16)
                        piece(k, off, left).start()

            return n

        return lax.fori_loop(0, plan.span // BLOCK, key_step, n)

    def own(i):
        return plan.given(me, i)[0] == 0, plan.chunk(me, i)

    n = walk(plan.per_dev, own, 0, steps + 2)
    for i in range(plan.per_dev):
        dq_ref[:, i * CHUNK : (i + 1) * CHUNK] = tall(acc[i] * head_dim ** (-0.5), heads).astype(bf16)

    def taken(k):
        found, home, i, _ = plan.taken(me, k)
        return found > 0, plan.chunk(home, i, me)

    for k in range(plan.slots):
        there, place = taken(k)
        home = plan.taken(me, k)[1]

        @pl.when(there)
        def _():
            for part, land in ((1, land_g), (2, land_s)):
                remote(land.at[k], land.at[k], help_send.at[part, 0], help_recv.at[part, k], home).wait_recv()
            prepare(k, land_q[k], land_g[k], land_s[k, :1, :], land_s[k, 1:2, :], place)
            acc[k] = jnp.zeros_like(acc[k])

    for i in givable:
        there, copies_out = sends(i)

        @pl.when(there)
        def _():
            for copy in copies_out:
                copy.wait_send()

    prepared()
    n = walk(plan.slots, taken, 1, n)
    for k in range(plan.slots):
        there, _ = taken(k)
        _, home, _, order = plan.taken(me, k)

        @pl.when(there)
        def _():
            land_q[k] = tall(acc[k] * head_dim ** (-0.5), heads).astype(bf16)
            remote(land_q.at[k], land_g.at[order], help_send.at[3, k], help_recv.at[3, order], home).start()

    mine = pl.ds(pl.multiple_of(plan.place(me, me), CHUNK), shard_len)
    acc_kv = total[:, mine]
    total[:, :shard_len] = jnp.concatenate(
        [acc_kv[:head_dim] * (1.0 / LOG2E), acc_kv[head_dim:]], axis=0
    )
    return n


def layer_kernel(
    plan, heads, head_dim,
    att_ref, tok_ref, ob_ref, gain_ref, shift_ref, db_ref, upb_ref, lse_ref, gain_one_ref,
    wo_hbm, cot_hbm, up_hbm, down_hbm, act_hbm, rest_hbm, q_hbm, taken_hbm, k_hbm, v_hbm, kt_hbm, normal_hbm, wq_hbm, wkv_hbm,
    sum_ref, out_hbm, end_mat, tiny_mat, res_ref,
    gatt_ref, q_ref, spare, low, inbox, land_q, land_g, land_s, give_s, mat, upb_mat,
    feed_fetch, back_fetch, kv_send, kv_recv, help_send, help_recv, load, *summing,
):
    me = lax.axis_index("seq")
    shard_len, width = tok_ref.shape
    pieces, height, _ = mat.shape
    third = len(summing) // 3
    refs = [summing[k * third : (k + 1) * third] for k in range(3)]
    summed = Summing(plan, ORDERS, TABLE, height, mat, *refs[0][:2], refs[0][2:])
    ending = FlatSumming(plan, LAST_ORDERS, LAST_TABLE, end_mat.shape[1], end_mat, *refs[1][:2], refs[1][2:])
    tiny = FlatSumming(plan, TINY_ORDERS, TINY_TABLE, tiny_mat.shape[1], tiny_mat, *refs[2][:2], refs[2][2:])
    greet(plan, me, summed.partners())
    givable = sorted({entry[1] for entry in plan.help})
    for k, (src, dst) in ((0, (q_hbm, q_ref)), (1, (rest_hbm, spare)), (5, (taken_hbm, land_q))):
        pltpu.make_async_copy(src, dst, back_fetch.at[k]).start()
    for t in range(upb_mat.shape[0]):
        wide_t = upb_mat.shape[2]
        upb_mat[t] = upb_ref[pl.ds(t * wide_t, wide_t)].reshape(1, wide_t)

    def store(p):
        pltpu.make_async_copy(mat.at[p], sum_ref.at[p], load.at[p]).start()

    def talk(n):
        summed.step(n, store)

    def first(up_buf, down_buf, act_buf, normal, out_acc, gn_acc, wo_ref, cot_ref, out_ref):
        feed_phase(
            att_ref, wo_hbm, tok_ref, cot_hbm, (ob_ref, gain_ref, shift_ref, db_ref), upb_mat, up_hbm, down_hbm, act_hbm,
            out_hbm, res_ref, gatt_ref, mat,
            up_buf, down_buf, act_buf, normal, out_acc, gn_acc, wo_ref, cot_ref, out_ref, feed_fetch, talk,
        )

    tile = height // 2
    pl.run_scoped(
        first,
        pltpu.VMEM((2, width, tile), bf16),
        pltpu.VMEM((2, tile, width), bf16),
        pltpu.VMEM((2, shard_len, tile), f32),
        pltpu.VMEM((shard_len, width), bf16),
        pltpu.VMEM((shard_len, width), f32),
        pltpu.VMEM((shard_len, width), f32),
        pltpu.VMEM((width, width), bf16),
        pltpu.VMEM((shard_len, width), bf16),
        pltpu.VMEM((shard_len, width), bf16),
    )
    talk(2 * pieces)
    window, columns = plan.window, heads * CHUNK
    chunks = plan.per_dev

    def second(k_ref, v_ref, kt_ref, q_aug, g_aug, acc, total, wkv):
        copies = [
            pltpu.make_async_copy(src, dst, back_fetch.at[6 + k])
            for k, (src, dst) in enumerate([(normal_hbm, gatt_ref), (wq_hbm, spare), (wkv_hbm, wkv)])
        ]

        def later():
            for copy in copies:
                copy.start()

        done = back_phase(
            plan, heads, head_dim, me, talk, 2 * pieces + 1,
            q_hbm, taken_hbm, k_hbm, v_hbm, kt_hbm, lse_ref, att_ref, rest_hbm, gatt_ref, q_ref,
            low, inbox, land_q, land_g, land_s, give_s, kv_send, kv_recv, help_send, help_recv,
            k_ref, v_ref, kt_ref, q_ref, q_aug, g_aug, acc, total, spare, back_fetch, later,
        )

        def drain(n, _):
            talk(n)
            return 0

        busy = 2 * pieces + 3 + plan.blocks
        lax.fori_loop(done, busy, drain, 0)
        for i in givable:
            found, helper, _, order = plan.given(me, i)

            @pl.when(found > 0)
            def _():
                land = land_g.at[order]
                remote(land, land, help_send.at[3, 0], help_recv.at[3, order], helper).wait_recv()
                q_ref[:, i * CHUNK : (i + 1) * CHUNK] = land_g[order]

        for copy in copies:
            copy.wait()
        normal, wq = gatt_ref, spare
        tall_part, wide_part = end_mat.shape[1:]
        grad = contract(normal[...], q_ref[...], 0, 1).astype(bf16)
        rest = width - tall_part
        for k in range(2):
            at = slice(k * wide_part, (k + 1) * wide_part)
            end_mat[k] = grad[:tall_part, at]
            end_mat[2, k * rest : (k + 1) * rest, :] = grad[tall_part:, at]

        def joint(n):
            talk(n)
            ending.step(n)
            tiny.step(n)

        for k in range(3):
            joint(busy + k)
        grad_qb = jnp.sum(q_ref[...].astype(f32).T, axis=0, keepdims=True)
        gn = contract(q_ref[...], wq[...], 0, 1)
        joint(busy + 3)

        for k, off in enumerate(plan.offsets):

            for there, left in plan.pairs(me, me + off):

                @pl.when(there)
                def _():
                    box = plan.box(me, off)
                    part = pl.ds(left, shard_len - left)
                    land = inbox.at[box, :, part]
                    remote(land, land, kv_send.at[0], kv_recv.at[box], me + off).wait_recv()
                    total[:, part] += inbox[box, :, part].astype(f32)

            for there, left in plan.pairs(me + off, me):

                @pl.when(there)
                def _():
                    some = inbox.at[0, :, pl.ds(left, shard_len - left)]
                    remote(some, some, kv_send.at[k], kv_recv.at[0], me + off).wait_send()

        for k in range(plan.slots):
            found, home, _, order = plan.taken(me, k)

            @pl.when(found > 0)
            def _():
                remote(
                    land_q.at[k], land_g.at[order], help_send.at[3, k], help_recv.at[3, order], home
                ).wait_send()

        grad_kv = total[:, :shard_len].astype(bf16)
        gn = gn + contract(grad_kv, wkv[...], 0, 1)
        grad = contract(grad_kv, normal[...], 1, 0).astype(bf16)
        pair, piece = 2 * head_dim, tiny_mat.shape[2]
        parts = width // piece
        for k in range(parts):
            tiny_mat[0, k * pair : (k + 1) * pair, :] = grad[:, k * piece : (k + 1) * piece]
        grad_vb = jnp.sum(grad_kv.astype(f32).T, axis=0, keepdims=True)

        tok = tok_ref[...].astype(f32)
        center = tok - jnp.mean(tok, axis=-1, keepdims=True)
        scale = lax.rsqrt(jnp.mean(center * center, axis=-1, keepdims=True) + epsilon)
        xhat = center * scale
        grads = [gn * xhat, gn]
        rows = [jnp.sum(grad, axis=0, keepdims=True) for grad in grads] + [grad_qb]
        rows.append(jnp.concatenate([grad_vb, jnp.zeros((1, width - 2 * head_dim), f32)], axis=1))
        rows.append(jnp.zeros((16 - len(rows), width), f32))
        rows = jnp.concatenate(rows, axis=0).astype(bf16)
        for k in range(parts):
            at = parts * pair + 16 * k
            tiny_mat[0, at : at + 16, :] = rows[:, k * piece : (k + 1) * piece]
        at = parts * (pair + 16)
        tiny_mat[0, at:, :] = jnp.zeros((tiny_mat.shape[1] - at, piece), bf16)
        joint(busy + 4)
        q = gn * line(gain_one_ref)
        res_ref[...] += scale * (
            q - jnp.mean(q, axis=-1, keepdims=True) - xhat * jnp.mean(q * xhat, axis=-1, keepdims=True)
        )


        def finish(n, _):
            joint(n)
            return 0

        lax.fori_loop(busy + 5, max(summed.end, ending.end, tiny.end), finish, 0)

    pl.run_scoped(
        second,
        pltpu.VMEM((window, 4 * head_dim), bf16),
        pltpu.VMEM((window, 2 * head_dim), bf16),
        pltpu.VMEM((head_dim, window), bf16),
        pltpu.VMEM((chunks, 4 * head_dim, columns), bf16),
        pltpu.VMEM((chunks, 2 * head_dim, columns), bf16),
        pltpu.VMEM((chunks, head_dim, columns), f32),
        pltpu.VMEM((2 * head_dim, window), f32),
        pltpu.VMEM(wkv_hbm.shape, bf16),
    )
    for p in range(pieces):
        pltpu.make_async_copy(mat.at[p], sum_ref.at[p], load.at[p]).wait()


def final_kernel(
    head_dim,
    sum_ref, w_ref, rest_ref, last_ref, small_ref, tok_ref, grad_ref,
    tok_out, grad_out, up_ref, down_ref, out_ref, q_ref, kv_ref, upb_ref,
    db_ref, ob_ref, gain_two_ref, shift_two_ref, gain_one_ref, shift_one_ref, qb_ref, vb_ref,
):
    tok_out[...] = tok_ref[...]
    grad_out[...] = grad_ref[...]
    i = pl.program_id(0)
    tile, width = down_ref.shape
    up_ref[...] = sum_ref[0, :tile, :].astype(f32).T
    down_ref[...] = sum_ref[0, tile:, :].astype(f32)
    out_ref[...] = w_ref[0].astype(f32)
    half, side, count = width // 2, width - tile, q_ref.shape[0]
    first = i * count < tile
    at = pl.multiple_of(jnp.where(first, i * count, 0), count)
    for k in range(2):
        place = slice(k * half, (k + 1) * half)

        @pl.when(first)
        def _():
            q_ref[:, place] = last_ref[k, pl.ds(at, count), :].astype(f32)

        @pl.when(jnp.logical_not(first))
        def _():
            low = pl.multiple_of(k * side + i * count - tile, count)
            q_ref[:, place] = last_ref[2, pl.ds(low, count), :].astype(f32)

    @pl.when(i == 0)
    def _():
        pair = 2 * head_dim
        small = small_ref[0].astype(f32)
        parts = width // small.shape[1]
        kv_ref[...] = jnp.concatenate([small[k * pair : (k + 1) * pair] for k in range(parts)], axis=1).T
        rows = rest_ref[0, :32, :].astype(f32)
        for k, ref in enumerate([db_ref, ob_ref, gain_two_ref, shift_two_ref]):
            ref[...] = rows[k : k + 1].reshape(width)
        for t in range(upb_ref.shape[0] // tile):
            upb_ref[pl.ds(t * tile, tile)] = rows[16 + t : 17 + t, :tile].reshape(tile)
        rows = [small[parts * pair + 16 * k : parts * pair + 16 * (k + 1)] for k in range(parts)]
        rows = jnp.concatenate(rows, axis=1)
        for k, ref in enumerate([gain_one_ref, shift_one_ref, qb_ref]):
            ref[...] = rows[k : k + 1].reshape(width)
        vb_ref[...] = rows[3:4, head_dim : 2 * head_dim].reshape(head_dim)


def whole(shape):
    return pl.BlockSpec(shape, lambda i: (0,) * len(shape))


def column(height):
    return pl.BlockSpec((height, CHUNK), lambda i: (0, i))


def lead(shape):
    return pl.BlockSpec((1,) + shape, lambda i: (i,) + (0,) * len(shape))


def per_device(
    plan,
    tokens,
    lengths,
    cotangent,
    norm1_gain,
    norm1_shift,
    query_weight,
    query_bias,
    keyval_weight,
    value_bias,
    out_weight,
    out_bias,
    norm2_gain,
    norm2_shift,
    up_weight,
    up_bias,
    down_weight,
    down_bias,
):
    shard_len, width = tokens.shape[1:]
    head_dim = keyval_weight.shape[1] // 2
    heads = width // head_dim
    columns = heads * CHUNK
    chunks = plan.per_dev
    window = plan.window
    limit = dict(vmem_limit_bytes=63 * 2**20)
    vmem = pl.BlockSpec(memory_space=pltpu.VMEM)
    anywhere = pl.BlockSpec(memory_space=pl.ANY)
    dma = pltpu.SemaphoreType.DMA

    hidden = up_weight.shape[1]
    tile = PIECE // 2
    tiles = hidden // tile
    normal_one, queries, keyvals, taken, grad_act = pl.pallas_call(
        partial(gather_kernel, plan),
        in_specs=[vmem] * 7 + [anywhere] * 2,
        out_specs=[vmem] * 4 + [anywhere],
        out_shape=[
            jax.ShapeDtypeStruct((shard_len, width), bf16),
            jax.ShapeDtypeStruct((width, shard_len), bf16),
            jax.ShapeDtypeStruct((window, 2 * head_dim), bf16),
            jax.ShapeDtypeStruct((plan.slots, width, CHUNK), bf16),
            jax.ShapeDtypeStruct((tiles, shard_len, tile), f32),
        ],
        scratch_shapes=[
            pltpu.VMEM((shard_len, 2 * head_dim), bf16),
            pltpu.VMEM((shard_len, width), bf16),
            pltpu.VMEM((hidden, width), bf16),
            pltpu.VMEM((2, shard_len, tile), f32),
        ]
        + [dma((len(plan.offsets),))] * 2
        + [dma((plan.slots,))] * 2
        + [dma((2,))],
        compiler_params=pltpu.CompilerParams(collective_id=0, has_side_effects=True, **limit),
        name="gather",
    )(
        tokens[0],
        norm1_gain,
        norm1_shift,
        keyval_weight,
        value_bias,
        query_weight,
        query_bias,
        cotangent[0],
        down_weight,
    )

    attended, attended_low, lse, k_aug, v_aug, k_turned = pl.pallas_call(
        partial(attend_kernel, plan, heads, head_dim),
        grid_spec=pltpu.PrefetchScalarGridSpec(
            num_scalar_prefetch=0,
            grid=(chunks,),
            in_specs=[
                pl.BlockSpec(memory_space=pltpu.SMEM),
                column(width),
                whole((window, 2 * head_dim)),
            ],
            out_specs=[
                column(width),
                column(width),
                lead((1, columns)),
                whole((window, 4 * head_dim)),
                whole((window, 2 * head_dim)),
                whole((head_dim, window)),
            ],
            scratch_shapes=[
                pltpu.VMEM((head_dim + 16, window), bf16),
                pltpu.VMEM((head_dim + 16, columns), f32),
                pltpu.VMEM((1, columns), f32),
                pltpu.VMEM((1, 1), f32),
            ],
        ),
        out_shape=[
            jax.ShapeDtypeStruct((width, shard_len), bf16),
            jax.ShapeDtypeStruct((width, shard_len), bf16),
            jax.ShapeDtypeStruct((chunks, 1, columns), f32),
            jax.ShapeDtypeStruct((window, 4 * head_dim), bf16),
            jax.ShapeDtypeStruct((window, 2 * head_dim), bf16),
            jax.ShapeDtypeStruct((head_dim, window), bf16),
        ],
        compiler_params=pltpu.CompilerParams(**limit),
        name="attend",
    )(lengths, queries, keyvals)

    inputs = tokens[0].astype(f32)
    pieces = tiles + 1
    assert pieces == len(ORDERS) and 2 * (width - tile) == tile and 3 * (2 * head_dim + 16) <= tile
    sums, outputs, last, small, grad_inputs = pl.pallas_call(
        partial(layer_kernel, plan, heads, head_dim),
        in_specs=[vmem] * 9 + [anywhere] * 14,
        out_specs=[anywhere] * 2 + [vmem] * 3,
        out_shape=[
            jax.ShapeDtypeStruct((pieces, PIECE, width), bf16),
            jax.ShapeDtypeStruct((shard_len, width), bf16),
            jax.ShapeDtypeStruct((3, tile, width // 2), bf16),
            jax.ShapeDtypeStruct((1, tile, width // 3), bf16),
            jax.ShapeDtypeStruct((shard_len, width), f32),
        ],
        scratch_shapes=[
            pltpu.VMEM((width, shard_len), bf16),
            pltpu.VMEM((width, shard_len), bf16),
            pltpu.VMEM((width, shard_len), bf16),
            pltpu.VMEM((2 * head_dim, window), bf16),
            pltpu.VMEM((plan.inboxes, 2 * head_dim, shard_len), bf16),
            pltpu.VMEM((plan.slots, width, CHUNK), bf16),
            pltpu.VMEM((plan.slots, width, CHUNK), bf16),
            pltpu.VMEM((plan.slots, 8, columns), f32),
            pltpu.VMEM((plan.slots, 8, columns), f32),
            pltpu.VMEM((pieces, PIECE, width), bf16),
            pltpu.VMEM((tiles, 1, tile), f32),
            dma((4, 2)),
            dma((9,)),
            dma((len(plan.offsets),)),
            dma((plan.inboxes,)),
            dma((4, plan.slots)),
            dma((4, plan.slots)),
            dma((pieces,)),
        ]
        + Summing.scratch(plan, pieces, PIECE, width)
        + Summing.scratch(plan, 3, tile, width // 2)
        + Summing.scratch(plan, 1, tile, width // 3),
        compiler_params=pltpu.CompilerParams(collective_id=1, has_side_effects=True, **limit),
        name="layer",
    )(
        attended,
        tokens[0],
        out_bias,
        norm2_gain,
        norm2_shift,
        down_bias,
        up_bias,
        lse,
        norm1_gain,
        out_weight,
        cotangent[0],
        up_weight,
        down_weight,
        grad_act,
        attended_low,
        queries,
        taken,
        k_aug,
        v_aug,
        k_turned,
        normal_one,
        query_weight,
        keyval_weight,
    )

    vector = jax.ShapeDtypeStruct((width,), f32)
    finals = pl.pallas_call(
        partial(final_kernel, head_dim),
        grid=(tiles,),
        in_specs=[
            lead((PIECE, width)),
            pl.BlockSpec((1, width // tiles, width), lambda i: (tiles, i, 0)),
            pl.BlockSpec((1, PIECE - width, width), lambda i: (tiles, width // (PIECE - width), 0)),
            whole((3, tile, width // 2)),
            whole((1, tile, width // 3)),
            pl.BlockSpec((shard_len // tiles, width), lambda i: (i, 0)),
            pl.BlockSpec((shard_len // tiles, width), lambda i: (i, 0)),
        ],
        out_specs=[
            pl.BlockSpec((shard_len // tiles, width), lambda i: (i, 0)),
            pl.BlockSpec((shard_len // tiles, width), lambda i: (i, 0)),
            pl.BlockSpec((width, tile), lambda i: (0, i)),
            pl.BlockSpec((tile, width), lambda i: (i, 0)),
            pl.BlockSpec((width // tiles, width), lambda i: (i, 0)),
            pl.BlockSpec((width // tiles, width), lambda i: (i, 0)),
            whole((width, 2 * head_dim)),
            whole((hidden,)),
        ]
        + [whole((width,))] * 7
        + [whole((head_dim,))],
        out_shape=[
            jax.ShapeDtypeStruct((shard_len, width), bf16),
            jax.ShapeDtypeStruct((shard_len, width), f32),
            jax.ShapeDtypeStruct((width, hidden), f32),
            jax.ShapeDtypeStruct((hidden, width), f32),
            jax.ShapeDtypeStruct((width, width), f32),
            jax.ShapeDtypeStruct((width, width), f32),
            jax.ShapeDtypeStruct((width, 2 * head_dim), f32),
            jax.ShapeDtypeStruct((hidden,), f32),
        ]
        + [vector] * 7
        + [jax.ShapeDtypeStruct((head_dim,), f32)],
        compiler_params=pltpu.CompilerParams(**limit),
        name="finals",
    )(sums, sums, sums, last, small, outputs, grad_inputs)
    outputs, grad_inputs, up_w, down_w, out_w, qw, kvw, up_b = finals[:8]
    down_b, out_b, gain_two, shift_two, gain_one, shift_one, qb, vb = finals[8:]
    return (
        outputs[None],
        grad_inputs[None],
        gain_one,
        shift_one,
        qw,
        qb,
        kvw,
        vb,
        out_w,
        out_b,
        gain_two,
        shift_two,
        up_w,
        up_b,
        down_w,
        down_b,
    )


def solution(mesh):
    split = P("dp", "seq", None)
    devices = mesh.shape["seq"]

    def run(*arrays):
        plan = Plan(devices, arrays[0].shape[1] // devices)
        return jax.shard_map(
            partial(per_device, plan),
            mesh=mesh,
            in_specs=(split, P("dp", None), split) + (P(),) * 14,
            out_specs=(split, split) + (P(),) * 14,
            check_vma=False,
        )(*arrays)

    return run
```
